32 devices in a mesh: patch: 4 (over z), mode: 8 (over y, x, core).
Axes of the slice: x: 2, y: 2, z: 4, core: 2. Of those that a mesh axis runs over, the one named last changes fastest.
Arguments:
- sky_map: bfloat16 [32, 8192, 64], P('patch', 'mode'), may hold values from -6 to 6
- pixel_mask: int32 [32, 8192], P('patch', 'mode'), may hold values 0 or 1
- noise_factor: float32 [32, 8, 64, 64], P('patch', 'mode'), as said below
- cycle_legendre: float32 [32, 6144, 4], P('patch', 'mode'), may hold values from -6 to 6
- band_power: float32 [6144, 4], P('mode', 'patch'), may hold values from 0.1 to 10
- channel_cov: float32 [64, 64], replicated
- test_matrix: bfloat16 [4, 6144, 2, 512], P('patch', 'mode'), may hold values from -6 to 6
Outputs:
- sketch: float32 [64, 512], P(None, ('patch', 'mode'))
The draws below stay inside these ranges and needn't reach their ends.
Inputs may be any that keep to these rules, and one draw needn't show every extreme that they name: `noise_factor`: each noise factor is lower triangular with a positive diagonal.
All inputs are finite; a program needn't handle non-finite values. No bound on the sum of `pixel_mask` on one device may be relied on, other than what follows from the above.
Results may differ from the reference program's by a relative error of at most 0.017.
Values may be sent and summed in bfloat16 or wider, within the bound.
No kernel may reach another device: no remote copies, remote signals or barrier semaphores. Data moves between devices by JAX's collectives and lax.ppermute only.
A program may use at most 64 MiB of HBM per device.

```python
import math
import jax
import jax.numpy as jnp
from jax import lax

C = 64
NPHI = 8192
MMAX = 6144
NS = 512
CYCLES = 32
LW = 4
PIECES = 8
NPHI_DEV = 1024


def draw_noise_factor(key, part):
    first, second = jax.random.split(key, 2)
    spread = jax.random.uniform(first, (CYCLES, PIECES, C, C), jnp.float32, -1.0, 1.0) / math.sqrt(C)
    lower = jnp.tril(spread, -1)
    diag = jnp.exp(jax.random.uniform(second, (CYCLES, PIECES, C), jnp.float32, math.log(0.5), math.log(2.0)))
    return lower + diag[:, :, :, None] * jnp.eye(C, dtype=jnp.float32)


def draw_channel_cov(key, part):
    first, second = jax.random.split(key, 2)
    spread = jax.random.uniform(first, (C, C), jnp.float32, -1.0, 1.0) / math.sqrt(C)
    symmetric = 0.5 * (spread + jnp.transpose(spread))
    diag = jnp.exp(jax.random.uniform(second, (C,), jnp.float32, 0.0, math.log(4.0)))
    return symmetric + diag[:, None] * jnp.eye(C, dtype=jnp.float32)


def with_ends(values, own_key, smallest, high):
    shape = values.shape
    spot = [jax.random.randint(jax.random.fold_in(own_key, axis), (), 0, shape[axis]) for axis in range(len(shape))]
    values = values.at[tuple(spot)].set(smallest)
    longest = shape.index(max(shape))
    spot[longest] = (spot[longest] + 1) % shape[longest]
    return values.at[tuple(spot)].set(high)


def spiked(drawn, rng, source, target, shards_of, factor):
    owner, partner = [(jnp.arange(drawn.shape[position]) // (drawn.shape[position] // shards_of)).reshape([-1 if axis == position else 1 for axis in range(drawn.ndim)]) for position in (source, target)]
    chosen = jax.random.permutation(rng, shards_of)[partner]
    strong = (owner == chosen) | (owner == (partner + shards_of // 2) % shards_of)
    return jnp.where(strong, factor * drawn, drawn)


def block_levels(rng, dims, cuts, low, top_value):
    level, own = 1.0, jax.random.fold_in(rng, 6)
    for position, parts in cuts:
        heights = jnp.exp(jax.random.uniform(jax.random.fold_in(own, position), (parts,), jnp.float32, low / len(cuts), top_value / len(cuts)))
        level = level * jnp.repeat(heights, dims[position] // parts).reshape([-1 if axis == position else 1 for axis in range(len(dims))])
    return level


def scatter_about(key, shape, width, limit, shards=(), kind=jnp.bfloat16):
    array = jax.random.normal(key, shape, jnp.float32) * width
    if len(shards) > 0:
        array = block_levels(key, shape, shards, -0.22, 0.18) * array
    return jnp.clip(array, min=-limit, max=limit).astype(kind)


def noise_with(own_key, dims, deviation, limit, cuts, heavy, kind=jnp.bfloat16):
    array = deviation * jax.random.normal(own_key, dims, jnp.float32)
    if cuts:
        array = array * block_levels(own_key, dims, cuts, -0.22, 0.18)
    return jnp.clip(spiked(array, jax.random.fold_in(own_key, 3), *heavy), -limit, limit).astype(kind)


def setup_inputs(seed: int = 0) -> dict:
    keys = jax.random.split(jax.random.key(seed), 8)
    return {
        "sky_map": scatter_about(keys[0], (CYCLES, NPHI, C), 1.0, 6.0, ((0, 4), (1, 8))),
        "pixel_mask": with_ends((jax.random.randint(keys[1], (CYCLES, NPHI), 0, 4) < 3).astype(jnp.int32), jax.random.fold_in(keys[1], 1), 0, 1),
        "noise_factor": draw_noise_factor(jax.random.fold_in(keys[7], 71), 0),
        "cycle_legendre": scatter_about(keys[3], (CYCLES, MMAX, LW), 1.0, 6.0, ((0, 4), (1, 8)), jnp.float32),
        "band_power": jnp.clip(jnp.exp(math.log(10.0) - 4.6051702 * jax.random.uniform(keys[4], (MMAX, LW), jnp.float32) ** block_levels(keys[4], (MMAX, LW), ((0, 8), (1, 4)), -0.2, 0.2)), 0.1, 10.0),
        "channel_cov": draw_channel_cov(jax.random.fold_in(keys[7], 71), 0),
        "test_matrix": noise_with(keys[6], (LW, MMAX, 2, NS), 1.0, 6.0, ((0, 4), (1, 8)), (1, 3, 8, 2.0)),
    }


def reference(sky_map, pixel_mask, noise_factor, cycle_legendre, band_power, channel_cov, test_matrix):
    pieces = sky_map.astype(jnp.float32).reshape(CYCLES, PIECES, NPHI_DEV, C)
    white = jnp.einsum("rqdc,rqjc->rqjd", noise_factor, pieces, precision=lax.Precision.HIGHEST)
    white = white.reshape(CYCLES, NPHI, C) * pixel_mask.astype(jnp.float32)[:, :, None]
    whitened = white.astype(jnp.bfloat16).astype(jnp.float32)
    spectrum = jnp.fft.fft(whitened, axis=1)[:, :MMAX]
    four = jnp.stack([jnp.real(spectrum), jnp.imag(spectrum)], axis=2).astype(jnp.float32)
    alm = jnp.einsum("rmk,rmtc->kmtc", cycle_legendre, four, precision=lax.Precision.HIGHEST)
    mixed = jnp.einsum("dc,kmtc->kmtd", channel_cov, alm, precision=lax.Precision.HIGHEST)
    scaled = (mixed * jnp.transpose(band_power)[:, :, None, None]).astype(jnp.bfloat16)
    left = scaled.reshape(LW * MMAX * 2, C)
    right = test_matrix.reshape(LW * MMAX * 2, NS)
    return jnp.dot(jnp.transpose(left), right, preferred_element_type=jnp.float32)
```

```python
import math

import jax
import jax.numpy as jnp
import ml_dtypes
import numpy as np
from jax import lax
from jax.experimental import pallas as pl
from jax.experimental.pallas import tpu as pltpu
from jax.sharding import PartitionSpec as P

LANES = 128
MIB = 1 << 20


def rotate(value, step, points):
    re, im = value
    step %= points
    if step == 0:
        return re, im
    if 2 * step == points:
        return -re, None if im is None else -im
    if 4 * step == points:
        return im, -re
    c, s = math.cos(2 * math.pi * step / points), math.sin(2 * math.pi * step / points)
    if im is None:
        return re * c, re * (-s)
    return re * c + im * s, im * c - re * s


def plus(one, other):
    return tuple(b if a is None else a if b is None else a + b for a, b in zip(one, other))


def conj(value):
    return value[0], None if value[1] is None else -value[1]


def real_dft(values):
    n = len(values)
    if n == 1:
        return [(values[0], None)]
    half = n // 2
    even, odd = real_dft(values[0::2]), real_dft(values[1::2])

    def get(part, b):
        b %= half
        return part[b] if 2 * b <= half else conj(part[half - b])

    return [plus(get(even, b), rotate(get(odd, b), b, n)) for b in range(half + 1)]


def whiten_kernel(sky_ref, mask_ref, factor_ref, out_ref):
    cycles, chans, pixels = sky_ref.shape
    groups = out_ref.shape[0]
    width = chans // groups
    for r in range(cycles):
        factor = factor_ref[r]
        high = factor.astype(jnp.bfloat16)
        low = (factor - high.astype(jnp.float32)).astype(jnp.bfloat16)
        sky = sky_ref[r]
        white = jnp.dot(high, sky, preferred_element_type=jnp.float32)
        white += jnp.dot(low, sky, preferred_element_type=jnp.float32)
        white = white * mask_ref[r : r + 1, :].astype(jnp.float32)
        out_ref[:, r * width : (r + 1) * width, :] = white.reshape(groups, width, pixels).astype(jnp.bfloat16)


def modes_kernel(z_ref, twiddle_ref, table_ref, leg_ref, out_ref, y_ref, alm_ref):
    radix, rows, pixels = z_ref.shape
    offsets, _, cycles, count = leg_ref.shape
    width = rows // cycles
    half = radix * rows
    chunk = 16

    @pl.loop(0, pixels // LANES)
    def _(tile):
        lanes = pl.ds(pl.multiple_of(tile * LANES, LANES), LANES)
        cosine, sine = twiddle_ref[0, :, lanes], twiddle_ref[1, :, lanes]
        for start in range(0, rows, chunk):
            values = [z_ref[q, start : start + chunk, lanes].astype(jnp.float32) for q in range(radix)]
            parts = real_dft(values)
            for b in range(radix):
                re, im = parts[b] if 2 * b <= radix else conj(parts[radix - b])
                c, s = cosine[b : b + 1, :], sine[b : b + 1, :]
                if b == 0:
                    im = jnp.zeros_like(re)
                elif im is None:
                    re, im = re * c, -(re * s)
                else:
                    re, im = re * c + im * s, im * c - re * s
                place = b * rows + start
                y_ref[place : place + chunk, lanes] = re.astype(jnp.bfloat16)
                y_ref[half + place : half + place + chunk, lanes] = im.astype(jnp.bfloat16)

    @pl.loop(0, count // LANES)
    def _(tile):
        lanes = pl.ds(pl.multiple_of(tile * LANES, LANES), LANES)
        wide = pl.ds(pl.multiple_of(tile * 2 * LANES, 2 * LANES), 2 * LANES)
        table = table_ref[:, wide]
        for b in range(radix):
            re = jnp.dot(y_ref[b * rows : (b + 1) * rows, :], table, preferred_element_type=jnp.float32)
            im = jnp.dot(
                y_ref[half + b * rows : half + (b + 1) * rows, :], table, preferred_element_type=jnp.float32
            )
            real_part = (re[:, :LANES] + im[:, LANES:]).reshape(cycles, width, LANES)
            imag_part = (im[:, :LANES] - re[:, LANES:]).reshape(cycles, width, LANES)
            for k in range(offsets):
                leg = leg_ref[k, b, :, lanes]
                alm_ref[k, 0, b, :, lanes] = jnp.sum(leg[:, None, :] * real_part, axis=0)
                alm_ref[k, 1, b, :, lanes] = jnp.sum(leg[:, None, :] * imag_part, axis=0)

    share = count // radix
    group = LANES // math.gcd(share, LANES)
    for k in range(offsets):
        for t in range(2):
            for d in range(radix):
                for top in range(radix // group):
                    row = (t * (radix // group) + top) * width
                    pieces = [
                        alm_ref[k, t, top * group + g, :, d * share : (d + 1) * share] for g in range(group)
                    ]
                    out_ref[k, d, row : row + width, :] = jnp.concatenate(pieces, axis=-1).astype(jnp.bfloat16)


def sketch_kernel(alm_ref, band_ref, cov_ref, test_ref, out_ref, left_ref):
    patches, groups, rows, lanes = alm_ref.shape
    chans = cov_ref.shape[0]
    width = chans // groups
    for step in range(rows // width):
        part = alm_ref[0, :, step * width : (step + 1) * width, :].astype(jnp.float32)
        for p in range(1, patches):
            part += alm_ref[p, :, step * width : (step + 1) * width, :].astype(jnp.float32)
        place = step * lanes
        band = band_ref[:, place % band_ref.shape[1] : place % band_ref.shape[1] + lanes]
        part = part.reshape(chans, lanes) * band
        left_ref[:, place : place + lanes] = part.astype(jnp.bfloat16)
    sketch = lax.dot_general(
        test_ref[...], left_ref[...], (((0,), (1,)), ((), ())), preferred_element_type=jnp.float32
    )
    mixed = lax.dot_general(
        sketch,
        cov_ref[...],
        (((1,), (1,)), ((), ())),
        precision=lax.Precision.HIGHEST,
        preferred_element_type=jnp.float32,
    )
    out_ref[...] = mixed


def call(kernel, shape, dtype, scratch, mib, *operands):
    return pl.pallas_call(
        kernel,
        out_shape=jax.ShapeDtypeStruct(shape, dtype),
        in_specs=[pl.BlockSpec(memory_space=pltpu.VMEM)] * len(operands),
        out_specs=pl.BlockSpec(memory_space=pltpu.VMEM),
        scratch_shapes=scratch,
        compiler_params=pltpu.CompilerParams(vmem_limit_bytes=mib * MIB),
    )(*operands)


def transform_tables(radix, pixels, count):
    cycle = radix * pixels
    step = np.arange(radix)[:, None] * np.arange(pixels)[None, :] % cycle
    angle = step * (2.0 * math.pi / cycle)
    twiddle = np.stack([np.cos(angle), np.sin(angle)]).astype(np.float32)
    step = np.arange(pixels)[:, None] * np.arange(count)[None, :] % pixels
    angle = step * (2.0 * math.pi / pixels)
    table = np.stack(
        [np.cos(angle).reshape(pixels, -1, LANES), np.sin(angle).reshape(pixels, -1, LANES)], axis=2
    )
    return twiddle, table.reshape(pixels, 2 * count).astype(ml_dtypes.bfloat16)


def local(sky_map, pixel_mask, noise_factor, cycle_legendre, band_power, channel_cov, test_matrix):
    cycles, pixels, chans = sky_map.shape
    modes, _ = band_power.shape
    offsets = cycle_legendre.shape[2]
    columns = test_matrix.shape[3]
    radix, patches = lax.axis_size("mode"), lax.axis_size("patch")
    width = chans // radix
    share = modes // radix
    group = LANES // math.gcd(share, LANES)
    everyone = ("patch", "mode")

    leg = cycle_legendre.reshape(cycles, share, radix, offsets).astype(jnp.bfloat16)
    leg = lax.all_gather(jnp.transpose(leg, (3, 2, 0, 1)), "mode", axis=3, tiled=True).astype(jnp.float32)

    white = call(
        whiten_kernel,
        (radix, cycles * width, pixels),
        jnp.bfloat16,
        [],
        16,
        jnp.transpose(sky_map, (0, 2, 1)),
        pixel_mask,
        noise_factor[:, 0],
    )
    z = lax.all_to_all(white, "mode", 0, 0, tiled=True)

    twiddle, table = transform_tables(radix, pixels, modes)
    rows = 2 * (radix // group) * width
    alm = call(
        modes_kernel,
        (offsets, radix, rows, group * share),
        jnp.bfloat16,
        [
            pltpu.VMEM((2 * radix * cycles * width, pixels), jnp.bfloat16),
            pltpu.VMEM((offsets, 2, radix, width, modes), jnp.float32),
        ],
        32,
        z,
        jnp.asarray(twiddle),
        jnp.asarray(table),
        leg,
    )
    alm = alm.reshape(patches * radix, rows, group * share)
    alm = lax.all_to_all(alm, everyone, 0, 0, tiled=True)
    alm = alm.reshape(patches, radix, rows, group * share)

    right = test_matrix.reshape(share, radix, 2, columns)
    right = jnp.transpose(right, (2, 1, 0, 3)).reshape(2 * modes, columns)
    band = jnp.transpose(band_power.reshape(share, radix)).reshape(1, modes)
    part = call(
        sketch_kernel,
        (columns, chans),
        jnp.float32,
        [pltpu.VMEM((chans, 2 * modes), jnp.bfloat16)],
        24,
        alm,
        band,
        channel_cov,
        right,
    )
    part = part.reshape(patches * radix, columns // (patches * radix), chans)
    part = lax.all_to_all(part, everyone, 0, 0, tiled=True)
    return jnp.transpose(jnp.sum(part, axis=0))


def solution(mesh):
    return jax.shard_map(
        local,
        mesh=mesh,
        in_specs=(
            P("patch", "mode", None),
            P("patch", "mode"),
            P("patch", "mode", None, None),
            P("patch", "mode", None),
            P("mode", "patch"),
            P(),
            P("patch", "mode", None, None),
        ),
        out_specs=P(None, ("patch", "mode")),
        check_vma=False,
    )
```

```python
import math

import jax
import jax.numpy as jnp
import ml_dtypes
import numpy as np
from jax import lax
from jax.experimental import pallas as pl
from jax.experimental.pallas import tpu as pltpu
from jax.sharding import PartitionSpec as P

LANES = 128
MIB = 1 << 20


def rotate(value, step, points):
    re, im = value
    step %= points
    if step == 0:
        return re, im
    if 2 * step == points:
        return -re, -im
    if 4 * step == points:
        return im, -re
    if 8 * step == points:
        return (re + im) * math.sqrt(0.5), (im - re) * math.sqrt(0.5)
    if 8 * step == 3 * points:
        return (im - re) * math.sqrt(0.5), (re + im) * -math.sqrt(0.5)
    c, s = math.cos(2 * math.pi * step / points), math.sin(2 * math.pi * step / points)
    return re * c + im * s, im * c - re * s


def dft(values):
    n = len(values)
    if n == 1:
        return values
    half = n // 2
    even, odd = dft(values[0::2]), dft(values[1::2])
    out = [None] * n
    for b in range(half):
        re, im = rotate(odd[b], b, n)
        out[b] = even[b][0] + re, even[b][1] + im
        out[b + half] = even[b][0] - re, even[b][1] - im
    return out


def whiten_kernel(sky_hbm, mask_hbm, factor_hbm, leg_hbm, sort_hbm, out_ref, sky, mask, factor, leg, sort, white, sems):
    cycles, chans, pixels = sky.shape
    groups = out_ref.shape[0]
    width = chans // groups
    split = pixels // LANES
    sources, targets = (sky_hbm, mask_hbm, factor_hbm, leg_hbm, sort_hbm), (sky, mask, factor, leg, sort)
    copies = [pltpu.make_async_copy(a, b, sems.at[n]) for n, (a, b) in enumerate(zip(sources, targets))]
    for copy in copies:
        copy.start()
    for copy in copies[:3]:
        copy.wait()
    for r in range(cycles):
        high = factor[r].astype(jnp.bfloat16)
        low = (factor[r] - high.astype(jnp.float32)).astype(jnp.bfloat16)
        both = jnp.concatenate([high, low], axis=1)
        pair = jnp.concatenate([sky[r], sky[r]], axis=0)
        value = jnp.dot(both, pair, preferred_element_type=jnp.float32)
        value = value * mask[r : r + 1, :].astype(jnp.float32)
        white[r * chans : (r + 1) * chans, :] = value.astype(jnp.bfloat16)
    copies[3].wait()
    rows = jnp.concatenate([leg[r] for r in range(cycles)], axis=0).astype(jnp.bfloat16)
    count = rows.shape[0]
    start = split * cycles * width
    for n in range(rows.shape[1] // LANES):
        for e in range(groups):
            out_ref[e, start + n * count : start + (n + 1) * count, :] = rows[:, n * LANES : (n + 1) * LANES]
    copies[4].wait()
    for pair in range(split // 2):
        wide = slice(pair * 2 * LANES, (pair + 1) * 2 * LANES)
        value = jnp.dot(white[...], sort[:, wide], preferred_element_type=jnp.float32)
        for half in range(2):
            s = pair * 2 + half
            part = value[:, half * LANES : (half + 1) * LANES]
            part = part.reshape(cycles, groups, width, LANES)
            part = jnp.swapaxes(part, 0, 1).reshape(groups, cycles * width, LANES).astype(jnp.bfloat16)
            out_ref[:, s * cycles * width : (s + 1) * cycles * width, :] = part


def modes_kernel(cycles, offsets, z_ref, twiddle_ref, table_hbm, out_ref, table, left, leg, prod_a, prod_b, x_ref, sems):
    sources = z_ref.shape[0]
    tiles = table.shape[0]
    split = twiddle_ref.shape[1]
    rows = left.shape[0]
    width = rows // (cycles * split)
    blocks = leg.shape[1] // (tiles * LANES)
    per = out_ref.shape[3] // LANES
    copies = [pltpu.make_async_copy(table_hbm.at[n], table.at[n], sems.at[n]) for n in range(tiles)]
    for copy in copies:
        copy.start()
    count = cycles * offsets
    for q in range(sources):
        left[:, q * LANES : (q + 1) * LANES] = z_ref[q, :rows, :]
        for n in range(per):
            place = (q * per + n) * LANES
            leg[:, place : place + LANES] = z_ref[q, rows + n * count : rows + (n + 1) * count, :].astype(jnp.float32)

    def product(tile, prod):
        copies[tile].wait()
        prod[...] = jnp.dot(left[...], table[tile], preferred_element_type=jnp.float32)

    def use(tile, prod):
        lanes = slice(tile * LANES, (tile + 1) * LANES)
        cosine, sine = twiddle_ref[0, :, lanes], twiddle_ref[1, :, lanes]
        for r in range(cycles):
            values = []
            for s in range(split):
                place = (s * cycles + r) * width
                re = prod[place : place + width, :LANES]
                im = prod[place : place + width, LANES:]
                if s == 0:
                    values.append((re, -im))
                else:
                    c, d = cosine[s : s + 1, :], sine[s : s + 1, :]
                    values.append((re * c - im * d, -(re * d) - im * c))
            parts = dft(values)
            for b in range(blocks):
                x_ref[b, 0, r] = parts[b][0]
                x_ref[b, 1, r] = parts[b][1]
        for b in range(blocks):
            mode_tile = b * tiles + tile
            d, n = mode_tile // per, mode_tile % per
            mode = slice(mode_tile * LANES, (mode_tile + 1) * LANES)
            for k in range(offsets):
                total = [None, None]
                for r in range(cycles):
                    row = leg[r * offsets + k : r * offsets + k + 1, mode]
                    for t in range(2):
                        term = row * x_ref[b, t, r]
                        total[t] = term if r == 0 else total[t] + term
                out_ref[k, d, :, n * LANES : (n + 1) * LANES] = jnp.concatenate(total, axis=0).astype(jnp.bfloat16)

    prods = (prod_a, prod_b)
    product(0, prods[0])
    for tile in range(tiles):
        if tile + 1 < tiles:
            product(tile + 1, prods[(tile + 1) % 2])
        use(tile, prods[tile % 2])


def sketch_kernel(alm_ref, band_ref, cov_ref, test_ref, out_ref, left_ref):
    patches, groups, rows, lanes = alm_ref.shape
    chans = cov_ref.shape[0]
    width = rows // 2
    for g in range(groups):
        part = alm_ref[0, g].astype(jnp.float32)
        for p in range(1, patches):
            part += alm_ref[p, g].astype(jnp.float32)
        part = part * band_ref[...]
        for t in range(2):
            left_ref[t, g * width : (g + 1) * width, :] = part[t * width : (t + 1) * width]
    sketch = None
    for t in range(2):
        term = lax.dot_general(
            test_ref[t],
            left_ref[t].astype(jnp.bfloat16),
            (((0,), (1,)), ((), ())),
            preferred_element_type=jnp.float32,
        )
        sketch = term if t == 0 else sketch + term
    mixed = lax.dot_general(
        sketch,
        cov_ref[...],
        (((1,), (1,)), ((), ())),
        precision=lax.Precision.HIGHEST,
        preferred_element_type=jnp.float32,
    )
    if out_ref.ndim == 2:
        out_ref[...] = mixed
    else:
        owners, block, _ = out_ref.shape
        fold = out_ref.shape[2] // chans
        mixed = mixed.reshape(owners, fold, block, chans)
        out_ref[...] = jnp.concatenate([mixed[:, n] for n in range(fold)], axis=-1)


def total_kernel(part_ref, out_ref):
    block, chans = part_ref.shape[1], out_ref.shape[1]
    total = jnp.sum(part_ref[...], axis=0)
    for n in range(part_ref.shape[2] // chans):
        out_ref[n * block : (n + 1) * block, :] = total[:, n * chans : (n + 1) * chans]


def call(kernel, shape, dtype, scratch, mib, spaces, *operands):
    return pl.pallas_call(
        kernel,
        out_shape=jax.ShapeDtypeStruct(shape, dtype),
        in_specs=[pl.BlockSpec(memory_space=space) for space in spaces],
        out_specs=pl.BlockSpec(memory_space=pltpu.VMEM),
        scratch_shapes=scratch,
        compiler_params=pltpu.CompilerParams(vmem_limit_bytes=mib * MIB),
    )(*operands)


def transform_tables(split, cycle):
    half = cycle // split
    step = np.arange(split)[:, None] * np.arange(half)[None, :] % cycle
    angle = step * (2.0 * math.pi / cycle)
    twiddle = np.stack([np.cos(angle), np.sin(angle)]).astype(np.float32)
    step = np.arange(half)[:, None] * np.arange(half)[None, :] % half
    angle = (step * (2.0 * math.pi / half)).reshape(half, half // LANES, LANES)
    table = np.transpose(np.concatenate([np.cos(angle), np.sin(angle)], axis=2), (1, 0, 2))
    return twiddle, table.astype(ml_dtypes.bfloat16)


def sorting(pixels, split):
    place = np.arange(pixels) % split * (pixels // split) + np.arange(pixels) // split
    return (place[:, None] == np.arange(pixels)[None, :]).astype(ml_dtypes.bfloat16)


def local(sky_map, pixel_mask, noise_factor, cycle_legendre, band_power, channel_cov, test_matrix):
    cycles, pixels, chans = sky_map.shape
    modes, _ = band_power.shape
    offsets = cycle_legendre.shape[2]
    columns = test_matrix.shape[3]
    mode_count, patches = lax.axis_size("mode"), lax.axis_size("patch")
    width = chans // mode_count
    split = pixels // LANES
    rows = split * cycles * width
    legs = cycles * offsets * (modes // LANES)
    tiles = mode_count
    everyone = ("patch", "mode")
    hbm, vmem, bf16, f32 = pl.ANY, pltpu.VMEM, jnp.bfloat16, jnp.float32

    message = call(
        whiten_kernel,
        (mode_count, rows + legs, LANES),
        bf16,
        [
            vmem((cycles, chans, pixels), bf16),
            vmem((cycles, pixels), jnp.int32),
            vmem((cycles, chans, chans), f32),
            vmem((cycles, offsets, modes), f32),
            vmem((pixels, pixels), bf16),
            vmem((cycles * chans, pixels), bf16),
            pltpu.SemaphoreType.DMA((5,)),
        ],
        56,
        [hbm] * 5,
        jnp.transpose(sky_map, (0, 2, 1)),
        pixel_mask,
        noise_factor[:, 0],
        jnp.transpose(cycle_legendre, (0, 2, 1)),
        jnp.asarray(sorting(pixels, split)),
    )
    message = lax.all_to_all(message, "mode", 0, 0, tiled=True)

    twiddle, table = transform_tables(split, pixels * mode_count)
    blocks = modes * mode_count // (tiles * LANES)
    alm = call(
        lambda *refs: modes_kernel(cycles, offsets, *refs),
        (offsets, mode_count, 2 * width, modes),
        bf16,
        [
            vmem((tiles, tiles * LANES, 2 * LANES), bf16),
            vmem((rows, tiles * LANES), bf16),
            vmem((cycles * offsets, mode_count * modes), f32),
            vmem((rows, 2 * LANES), f32),
            vmem((rows, 2 * LANES), f32),
            vmem((blocks, 2, cycles, width, LANES), f32),
            pltpu.SemaphoreType.DMA((tiles,)),
        ],
        56,
        [vmem, vmem, hbm],
        message,
        jnp.asarray(twiddle),
        jnp.asarray(table),
    )
    alm = alm.reshape(patches * mode_count, 2 * width, modes)
    alm = lax.all_to_all(alm, everyone, 0, 0, tiled=True)
    alm = alm.reshape(patches, mode_count, 2 * width, modes)

    share = columns // (patches * mode_count)
    fold = LANES // chans
    packed = share % (8 * fold) == 0
    part = call(
        sketch_kernel,
        (patches * mode_count, share // fold, LANES) if packed else (columns, chans),
        f32,
        [vmem((2, chans, modes), f32)],
        24,
        [vmem] * 4,
        alm,
        jnp.transpose(band_power),
        channel_cov,
        jnp.transpose(test_matrix[0], (1, 0, 2)),
    )
    if not packed:
        part = part.reshape(patches * mode_count, share, chans)
    part = lax.all_to_all(part, everyone, 0, 0, tiled=True)
    return jnp.transpose(call(total_kernel, (share, chans), f32, [], 16, [vmem], part))


def solution(mesh):
    return jax.shard_map(
        local,
        mesh=mesh,
        in_specs=(
            P("patch", "mode", None),
            P("patch", "mode"),
            P("patch", "mode", None, None),
            P("patch", "mode", None),
            P("mode", "patch"),
            P(),
            P("patch", "mode", None, None),
        ),
        out_specs=P(None, ("patch", "mode")),
        check_vma=False,
    )
```

```python
import math

import jax
import jax.numpy as jnp
import ml_dtypes
import numpy as np
from jax import lax
from jax.experimental import pallas as pl
from jax.experimental.pallas import tpu as pltpu
from jax.sharding import PartitionSpec as P

LANES = 128
MIB = 1 << 20


def rotate(value, step, points):
    re, im = value
    step %= points
    if step == 0:
        return re, im
    if 2 * step == points:
        return -re, -im
    if 4 * step == points:
        return im, -re
    if 8 * step == points:
        return (re + im) * math.sqrt(0.5), (im - re) * math.sqrt(0.5)
    if 8 * step == 3 * points:
        return (im - re) * math.sqrt(0.5), (re + im) * -math.sqrt(0.5)
    c, s = math.cos(2 * math.pi * step / points), math.sin(2 * math.pi * step / points)
    return re * c + im * s, im * c - re * s


def dft(values):
    n = len(values)
    if n == 1:
        return values
    half = n // 2
    even, odd = dft(values[0::2]), dft(values[1::2])
    out = [None] * n
    for b in range(half):
        re, im = rotate(odd[b], b, n)
        out[b] = even[b][0] + re, even[b][1] + im
        out[b + half] = even[b][0] - re, even[b][1] - im
    return out


def whiten_kernel(me_ref, sky_hbm, mask_hbm, factor_hbm, leg_hbm, sort_hbm, *refs):
    sky, mask, factor, leg, sort, white, stage, sems = refs[-8:]
    outs = refs[:-8]
    cycles, chans, pixels = sky.shape
    groups = len(outs)
    width = chans // groups
    split = pixels // LANES
    sources, targets = (sky_hbm, mask_hbm, factor_hbm, leg_hbm, sort_hbm), (sky, mask, factor, leg, sort)
    copies = [pltpu.make_async_copy(a, b, sems.at[n]) for n, (a, b) in enumerate(zip(sources, targets))]
    for copy in copies:
        copy.start()
    for copy in copies[:3]:
        copy.wait()
    for r in range(cycles):
        high = factor[r].astype(jnp.bfloat16)
        low = (factor[r] - high.astype(jnp.float32)).astype(jnp.bfloat16)
        both = jnp.concatenate([high, low], axis=1)
        pair = jnp.concatenate([sky[r], sky[r]], axis=0)
        value = jnp.dot(both, pair, preferred_element_type=jnp.float32)
        value = value * mask[r : r + 1, :].astype(jnp.float32)
        white[r * chans : (r + 1) * chans, :] = value.astype(jnp.bfloat16)
    copies[3].wait()
    rows = jnp.concatenate([leg[r] for r in range(cycles)], axis=0).astype(jnp.bfloat16)
    count = rows.shape[0]
    start = split * cycles * width
    for n in range(rows.shape[1] // LANES):
        for e in range(groups):
            stage[e, start + n * count : start + (n + 1) * count, :] = rows[:, n * LANES : (n + 1) * LANES]
    copies[4].wait()
    for pair in range(split // 2):
        wide = slice(pair * 2 * LANES, (pair + 1) * 2 * LANES)
        value = jnp.dot(white[...], sort[:, wide], preferred_element_type=jnp.float32)
        for half in range(2):
            s = pair * 2 + half
            part = value[:, half * LANES : (half + 1) * LANES]
            part = part.reshape(cycles, groups, width, LANES)
            part = jnp.swapaxes(part, 0, 1).reshape(groups, cycles * width, LANES).astype(jnp.bfloat16)
            stage[:, s * cycles * width : (s + 1) * cycles * width, :] = part
    me = me_ref[0]
    sends = [
        pltpu.make_async_copy(stage.at[jnp.bitwise_xor(me, n)], outs[n], sems.at[5 + n]) for n in range(groups)
    ]
    for send in sends:
        send.start()
    for send in sends:
        send.wait()


def modes_kernel(cycles, offsets, sources, me_ref, twiddle_ref, table_hbm, *refs):
    slots = refs[:sources]
    out_ref, table, left, leg, prod_a, prod_b, x_ref, table_sems = refs[sources:]
    tiles = table.shape[0]
    split = twiddle_ref.shape[1]
    rows = left.shape[0]
    width = rows // (cycles * split)
    blocks = leg.shape[1] // (tiles * LANES)
    per = out_ref.shape[3] // LANES
    count = cycles * offsets
    me = me_ref[0]
    def copy(tile):
        return pltpu.make_async_copy(table_hbm.at[tile], table.at[tile], table_sems.at[tile])

    for tile in range(tiles):
        copy(tile).start()
    for slot in range(sources):
        q = jnp.bitwise_xor(me, slot)
        left[:, pl.ds(pl.multiple_of(q * LANES, LANES), LANES)] = slots[slot][:rows, :]
        for n in range(per):
            lanes = pl.ds(pl.multiple_of((q * per + n) * LANES, LANES), LANES)
            leg[:, lanes] = slots[slot][rows + n * count : rows + (n + 1) * count, :].astype(jnp.float32)

    def product(tile, prod):
        prod[...] = jnp.dot(left[...], table[tile], preferred_element_type=jnp.float32)

    def use(tile, prod):
        lanes = pl.ds(pl.multiple_of(tile * LANES, LANES), LANES)
        cosine, sine = twiddle_ref[0, :, lanes], twiddle_ref[1, :, lanes]
        for r in range(cycles):
            values = []
            for s in range(split):
                place = (s * cycles + r) * width
                re = prod[place : place + width, :LANES]
                im = prod[place : place + width, LANES:]
                if s == 0:
                    values.append((re, -im))
                else:
                    c, d = cosine[s : s + 1, :], sine[s : s + 1, :]
                    values.append((re * c - im * d, -(re * d) - im * c))
            parts = dft(values)
            for b in range(blocks):
                x_ref[b, 0, r] = parts[b][0]
                x_ref[b, 1, r] = parts[b][1]
        for b in range(blocks):
            mode_tile = b * tiles + tile
            d, n = mode_tile // per, mode_tile % per
            mode = pl.ds(pl.multiple_of(mode_tile * LANES, LANES), LANES)
            for k in range(offsets):
                total = [None, None]
                for r in range(cycles):
                    row = leg[r * offsets + k : r * offsets + k + 1, mode]
                    for t in range(2):
                        term = row * x_ref[b, t, r]
                        total[t] = term if r == 0 else total[t] + term
                place = pl.ds(pl.multiple_of(n * LANES, LANES), LANES)
                out_ref[k, d, :, place] = jnp.concatenate(total, axis=0).astype(jnp.bfloat16)

    copy(0).wait()
    product(0, prod_a)

    @pl.loop(0, tiles // 2)
    def _(step):
        copy(2 * step + 1).wait()

        @pl.when(2 * step + 2 < tiles)
        def _():
            copy(2 * step + 2).wait()

        product(2 * step + 1, prod_b)
        use(2 * step, prod_a)
        product(jnp.minimum(2 * step + 2, tiles - 1), prod_a)
        use(2 * step + 1, prod_b)


def sketch_kernel(alm_ref, band_ref, cov_ref, test_ref, out_ref, left_ref):
    patches, groups, rows, lanes = alm_ref.shape
    chans = cov_ref.shape[0]
    width = rows // 2
    for g in range(groups):
        part = alm_ref[0, g].astype(jnp.float32)
        for p in range(1, patches):
            part += alm_ref[p, g].astype(jnp.float32)
        part = part * band_ref[...]
        for t in range(2):
            left_ref[t, g * width : (g + 1) * width, :] = part[t * width : (t + 1) * width]
    sketch = None
    for t in range(2):
        term = lax.dot_general(
            test_ref[t],
            left_ref[t].astype(jnp.bfloat16),
            (((0,), (1,)), ((), ())),
            preferred_element_type=jnp.float32,
        )
        sketch = term if t == 0 else sketch + term
    mixed = lax.dot_general(
        sketch,
        cov_ref[...],
        (((1,), (1,)), ((), ())),
        precision=lax.Precision.HIGHEST,
        preferred_element_type=jnp.float32,
    )
    if out_ref.ndim == 2:
        out_ref[...] = mixed
    else:
        owners, block, _ = out_ref.shape
        fold = out_ref.shape[2] // chans
        mixed = mixed.reshape(owners, fold, block, chans)
        out_ref[...] = jnp.concatenate([mixed[:, n] for n in range(fold)], axis=-1)


def total_kernel(part_ref, out_ref):
    block, chans = part_ref.shape[1], out_ref.shape[1]
    total = jnp.sum(part_ref[...], axis=0)
    for n in range(part_ref.shape[2] // chans):
        out_ref[n * block : (n + 1) * block, :] = total[:, n * chans : (n + 1) * chans]


def call(kernel, shape, scratch, mib, spaces, *operands, out_space=pltpu.VMEM):
    return pl.pallas_call(
        kernel,
        out_shape=shape,
        in_specs=[pl.BlockSpec(memory_space=space) for space in spaces],
        out_specs=jax.tree.map(lambda _: pl.BlockSpec(memory_space=out_space), shape),
        scratch_shapes=scratch,
        compiler_params=pltpu.CompilerParams(vmem_limit_bytes=mib * MIB),
    )(*operands)


def transform_tables(split, cycle):
    half = cycle // split
    step = np.arange(split)[:, None] * np.arange(half)[None, :] % cycle
    angle = step * (2.0 * math.pi / cycle)
    twiddle = np.stack([np.cos(angle), np.sin(angle)]).astype(np.float32)
    step = np.arange(half)[:, None] * np.arange(half)[None, :] % half
    angle = (step * (2.0 * math.pi / half)).reshape(half, half // LANES, LANES)
    table = np.transpose(np.concatenate([np.cos(angle), np.sin(angle)], axis=2), (1, 0, 2))
    return twiddle, table.astype(ml_dtypes.bfloat16)


def sorting(pixels, split):
    place = np.arange(pixels) % split * (pixels // split) + np.arange(pixels) // split
    return (place[:, None] == np.arange(pixels)[None, :]).astype(ml_dtypes.bfloat16)


def local(sky_map, pixel_mask, noise_factor, cycle_legendre, band_power, channel_cov, test_matrix):
    cycles, pixels, chans = sky_map.shape
    modes, _ = band_power.shape
    offsets = cycle_legendre.shape[2]
    columns = test_matrix.shape[3]
    mode_count, patches = lax.axis_size("mode"), lax.axis_size("patch")
    width = chans // mode_count
    split = pixels // LANES
    rows = split * cycles * width
    legs = cycles * offsets * (modes // LANES)
    tiles = mode_count
    everyone = ("patch", "mode")
    hbm, vmem, bf16, f32 = pl.ANY, pltpu.VMEM, jnp.bfloat16, jnp.float32

    me = lax.axis_index("mode").astype(jnp.int32).reshape(1)
    shape = jax.ShapeDtypeStruct
    messages = call(
        whiten_kernel,
        [shape((rows + legs, LANES), bf16)] * mode_count,
        [
            vmem((cycles, chans, pixels), bf16),
            vmem((cycles, pixels), jnp.int32),
            vmem((cycles, chans, chans), f32),
            vmem((cycles, offsets, modes), f32),
            vmem((pixels, pixels), bf16),
            vmem((cycles * chans, pixels), bf16),
            vmem((mode_count, rows + legs, LANES), bf16),
            pltpu.SemaphoreType.DMA((5 + mode_count,)),
        ],
        56,
        [pltpu.SMEM] + [hbm] * 5,
        me,
        jnp.transpose(sky_map, (0, 2, 1)),
        pixel_mask,
        noise_factor[:, 0],
        jnp.transpose(cycle_legendre, (0, 2, 1)),
        jnp.asarray(sorting(pixels, split)),
        out_space=hbm,
    )
    slots = [messages[0]]
    for n in range(1, mode_count):
        slots.append(lax.ppermute(messages[n], "mode", [(i, i ^ n) for i in range(mode_count)]))

    twiddle, table = transform_tables(split, pixels * mode_count)
    blocks = modes * mode_count // (tiles * LANES)
    alm = call(
        lambda *refs: modes_kernel(cycles, offsets, mode_count, *refs),
        shape((offsets, mode_count, 2 * width, modes), bf16),
        [
            vmem((tiles, tiles * LANES, 2 * LANES), bf16),
            vmem((rows, tiles * LANES), bf16),
            vmem((cycles * offsets, mode_count * modes), f32),
            vmem((rows, 2 * LANES), f32),
            vmem((rows, 2 * LANES), f32),
            vmem((blocks, 2, cycles, width, LANES), f32),
            pltpu.SemaphoreType.DMA((tiles,)),
        ],
        56,
        [pltpu.SMEM, vmem, hbm] + [vmem] * mode_count,
        me,
        jnp.asarray(twiddle),
        jnp.asarray(table),
        *slots,
    )
    alm = alm.reshape(patches * mode_count, 2 * width, modes)
    alm = lax.all_to_all(alm, everyone, 0, 0, tiled=True)
    alm = alm.reshape(patches, mode_count, 2 * width, modes)

    share = columns // (patches * mode_count)
    fold = LANES // chans
    packed = share % (8 * fold) == 0
    part = call(
        sketch_kernel,
        shape((patches * mode_count, share // fold, LANES) if packed else (columns, chans), f32),
        [vmem((2, chans, modes), f32)],
        24,
        [vmem] * 4,
        alm,
        jnp.transpose(band_power),
        channel_cov,
        jnp.transpose(test_matrix[0], (1, 0, 2)),
    )
    if not packed:
        part = part.reshape(patches * mode_count, share, chans)
    part = lax.all_to_all(part, everyone, 0, 0, tiled=True)
    return jnp.transpose(call(total_kernel, shape((share, chans), f32), [], 16, [vmem], part))


def solution(mesh):
    return jax.shard_map(
        local,
        mesh=mesh,
        in_specs=(
            P("patch", "mode", None),
            P("patch", "mode"),
            P("patch", "mode", None, None),
            P("patch", "mode", None),
            P("mode", "patch"),
            P(),
            P("patch", "mode", None, None),
        ),
        out_specs=P(None, ("patch", "mode")),
        check_vma=False,
    )
```

```python
import functools
import math

import jax
import jax.numpy as jnp
import ml_dtypes
import numpy as np
from jax import lax
from jax.experimental import pallas as pl
from jax.experimental.pallas import tpu as pltpu
from jax.sharding import PartitionSpec as P

LANES = 128
MIB = 1 << 20
HALVES = 2


def rotate(value, step, points):
    re, im = value
    step %= points
    if step == 0:
        return re, im
    if 2 * step == points:
        return -re, -im
    if 4 * step == points:
        return im, -re
    if 8 * step == points:
        return (re + im) * math.sqrt(0.5), (im - re) * math.sqrt(0.5)
    if 8 * step == 3 * points:
        return (im - re) * math.sqrt(0.5), (re + im) * -math.sqrt(0.5)
    c, s = math.cos(2 * math.pi * step / points), math.sin(2 * math.pi * step / points)
    return re * c + im * s, im * c - re * s


def dft(values):
    n = len(values)
    if n == 1:
        return values
    half = n // 2
    even, odd = dft(values[0::2]), dft(values[1::2])
    out = [None] * n
    for b in range(half):
        re, im = rotate(odd[b], b, n)
        out[b] = even[b][0] + re, even[b][1] + im
        out[b + half] = even[b][0] - re, even[b][1] - im
    return out


def whiten_kernel(half, with_leg, me_ref, after_ref, sky_hbm, mask_hbm, factor_hbm, leg_hbm, sort_hbm, *refs):
    sky, mask, factor, leg, sort, white, stage, sems = refs[-8:]
    outs = refs[:-8]
    cycles, chans, pixels = sky.shape
    groups = len(outs)
    part = white.shape[0] // cycles
    width = part // groups
    split = pixels // LANES
    sources, targets = (sky_hbm, mask_hbm, factor_hbm, sort_hbm), (sky, mask, factor, sort)
    if with_leg:
        sources, targets = sources + (leg_hbm,), targets + (leg,)
    copies = [pltpu.make_async_copy(a, b, sems.at[n]) for n, (a, b) in enumerate(zip(sources, targets))]
    for copy in copies:
        copy.start()
    for copy in copies[:3]:
        copy.wait()
    for r in range(cycles):
        rows = factor[r, half * part : (half + 1) * part, :]
        high = rows.astype(jnp.bfloat16)
        low = (rows - high.astype(jnp.float32)).astype(jnp.bfloat16)
        both = jnp.concatenate([high, low], axis=1)
        pair = jnp.concatenate([sky[r], sky[r]], axis=0)
        value = jnp.dot(both, pair, preferred_element_type=jnp.float32)
        value = value * mask[r : r + 1, :].astype(jnp.float32)
        white[r * part : (r + 1) * part, :] = value.astype(jnp.bfloat16)
    for copy in copies[3:]:
        copy.wait()
    start = split * cycles * width
    if with_leg:
        rows = jnp.concatenate([leg[r] for r in range(cycles)], axis=0).astype(jnp.bfloat16)
        count = rows.shape[0]
        for n in range(rows.shape[1] // LANES):
            for e in range(groups):
                stage[e, start + n * count : start + (n + 1) * count, :] = rows[:, n * LANES : (n + 1) * LANES]
    for pair in range(split // 2):
        wide = slice(pair * 2 * LANES, (pair + 1) * 2 * LANES)
        value = jnp.dot(white[...], sort[:, wide], preferred_element_type=jnp.float32)
        for side in range(2):
            s = pair * 2 + side
            block = value[:, side * LANES : (side + 1) * LANES]
            for e in range(groups):
                rows = [block[r * part + e * width : r * part + (e + 1) * width] for r in range(cycles)]
                rows = jnp.concatenate(rows, axis=0).astype(jnp.bfloat16)
                stage[e, s * cycles * width : (s + 1) * cycles * width, :] = rows
    me = me_ref[0]
    sends = [
        pltpu.make_async_copy(stage.at[jnp.bitwise_xor(me, n)], outs[n], sems.at[5 + n]) for n in range(groups)
    ]
    for send in sends:
        send.start()
    for send in sends:
        send.wait()


def modes_kernel(cycles, offsets, sources, own_leg, me_ref, after_ref, twiddle_ref, table_hbm, *refs):
    slots, legs = refs[:sources], refs[sources : 2 * sources]
    out_ref, table, left, leg, prod_a, prod_b, x_ref, table_sems = refs[2 * sources :]
    tiles = table.shape[0]
    split = twiddle_ref.shape[1]
    rows = left.shape[0]
    width = rows // (cycles * split)
    group = x_ref.shape[3] // width
    blocks = leg.shape[1] // (tiles * LANES)
    per = out_ref.shape[3] // LANES
    count = cycles * offsets
    me = me_ref[0]

    def copy(tile):
        return pltpu.make_async_copy(table_hbm.at[tile], table.at[tile], table_sems.at[tile])

    for tile in range(tiles):
        copy(tile).start()
    for slot in range(sources):
        q = jnp.bitwise_xor(me, slot)
        left[:, pl.ds(pl.multiple_of(q * LANES, LANES), LANES)] = slots[slot][:rows, :]
        for n in range(per):
            lanes = pl.ds(pl.multiple_of((q * per + n) * LANES, LANES), LANES)
            leg[:, lanes] = legs[slot][own_leg + n * count : own_leg + (n + 1) * count, :].astype(jnp.float32)

    def product(tile, prod):
        prod[...] = jnp.dot(left[...], table[tile], preferred_element_type=jnp.float32)

    def use(tile, prod):
        lanes = pl.ds(pl.multiple_of(tile * LANES, LANES), LANES)
        cosine, sine = twiddle_ref[0, :, lanes], twiddle_ref[1, :, lanes]
        tall = group * width
        place_in = lax.broadcasted_iota(jnp.int32, (tall, LANES), 0)
        for pack in range(cycles // group):
            values = []
            for s in range(split):
                place = (s * cycles + pack * group) * width
                re = prod[place : place + tall, :LANES]
                im = prod[place : place + tall, LANES:]
                if s == 0:
                    values.append((re, -im))
                else:
                    c, d = cosine[s : s + 1, :], sine[s : s + 1, :]
                    values.append((re * c - im * d, -(re * d) - im * c))
            parts = dft(values)
            for b in range(blocks):
                x_ref[b, 0, pack] = parts[b][0]
                x_ref[b, 1, pack] = parts[b][1]
        for b in range(blocks):
            mode_tile = b * tiles + tile
            d, n = mode_tile // per, mode_tile % per
            mode = pl.ds(pl.multiple_of(mode_tile * LANES, LANES), LANES)
            for k in range(offsets):
                total = [None, None]
                for pack in range(cycles // group):
                    row = None
                    for g in range(group):
                        r = pack * group + g
                        next_row = leg[r * offsets + k : r * offsets + k + 1, mode]
                        if g == 0:
                            row = jnp.broadcast_to(next_row, (tall, LANES))
                        else:
                            row = jnp.where(place_in < g * width, row, next_row)
                    for t in range(2):
                        term = row * x_ref[b, t, pack]
                        total[t] = term if pack == 0 else total[t] + term
                step = tall // 2
                while step >= width:
                    total = [value + pltpu.roll(value, step, 0) for value in total]
                    step //= 2
                if group == 1:
                    both = jnp.concatenate(total, axis=0)
                else:
                    both = jnp.where(place_in < width, total[0], total[1])[: 2 * width]
                place = pl.ds(pl.multiple_of(n * LANES, LANES), LANES)
                out_ref[k, d, :, place] = both.astype(jnp.bfloat16)

    copy(0).wait()
    product(0, prod_a)

    @pl.loop(0, tiles // 2)
    def _(step):
        copy(2 * step + 1).wait()

        @pl.when(2 * step + 2 < tiles)
        def _():
            copy(2 * step + 2).wait()

        product(2 * step + 1, prod_b)
        use(2 * step, prod_a)
        product(jnp.minimum(2 * step + 2, tiles - 1), prod_a)
        use(2 * step + 1, prod_b)


def sketch_kernel(band_ref, cov_ref, test_ref, *refs):
    out_ref, left_ref = refs[-2:]
    chans = cov_ref.shape[0]
    for half, alm_ref in enumerate(refs[:-2]):
        patches, groups, rows, lanes = alm_ref.shape
        width = rows // 2
        for g in range(groups):
            part = alm_ref[0, g].astype(jnp.float32)
            for p in range(1, patches):
                part += alm_ref[p, g].astype(jnp.float32)
            part = part * band_ref[...]
            place = (half * groups + g) * width
            for t in range(2):
                left_ref[t, place : place + width, :] = part[t * width : (t + 1) * width]
    sketch = None
    for t in range(2):
        term = lax.dot_general(
            test_ref[t],
            left_ref[t].astype(jnp.bfloat16),
            (((0,), (1,)), ((), ())),
            preferred_element_type=jnp.float32,
        )
        sketch = term if t == 0 else sketch + term
    mixed = lax.dot_general(
        sketch,
        cov_ref[...],
        (((1,), (1,)), ((), ())),
        precision=lax.Precision.HIGHEST,
        preferred_element_type=jnp.float32,
    )
    if out_ref.ndim == 2:
        out_ref[...] = mixed
    else:
        owners, block, _ = out_ref.shape
        fold = out_ref.shape[2] // chans
        mixed = mixed.reshape(owners, fold, block, chans)
        out_ref[...] = jnp.concatenate([mixed[:, n] for n in range(fold)], axis=-1)


def total_kernel(part_ref, out_ref):
    block, chans = part_ref.shape[1], out_ref.shape[1]
    total = jnp.sum(part_ref[...], axis=0)
    for n in range(part_ref.shape[2] // chans):
        out_ref[n * block : (n + 1) * block, :] = total[:, n * chans : (n + 1) * chans]


def call(kernel, shape, scratch, mib, spaces, *operands, out_space=pltpu.VMEM, cost=(0, 0)):
    return pl.pallas_call(
        kernel,
        out_shape=shape,
        in_specs=[pl.BlockSpec(memory_space=space) for space in spaces],
        out_specs=jax.tree.map(lambda _: pl.BlockSpec(memory_space=out_space), shape),
        scratch_shapes=scratch,
        compiler_params=pltpu.CompilerParams(vmem_limit_bytes=mib * MIB),
        cost_estimate=pl.CostEstimate(flops=cost[0], bytes_accessed=cost[1], transcendentals=0),
    )(*operands)


def transform_tables(split, cycle):
    half = cycle // split
    step = np.arange(split)[:, None] * np.arange(half)[None, :] % cycle
    angle = step * (2.0 * math.pi / cycle)
    twiddle = np.stack([np.cos(angle), np.sin(angle)]).astype(np.float32)
    step = np.arange(half)[:, None] * np.arange(half)[None, :] % half
    angle = (step * (2.0 * math.pi / half)).reshape(half, half // LANES, LANES)
    table = np.transpose(np.concatenate([np.cos(angle), np.sin(angle)], axis=2), (1, 0, 2))
    return twiddle, table.astype(ml_dtypes.bfloat16)


def sorting(pixels, split):
    place = np.arange(pixels) % split * (pixels // split) + np.arange(pixels) // split
    return (place[:, None] == np.arange(pixels)[None, :]).astype(ml_dtypes.bfloat16)


def local(sky_map, pixel_mask, noise_factor, cycle_legendre, band_power, channel_cov, test_matrix):
    cycles, pixels, chans = sky_map.shape
    modes, _ = band_power.shape
    offsets = cycle_legendre.shape[2]
    columns = test_matrix.shape[3]
    mode_count, patches = lax.axis_size("mode"), lax.axis_size("patch")
    part_chans = chans // HALVES
    width = part_chans // mode_count
    group = max(1, 8 // width)
    split = pixels // LANES
    rows = split * cycles * width
    legs = cycles * offsets * (modes // LANES)
    tiles = mode_count
    blocks = modes * mode_count // (tiles * LANES)
    everyone = ("patch", "mode")
    hbm, vmem, bf16, f32, shape = pl.ANY, pltpu.VMEM, jnp.bfloat16, jnp.float32, jax.ShapeDtypeStruct

    me = lax.axis_index("mode").astype(jnp.int32).reshape(1)
    twiddle, table = transform_tables(split, pixels * mode_count)
    twiddle, table = jnp.asarray(twiddle), jnp.asarray(table)
    sort = jnp.asarray(sorting(pixels, split))
    order = sorted(range(1, mode_count), key=lambda n: (n < 2, -(n // 2 & n // 4 & 1), n % 2))

    sky = jnp.transpose(sky_map, (0, 2, 1))
    slots = []
    for half in range(HALVES):
        extra = legs if half == 0 else 0
        messages = call(
            functools.partial(whiten_kernel, half, half == 0),
            [shape((rows + extra, LANES), bf16)] * mode_count,
            [
                vmem((cycles, chans, pixels), bf16),
                vmem((cycles, pixels), jnp.int32),
                vmem((cycles, chans, chans), f32),
                vmem((cycles, offsets, modes), f32),
                vmem((pixels, pixels), bf16),
                vmem((cycles * part_chans, pixels), bf16),
                vmem((mode_count, rows + extra, LANES), bf16),
                pltpu.SemaphoreType.DMA((5 + mode_count,)),
            ],
            56,
            [pltpu.SMEM] + [hbm] * 6,
            me,
            slots[0][0] if half else sky,
            sky,
            pixel_mask,
            noise_factor[:, 0],
            jnp.transpose(cycle_legendre, (0, 2, 1)),
            sort,
            out_space=hbm,
            cost=(2 * cycles * part_chans * pixels * (pixels + 2 * chans), 8 * MIB),
        )
        received = [messages[0]] + [None] * (mode_count - 1)
        for n in order:
            received[n] = lax.ppermute(messages[n], "mode", [(i, i ^ n) for i in range(mode_count)])
        slots.append(received)

    parts = []
    for half in range(HALVES):
        alm = call(
            functools.partial(modes_kernel, cycles, offsets, mode_count, rows),
            shape((offsets, mode_count, 2 * width, modes), bf16),
            [
                vmem((tiles, tiles * LANES, 2 * LANES), bf16),
                vmem((rows, tiles * LANES), bf16),
                vmem((cycles * offsets, mode_count * modes), f32),
                vmem((rows, 2 * LANES), f32),
                vmem((rows, 2 * LANES), f32),
                vmem((blocks, 2, cycles // group, group * width, LANES), f32),
                pltpu.SemaphoreType.DMA((tiles,)),
            ],
            40,
            [pltpu.SMEM, hbm, vmem, hbm] + [vmem] * (2 * mode_count),
            me,
            parts[0] if half else sky,
            twiddle,
            table,
            *slots[half],
            *slots[0],
            cost=(4 * rows * (tiles * LANES) ** 2 * 2, 8 * MIB),
        )
        parts.append(alm.reshape(patches * mode_count, 2 * width, modes))
    parts = [lax.all_to_all(alm, everyone, 0, 0, tiled=True) for alm in parts]
    parts = [alm.reshape(patches, mode_count, 2 * width, modes) for alm in parts]

    share = columns // (patches * mode_count)
    fold = LANES // chans
    packed = share % (8 * fold) == 0
    part = call(
        sketch_kernel,
        shape((patches * mode_count, share // fold, LANES) if packed else (columns, chans), f32),
        [vmem((2, chans, modes), f32)],
        24,
        [vmem] * (3 + HALVES),
        jnp.transpose(band_power),
        channel_cov,
        jnp.transpose(test_matrix[0], (1, 0, 2)),
        *parts,
    )
    if not packed:
        part = part.reshape(patches * mode_count, share, chans)
    part = lax.all_to_all(part, everyone, 0, 0, tiled=True)
    return jnp.transpose(call(total_kernel, shape((share, chans), f32), [], 16, [vmem], part))


def solution(mesh):
    return jax.shard_map(
        local,
        mesh=mesh,
        in_specs=(
            P("patch", "mode", None),
            P("patch", "mode"),
            P("patch", "mode", None, None),
            P("patch", "mode", None),
            P("mode", "patch"),
            P(),
            P("patch", "mode", None, None),
        ),
        out_specs=P(None, ("patch", "mode")),
        check_vma=False,
    )
```

```python
import functools
import math

import jax
import jax.numpy as jnp
import ml_dtypes
import numpy as np
from jax import lax
from jax.experimental import pallas as pl
from jax.experimental.pallas import tpu as pltpu
from jax.sharding import PartitionSpec as P

LANES = 128
MIB = 1 << 20
SUBLANES = 8
PAIR = 2


def rotate(value, step, points):
    re, im = value
    step %= points
    if step == 0:
        return re, im
    if 2 * step == points:
        return -re, -im
    if 4 * step == points:
        return im, -re
    if 8 * step == points:
        return (re + im) * math.sqrt(0.5), (im - re) * math.sqrt(0.5)
    if 8 * step == 3 * points:
        return (im - re) * math.sqrt(0.5), (re + im) * -math.sqrt(0.5)
    c, s = math.cos(2 * math.pi * step / points), math.sin(2 * math.pi * step / points)
    return re * c + im * s, im * c - re * s


def dft(values):
    n = len(values)
    if n == 1:
        return values
    half = n // 2
    even, odd = dft(values[0::2]), dft(values[1::2])
    out = [None] * n
    for b in range(half):
        re, im = rotate(odd[b], b, n)
        out[b] = even[b][0] + re, even[b][1] + im
        out[b + half] = even[b][0] - re, even[b][1] - im
    return out


def whiten_kernel(order, me_ref, sky_hbm, mask_hbm, factor_hbm, sort_hbm, *refs):
    sky, mask, factor, sort, white, stage, sems = refs[-7:]
    outs = refs[:-7]
    cycles, chans, pixels = sky.shape
    groups = len(outs)
    width = chans // groups
    group = max(1, SUBLANES // width)
    tall = group * width
    split = pixels // LANES
    sources, targets = (factor_hbm, sky_hbm, mask_hbm, sort_hbm), (factor, sky, mask, sort)
    copies = [pltpu.make_async_copy(a, b, sems.at[n]) for n, (a, b) in enumerate(zip(sources, targets))]
    for copy in copies:
        copy.start()
    copies[0].wait()
    row_of = lax.broadcasted_iota(jnp.int32, (tall, group * chans), 0) // width
    lane_of = lax.broadcasted_iota(jnp.int32, (tall, group * chans), 1) // chans
    lefts = []
    for pack in range(cycles // group):
        rows = []
        for e in range(groups):
            tile = [factor[pack * group + g, e * width : (e + 1) * width, :] for g in range(group)]
            tile = jnp.concatenate(tile, axis=0)
            rows.append(jnp.where(row_of == lane_of, jnp.concatenate([tile] * group, axis=1), 0.0))
        rows = jnp.concatenate(rows, axis=0)
        high = rows.astype(jnp.bfloat16)
        low = (rows - high.astype(jnp.float32)).astype(jnp.bfloat16)
        lefts.append((high, low))
    for copy in copies[1:3]:
        copy.wait()
    cycle_of = lax.broadcasted_iota(jnp.int32, (tall, pixels), 0) // width
    for pack in range(cycles // group):
        data = jnp.concatenate([sky[pack * group + g] for g in range(group)], axis=0)
        value = jnp.dot(lefts[pack][0], data, preferred_element_type=jnp.float32)
        value += jnp.dot(lefts[pack][1], data, preferred_element_type=jnp.float32)
        keep = jnp.broadcast_to(mask[pack * group : pack * group + 1, :], (tall, pixels))
        for g in range(1, group):
            keep = jnp.where(cycle_of < g, keep, mask[pack * group + g : pack * group + g + 1, :])
        keep = keep.astype(jnp.float32)
        for e in range(groups):
            place = (e * (cycles // group) + pack) * tall
            white[place : place + tall, :] = (value[e * tall : (e + 1) * tall] * keep).astype(jnp.bfloat16)
    copies[3].wait()
    count = cycles * width
    for pair in range(split // 2):
        wide = slice(pair * 2 * LANES, (pair + 1) * 2 * LANES)
        value = jnp.dot(white[...], sort[:, wide], preferred_element_type=jnp.float32).astype(jnp.bfloat16)
        for side in range(2):
            s = pair * 2 + side
            for e in range(groups):
                stage[e, s * count : (s + 1) * count, :] = value[
                    e * count : (e + 1) * count, side * LANES : (side + 1) * LANES
                ]
    me = me_ref[0]
    sends = [
        pltpu.make_async_copy(stage.at[jnp.bitwise_xor(me, n)], outs[slot], sems.at[4 + slot])
        for slot, n in enumerate(order)
    ]
    for send in sends:
        send.start()
    for send in sends:
        send.wait()


def modes_kernel(order, cycles, width, offsets, me_ref, twiddle_ref, table_hbm, leg_ref, *refs):
    slots = refs[: len(order)]
    out_ref, table, left, leg, prod_a, prod_b, x_ref, table_sems = refs[len(order) :]
    tiles = table.shape[0]
    split = twiddle_ref.shape[1]
    tall = x_ref.shape[3]
    group = tall // width
    modes = out_ref.shape[3]
    sources = leg_ref.shape[0]
    blocks = sources * modes // (tiles * LANES)
    per = modes // LANES
    count = slots[0].shape[0] // split
    me = me_ref[0]

    def copy(tile):
        return pltpu.make_async_copy(table_hbm.at[tile], table.at[tile], table_sems.at[tile])

    for tile in range(tiles):
        copy(tile).start()
    for slot, n in enumerate(order):
        q = jnp.bitwise_xor(me, n) % sources
        lanes = pl.ds(pl.multiple_of(q * LANES, LANES), LANES)
        for s in range(split):
            place = (s * PAIR + n // sources) * count
            left[place : place + count, lanes] = slots[slot][s * count : (s + 1) * count, :]
    for q in range(sources):
        leg[:, q * modes : (q + 1) * modes] = leg_ref[q].astype(jnp.float32)

    def product(tile, prod):
        prod[...] = jnp.dot(left[...], table[tile], preferred_element_type=jnp.float32)

    def use(tile, prod):
        lanes = pl.ds(pl.multiple_of(tile * LANES, LANES), LANES)
        cosine, sine = twiddle_ref[0, :, lanes], twiddle_ref[1, :, lanes]
        cycle_of = lax.broadcasted_iota(jnp.int32, (tall, LANES), 0) // width
        for pack in range(cycles // group):
            values = []
            for s in range(split):
                place = (s * cycles + pack * group) * width
                re = prod[place : place + tall, :LANES]
                im = prod[place : place + tall, LANES:]
                if s == 0:
                    values.append((re, -im))
                else:
                    c, d = cosine[s : s + 1, :], sine[s : s + 1, :]
                    values.append((re * c - im * d, -(re * d) - im * c))
            parts = dft(values)
            for b in range(blocks):
                x_ref[b, 0, pack] = parts[b][0]
                x_ref[b, 1, pack] = parts[b][1]
        for b in range(blocks):
            mode_tile = b * tiles + tile
            d, n = mode_tile // per, mode_tile % per
            mode = pl.ds(pl.multiple_of(mode_tile * LANES, LANES), LANES)
            for k in range(offsets):
                total = [None, None]
                for pack in range(cycles // group):
                    row = None
                    for g in range(group):
                        r = pack * group + g
                        next_row = leg[r * offsets + k : r * offsets + k + 1, mode]
                        if g == 0:
                            row = jnp.broadcast_to(next_row, (tall, LANES))
                        else:
                            row = jnp.where(cycle_of < g, row, next_row)
                    for t in range(2):
                        term = row * x_ref[b, t, pack]
                        total[t] = term if pack == 0 else total[t] + term
                step = tall // 2
                while step >= width:
                    total = [value + pltpu.roll(value, step, 0) for value in total]
                    step //= 2
                if group == 1:
                    both = jnp.concatenate(total, axis=0)
                else:
                    both = jnp.where(cycle_of < 1, total[0], total[1])[: 2 * width]
                place = pl.ds(pl.multiple_of(n * LANES, LANES), LANES)
                out_ref[k, d, :, place] = both.astype(jnp.bfloat16)

    copy(0).wait()
    product(0, prod_a)

    @pl.loop(0, tiles // 2)
    def _(step):
        copy(2 * step + 1).wait()

        @pl.when(2 * step + 2 < tiles)
        def _():
            copy(2 * step + 2).wait()

        product(2 * step + 1, prod_b)
        use(2 * step, prod_a)
        product(jnp.minimum(2 * step + 2, tiles - 1), prod_a)
        use(2 * step + 1, prod_b)


def sketch_kernel(alm_ref, band_ref, cov_ref, test_ref, out_ref, left_ref):
    patches, groups, rows, lanes = alm_ref.shape
    chans = cov_ref.shape[0]
    width = rows // 2
    for low in range(PAIR):
        for g in range(groups):
            part = alm_ref[low, g].astype(jnp.float32)
            for p in range(low + PAIR, patches, PAIR):
                part += alm_ref[p, g].astype(jnp.float32)
            part = part * band_ref[...]
            place = (low * groups + g) * width
            for t in range(2):
                left_ref[t, place : place + width, :] = part[t * width : (t + 1) * width]
    sketch = None
    for t in range(2):
        term = lax.dot_general(
            test_ref[t],
            left_ref[t].astype(jnp.bfloat16),
            (((0,), (1,)), ((), ())),
            preferred_element_type=jnp.float32,
        )
        sketch = term if t == 0 else sketch + term
    mixed = lax.dot_general(
        sketch,
        cov_ref[...],
        (((1,), (1,)), ((), ())),
        precision=lax.Precision.HIGHEST,
        preferred_element_type=jnp.float32,
    )
    if out_ref.ndim == 2:
        out_ref[...] = mixed
    else:
        owners, block, _ = out_ref.shape
        fold = out_ref.shape[2] // chans
        mixed = mixed.reshape(owners, fold, block, chans)
        out_ref[...] = jnp.concatenate([mixed[:, n] for n in range(fold)], axis=-1)


def total_kernel(part_ref, out_ref):
    block, chans = part_ref.shape[1], out_ref.shape[1]
    total = jnp.sum(part_ref[...], axis=0)
    for n in range(part_ref.shape[2] // chans):
        out_ref[n * block : (n + 1) * block, :] = total[:, n * chans : (n + 1) * chans]


def call(kernel, shape, scratch, mib, spaces, *operands, out_space=pltpu.VMEM, cost=(0, 0)):
    return pl.pallas_call(
        kernel,
        out_shape=shape,
        in_specs=[pl.BlockSpec(memory_space=space) for space in spaces],
        out_specs=jax.tree.map(lambda _: pl.BlockSpec(memory_space=out_space), shape),
        scratch_shapes=scratch,
        compiler_params=pltpu.CompilerParams(vmem_limit_bytes=mib * MIB),
        cost_estimate=pl.CostEstimate(flops=cost[0], bytes_accessed=cost[1], transcendentals=0),
    )(*operands)


def transform_tables(split, cycle):
    half = cycle // split
    step = np.arange(split)[:, None] * np.arange(half)[None, :] % cycle
    angle = step * (2.0 * math.pi / cycle)
    twiddle = np.stack([np.cos(angle), np.sin(angle)]).astype(np.float32)
    step = np.arange(half)[:, None] * np.arange(half)[None, :] % half
    angle = (step * (2.0 * math.pi / half)).reshape(half, half // LANES, LANES)
    table = np.transpose(np.concatenate([np.cos(angle), np.sin(angle)], axis=2), (1, 0, 2))
    return twiddle, table.astype(ml_dtypes.bfloat16)


def sorting(pixels, split):
    place = np.arange(pixels) % split * (pixels // split) + np.arange(pixels) // split
    return (place[:, None] == np.arange(pixels)[None, :]).astype(ml_dtypes.bfloat16)


def local(sky_map, pixel_mask, noise_factor, cycle_legendre, band_power, channel_cov, test_matrix):
    cycles, pixels, chans = sky_map.shape
    modes, _ = band_power.shape
    offsets = cycle_legendre.shape[2]
    columns = test_matrix.shape[3]
    mode_count, patches = lax.axis_size("mode"), lax.axis_size("patch")
    groups = PAIR * mode_count
    width = chans // groups
    group = max(1, SUBLANES // width)
    split = pixels // LANES
    rows = split * cycles * width
    tiles = mode_count
    blocks = modes * mode_count // (tiles * LANES)
    everyone = ("patch", "mode")
    hbm, vmem, bf16, f32, shape = pl.ANY, pltpu.VMEM, jnp.bfloat16, jnp.float32, jax.ShapeDtypeStruct

    place = lax.axis_index("patch") % PAIR * mode_count + lax.axis_index("mode")
    me = place.astype(jnp.int32).reshape(1)

    def partner(place, n):
        return (place // groups) * groups + (place % groups ^ n)

    def swap(value, n):
        pairs = [(i, partner(i, n)) for i in range(patches * mode_count)]
        return lax.ppermute(value, everyone, pairs)

    own_leg = jnp.transpose(cycle_legendre, (0, 2, 1)).reshape(cycles * offsets, modes)
    leg = jnp.concatenate([own_leg, swap(own_leg, mode_count)], axis=0).astype(bf16)
    leg = lax.all_gather(leg, "mode", axis=0, tiled=False)

    twiddle, table = transform_tables(split, pixels * mode_count)
    order = sorted(range(groups), key=lambda n: (-(n >> 1).bit_count(), n % 2 - (n < 2), -n))

    messages = call(
        functools.partial(whiten_kernel, order),
        [shape((rows, LANES), bf16)] * groups,
        [
            vmem((cycles, chans, pixels), bf16),
            vmem((cycles, pixels), jnp.int32),
            vmem((cycles, chans, chans), f32),
            vmem((pixels, pixels), bf16),
            vmem((cycles * chans, pixels), bf16),
            vmem((groups, rows, LANES), bf16),
            pltpu.SemaphoreType.DMA((4 + groups,)),
        ],
        56,
        [pltpu.SMEM] + [hbm] * 4,
        me,
        jnp.transpose(sky_map, (0, 2, 1)),
        pixel_mask,
        noise_factor[:, 0],
        jnp.asarray(sorting(pixels, split)),
        out_space=hbm,
        cost=(2 * cycles * chans * pixels * (pixels + 4 * chans), 8 * MIB),
    )
    slots = [messages[slot] if n == 0 else swap(messages[slot], n) for slot, n in enumerate(order)]

    alm = call(
        functools.partial(modes_kernel, order, PAIR * cycles, width, offsets),
        shape((offsets, mode_count, 2 * width, modes), bf16),
        [
            vmem((tiles, tiles * LANES, 2 * LANES), bf16),
            vmem((PAIR * rows, tiles * LANES), bf16),
            vmem((PAIR * cycles * offsets, mode_count * modes), f32),
            vmem((PAIR * rows, 2 * LANES), f32),
            vmem((PAIR * rows, 2 * LANES), f32),
            vmem((blocks, 2, PAIR * cycles // group, group * width, LANES), f32),
            pltpu.SemaphoreType.DMA((tiles,)),
        ],
        40,
        [pltpu.SMEM, vmem, hbm, vmem] + [vmem] * groups,
        me,
        jnp.asarray(twiddle),
        jnp.asarray(table),
        leg,
        *slots,
        cost=(4 * PAIR * rows * (tiles * LANES) ** 2, 8 * MIB),
    )
    alm = alm.reshape(patches * mode_count, 2 * width, modes)
    alm = lax.all_to_all(alm, everyone, 0, 0, tiled=True)
    alm = alm.reshape(patches, mode_count, 2 * width, modes)

    share = columns // (patches * mode_count)
    fold = LANES // chans
    packed = share % (8 * fold) == 0
    part = call(
        sketch_kernel,
        shape((patches * mode_count, share // fold, LANES) if packed else (columns, chans), f32),
        [vmem((2, chans, modes), f32)],
        24,
        [vmem] * 4,
        alm,
        jnp.transpose(band_power),
        channel_cov,
        jnp.transpose(test_matrix[0], (1, 0, 2)),
    )
    if not packed:
        part = part.reshape(patches * mode_count, share, chans)
    part = lax.all_to_all(part, everyone, 0, 0, tiled=True)
    return jnp.transpose(call(total_kernel, shape((share, chans), f32), [], 16, [vmem], part))


def solution(mesh):
    return jax.shard_map(
        local,
        mesh=mesh,
        in_specs=(
            P("patch", "mode", None),
            P("patch", "mode"),
            P("patch", "mode", None, None),
            P("patch", "mode", None),
            P("mode", "patch"),
            P(),
            P("patch", "mode", None, None),
        ),
        out_specs=P(None, ("patch", "mode")),
        check_vma=False,
    )
```

```python
import functools
import math

import jax
import jax.numpy as jnp
import ml_dtypes
import numpy as np
from jax import lax
from jax.experimental import pallas as pl
from jax.experimental.pallas import tpu as pltpu
from jax.sharding import PartitionSpec as P

LANES = 128
MIB = 1 << 20
SUBLANES = 8
PAIR = 2


def rotate(value, step, points):
    re, im = value
    step %= points
    if step == 0:
        return re, im
    if 2 * step == points:
        return -re, -im
    if 4 * step == points:
        return im, -re
    if 8 * step == points:
        return (re + im) * math.sqrt(0.5), (im - re) * math.sqrt(0.5)
    if 8 * step == 3 * points:
        return (im - re) * math.sqrt(0.5), (re + im) * -math.sqrt(0.5)
    c, s = math.cos(2 * math.pi * step / points), math.sin(2 * math.pi * step / points)
    return re * c + im * s, im * c - re * s


def dft(values):
    n = len(values)
    if n == 1:
        return values
    half = n // 2
    even, odd = dft(values[0::2]), dft(values[1::2])
    out = [None] * n
    for b in range(half):
        re, im = rotate(odd[b], b, n)
        out[b] = even[b][0] + re, even[b][1] + im
        out[b + half] = even[b][0] - re, even[b][1] - im
    return out


def whiten_kernel(order, me_ref, sky_hbm, mask_hbm, factor_hbm, leg_hbm, sort_hbm, *refs):
    sky, mask, factor, leg, sort, white, stage, sems = refs[-8:]
    outs = refs[:-8]
    cycles, chans, pixels = sky.shape
    groups = len(outs)
    width = chans // groups
    group = max(1, SUBLANES // width)
    tall = group * width
    split = pixels // LANES
    sources, targets = (factor_hbm, sky_hbm, mask_hbm, leg_hbm, sort_hbm), (factor, sky, mask, leg, sort)
    copies = [pltpu.make_async_copy(a, b, sems.at[n]) for n, (a, b) in enumerate(zip(sources, targets))]
    for copy in copies:
        copy.start()
    copies[0].wait()
    row_of = lax.broadcasted_iota(jnp.int32, (tall, group * chans), 0) // width
    lane_of = lax.broadcasted_iota(jnp.int32, (tall, group * chans), 1) // chans
    lefts = []
    for pack in range(cycles // group):
        rows = []
        for e in range(groups):
            tile = [factor[pack * group + g, e * width : (e + 1) * width, :] for g in range(group)]
            tile = jnp.concatenate(tile, axis=0)
            rows.append(jnp.where(row_of == lane_of, jnp.concatenate([tile] * group, axis=1), 0.0))
        rows = jnp.concatenate(rows, axis=0)
        high = rows.astype(jnp.bfloat16)
        low = (rows - high.astype(jnp.float32)).astype(jnp.bfloat16)
        lefts.append((high, low))
    for copy in copies[1:3]:
        copy.wait()
    cycle_of = lax.broadcasted_iota(jnp.int32, (tall, pixels), 0) // width
    for pack in range(cycles // group):
        data = jnp.concatenate([sky[pack * group + g] for g in range(group)], axis=0)
        value = jnp.dot(lefts[pack][0], data, preferred_element_type=jnp.float32)
        value += jnp.dot(lefts[pack][1], data, preferred_element_type=jnp.float32)
        keep = jnp.broadcast_to(mask[pack * group : pack * group + 1, :], (tall, pixels))
        for g in range(1, group):
            keep = jnp.where(cycle_of < g, keep, mask[pack * group + g : pack * group + g + 1, :])
        keep = keep.astype(jnp.float32)
        for e in range(groups):
            place = (e * (cycles // group) + pack) * tall
            white[place : place + tall, :] = (value[e * tall : (e + 1) * tall] * keep).astype(jnp.bfloat16)
    copies[3].wait()
    count = cycles * width
    rows = jnp.concatenate([leg[r] for r in range(cycles)], axis=0).astype(jnp.bfloat16)
    high = rows.shape[0]
    for n in range(rows.shape[1] // LANES):
        for e in range(groups):
            place = split * count + n * high
            stage[e, place : place + high, :] = rows[:, n * LANES : (n + 1) * LANES]
    copies[4].wait()
    for pair in range(split // 2):
        wide = slice(pair * 2 * LANES, (pair + 1) * 2 * LANES)
        value = jnp.dot(white[...], sort[:, wide], preferred_element_type=jnp.float32).astype(jnp.bfloat16)
        for side in range(2):
            s = pair * 2 + side
            for e in range(groups):
                stage[e, s * count : (s + 1) * count, :] = value[
                    e * count : (e + 1) * count, side * LANES : (side + 1) * LANES
                ]
    me = me_ref[0]
    sends = [
        pltpu.make_async_copy(stage.at[jnp.bitwise_xor(me, n)], outs[slot], sems.at[5 + slot])
        for slot, n in enumerate(order)
    ]
    for send in sends:
        send.start()
    for send in sends:
        send.wait()


def modes_kernel(order, cycles, width, offsets, me_ref, twiddle_ref, table_hbm, *refs):
    slots = refs[: len(order)]
    out_ref, table, left, leg, prod_a, prod_b, x_ref, table_sems = refs[len(order) :]
    tiles = table.shape[0]
    split = twiddle_ref.shape[1]
    tall = x_ref.shape[3]
    group = tall // width
    modes = out_ref.shape[3]
    sources = len(order) // PAIR
    blocks = sources * modes // (tiles * LANES)
    per = modes // LANES
    count = cycles // PAIR * width
    high = cycles // PAIR * offsets
    me = me_ref[0]

    def copy(tile):
        return pltpu.make_async_copy(table_hbm.at[tile], table.at[tile], table_sems.at[tile])

    for tile in range(tiles):
        copy(tile).start()
    for slot, n in enumerate(order):
        q = jnp.bitwise_xor(me, n) % sources
        lanes = pl.ds(pl.multiple_of(q * LANES, LANES), LANES)
        for s in range(split):
            place = (s * PAIR + n // sources) * count
            left[place : place + count, lanes] = slots[slot][s * count : (s + 1) * count, :]
        for j in range(per):
            lanes = pl.ds(pl.multiple_of((q * per + j) * LANES, LANES), LANES)
            place = split * count + j * high
            rows = slots[slot][place : place + high, :].astype(jnp.float32)
            leg[n // sources * high : (n // sources + 1) * high, lanes] = rows

    def product(tile, prod):
        prod[...] = jnp.dot(left[...], table[tile], preferred_element_type=jnp.float32)

    def use(tile, prod):
        lanes = pl.ds(pl.multiple_of(tile * LANES, LANES), LANES)
        cosine, sine = twiddle_ref[0, :, lanes], twiddle_ref[1, :, lanes]
        cycle_of = lax.broadcasted_iota(jnp.int32, (tall, LANES), 0) // width
        for pack in range(cycles // group):
            values = []
            for s in range(split):
                place = (s * cycles + pack * group) * width
                re = prod[place : place + tall, :LANES]
                im = prod[place : place + tall, LANES:]
                if s == 0:
                    values.append((re, -im))
                else:
                    c, d = cosine[s : s + 1, :], sine[s : s + 1, :]
                    values.append((re * c - im * d, -(re * d) - im * c))
            parts = dft(values)
            for b in range(blocks):
                x_ref[b, 0, pack] = parts[b][0]
                x_ref[b, 1, pack] = parts[b][1]
        for b in range(blocks):
            mode_tile = b * tiles + tile
            d, n = mode_tile // per, mode_tile % per
            mode = pl.ds(pl.multiple_of(mode_tile * LANES, LANES), LANES)
            for k in range(offsets):
                total = [None, None]
                for pack in range(cycles // group):
                    row = None
                    for g in range(group):
                        r = pack * group + g
                        next_row = leg[r * offsets + k : r * offsets + k + 1, mode]
                        if g == 0:
                            row = jnp.broadcast_to(next_row, (tall, LANES))
                        else:
                            row = jnp.where(cycle_of < g, row, next_row)
                    for t in range(2):
                        term = row * x_ref[b, t, pack]
                        total[t] = term if pack == 0 else total[t] + term
                step = tall // 2
                while step >= width:
                    total = [value + pltpu.roll(value, step, 0) for value in total]
                    step //= 2
                if group == 1:
                    both = jnp.concatenate(total, axis=0)
                else:
                    both = jnp.where(cycle_of < 1, total[0], total[1])[: 2 * width]
                place = pl.ds(pl.multiple_of(n * LANES, LANES), LANES)
                out_ref[k, d, :, place] = both.astype(jnp.bfloat16)

    copy(0).wait()
    product(0, prod_a)

    @pl.loop(0, tiles // 2)
    def _(step):
        copy(2 * step + 1).wait()

        @pl.when(2 * step + 2 < tiles)
        def _():
            copy(2 * step + 2).wait()

        product(2 * step + 1, prod_b)
        use(2 * step, prod_a)
        product(jnp.minimum(2 * step + 2, tiles - 1), prod_a)
        use(2 * step + 1, prod_b)


def sketch_kernel(alm_ref, band_ref, cov_ref, test_ref, out_ref, left_ref):
    patches, groups, rows, lanes = alm_ref.shape
    chans = cov_ref.shape[0]
    width = rows // 2
    for low in range(PAIR):
        for g in range(groups):
            part = alm_ref[low, g].astype(jnp.float32)
            for p in range(low + PAIR, patches, PAIR):
                part += alm_ref[p, g].astype(jnp.float32)
            part = part * band_ref[...]
            place = (low * groups + g) * width
            for t in range(2):
                left_ref[t, place : place + width, :] = part[t * width : (t + 1) * width]
    sketch = None
    for t in range(2):
        term = lax.dot_general(
            test_ref[t],
            left_ref[t].astype(jnp.bfloat16),
            (((0,), (1,)), ((), ())),
            preferred_element_type=jnp.float32,
        )
        sketch = term if t == 0 else sketch + term
    mixed = lax.dot_general(
        sketch,
        cov_ref[...],
        (((1,), (1,)), ((), ())),
        precision=lax.Precision.HIGHEST,
        preferred_element_type=jnp.float32,
    )
    if out_ref.ndim == 2:
        out_ref[...] = mixed
    else:
        owners, block, _ = out_ref.shape
        fold = out_ref.shape[2] // chans
        mixed = mixed.reshape(owners, fold, block, chans)
        out_ref[...] = jnp.concatenate([mixed[:, n] for n in range(fold)], axis=-1)


def total_kernel(part_ref, out_ref):
    block, chans = part_ref.shape[1], out_ref.shape[1]
    total = jnp.sum(part_ref[...], axis=0)
    for n in range(part_ref.shape[2] // chans):
        out_ref[n * block : (n + 1) * block, :] = total[:, n * chans : (n + 1) * chans]


def call(kernel, shape, scratch, mib, spaces, *operands, out_space=pltpu.VMEM, cost=(0, 0)):
    return pl.pallas_call(
        kernel,
        out_shape=shape,
        in_specs=[pl.BlockSpec(memory_space=space) for space in spaces],
        out_specs=jax.tree.map(lambda _: pl.BlockSpec(memory_space=out_space), shape),
        scratch_shapes=scratch,
        compiler_params=pltpu.CompilerParams(vmem_limit_bytes=mib * MIB),
        cost_estimate=pl.CostEstimate(flops=cost[0], bytes_accessed=cost[1], transcendentals=0),
    )(*operands)


def transform_tables(split, cycle):
    half = cycle // split
    step = np.arange(split)[:, None] * np.arange(half)[None, :] % cycle
    angle = step * (2.0 * math.pi / cycle)
    twiddle = np.stack([np.cos(angle), np.sin(angle)]).astype(np.float32)
    step = np.arange(half)[:, None] * np.arange(half)[None, :] % half
    angle = (step * (2.0 * math.pi / half)).reshape(half, half // LANES, LANES)
    table = np.transpose(np.concatenate([np.cos(angle), np.sin(angle)], axis=2), (1, 0, 2))
    return twiddle, table.astype(ml_dtypes.bfloat16)


def sorting(pixels, split):
    place = np.arange(pixels) % split * (pixels // split) + np.arange(pixels) // split
    return (place[:, None] == np.arange(pixels)[None, :]).astype(ml_dtypes.bfloat16)


def local(sky_map, pixel_mask, noise_factor, cycle_legendre, band_power, channel_cov, test_matrix):
    cycles, pixels, chans = sky_map.shape
    modes, _ = band_power.shape
    offsets = cycle_legendre.shape[2]
    columns = test_matrix.shape[3]
    mode_count, patches = lax.axis_size("mode"), lax.axis_size("patch")
    groups = PAIR * mode_count
    width = chans // groups
    group = max(1, SUBLANES // width)
    split = pixels // LANES
    rows = split * cycles * width
    legs = cycles * offsets * (modes // LANES)
    tiles = mode_count
    blocks = modes * mode_count // (tiles * LANES)
    everyone = ("patch", "mode")
    hbm, vmem, bf16, f32, shape = pl.ANY, pltpu.VMEM, jnp.bfloat16, jnp.float32, jax.ShapeDtypeStruct

    place = lax.axis_index("patch") % PAIR * mode_count + lax.axis_index("mode")
    me = place.astype(jnp.int32).reshape(1)

    def partner(place, n):
        return (place // groups) * groups + (place % groups ^ n)

    def swap(value, n):
        pairs = [(i, partner(i, n)) for i in range(patches * mode_count)]
        return lax.ppermute(value, everyone, pairs)

    twiddle, table = transform_tables(split, pixels * mode_count)
    order = sorted(range(groups), key=lambda n: (-(n >> 1).bit_count(), n % 2 - (n < 2), -n))

    messages = call(
        functools.partial(whiten_kernel, order),
        [shape((rows + legs, LANES), bf16)] * groups,
        [
            vmem((cycles, chans, pixels), bf16),
            vmem((cycles, pixels), jnp.int32),
            vmem((cycles, chans, chans), f32),
            vmem((cycles, offsets, modes), f32),
            vmem((pixels, pixels), bf16),
            vmem((cycles * chans, pixels), bf16),
            vmem((groups, rows + legs, LANES), bf16),
            pltpu.SemaphoreType.DMA((5 + groups,)),
        ],
        56,
        [pltpu.SMEM] + [hbm] * 5,
        me,
        jnp.transpose(sky_map, (0, 2, 1)),
        pixel_mask,
        noise_factor[:, 0],
        jnp.transpose(cycle_legendre, (0, 2, 1)),
        jnp.asarray(sorting(pixels, split)),
        out_space=hbm,
        cost=(2 * cycles * chans * pixels * (pixels + 4 * chans), 8 * MIB),
    )
    slots = [messages[slot] if n == 0 else swap(messages[slot], n) for slot, n in enumerate(order)]

    alm = call(
        functools.partial(modes_kernel, order, PAIR * cycles, width, offsets),
        shape((offsets, mode_count, 2 * width, modes), bf16),
        [
            vmem((tiles, tiles * LANES, 2 * LANES), bf16),
            vmem((PAIR * rows, tiles * LANES), bf16),
            vmem((PAIR * cycles * offsets, mode_count * modes), f32),
            vmem((PAIR * rows, 2 * LANES), f32),
            vmem((PAIR * rows, 2 * LANES), f32),
            vmem((blocks, 2, PAIR * cycles // group, group * width, LANES), f32),
            pltpu.SemaphoreType.DMA((tiles,)),
        ],
        40,
        [pltpu.SMEM, vmem, hbm] + [vmem] * groups,
        me,
        jnp.asarray(twiddle),
        jnp.asarray(table),
        *slots,
        cost=(4 * PAIR * rows * (tiles * LANES) ** 2, 8 * MIB),
    )
    alm = alm.reshape(patches * mode_count, 2 * width, modes)
    alm = lax.all_to_all(alm, everyone, 0, 0, tiled=True)
    alm = alm.reshape(patches, mode_count, 2 * width, modes)

    share = columns // (patches * mode_count)
    fold = LANES // chans
    packed = share % (8 * fold) == 0
    part = call(
        sketch_kernel,
        shape((patches * mode_count, share // fold, LANES) if packed else (columns, chans), f32),
        [vmem((2, chans, modes), f32)],
        24,
        [vmem] * 4,
        alm,
        jnp.transpose(band_power),
        channel_cov,
        jnp.transpose(test_matrix[0], (1, 0, 2)),
    )
    if not packed:
        part = part.reshape(patches * mode_count, share, chans)
    part = lax.all_to_all(part, everyone, 0, 0, tiled=True)
    return jnp.transpose(call(total_kernel, shape((share, chans), f32), [], 16, [vmem], part))


def solution(mesh):
    return jax.shard_map(
        local,
        mesh=mesh,
        in_specs=(
            P("patch", "mode", None),
            P("patch", "mode"),
            P("patch", "mode", None, None),
            P("patch", "mode", None),
            P("mode", "patch"),
            P(),
            P("patch", "mode", None, None),
        ),
        out_specs=P(None, ("patch", "mode")),
        check_vma=False,
    )
```

```python
import functools
import math

import jax
import jax.numpy as jnp
import ml_dtypes
import numpy as np
from jax import lax
from jax.experimental import pallas as pl
from jax.experimental.pallas import tpu as pltpu
from jax.sharding import PartitionSpec as P

LANES = 128
MIB = 1 << 20
SUBLANES = 8
PAIR = 1


def rotate(value, step, points):
    re, im = value
    step %= points
    if step == 0:
        return re, im
    if 2 * step == points:
        return -re, -im
    if 4 * step == points:
        return im, -re
    if 8 * step == points:
        return (re + im) * math.sqrt(0.5), (im - re) * math.sqrt(0.5)
    if 8 * step == 3 * points:
        return (im - re) * math.sqrt(0.5), (re + im) * -math.sqrt(0.5)
    c, s = math.cos(2 * math.pi * step / points), math.sin(2 * math.pi * step / points)
    return re * c + im * s, im * c - re * s


def dft(values):
    n = len(values)
    if n == 1:
        return values
    half = n // 2
    even, odd = dft(values[0::2]), dft(values[1::2])
    out = [None] * n
    for b in range(half):
        re, im = rotate(odd[b], b, n)
        out[b] = even[b][0] + re, even[b][1] + im
        out[b + half] = even[b][0] - re, even[b][1] - im
    return out


def whiten_kernel(order, me_ref, sky_hbm, mask_hbm, factor_hbm, leg_hbm, sort_hbm, *refs):
    sky, mask, factor, leg, sort, white, stage, sems = refs[-8:]
    outs = refs[:-8]
    cycles, chans, pixels = sky.shape
    groups = len(outs)
    width = chans // groups
    group = max(1, SUBLANES // width)
    tall = group * width
    split = pixels // LANES
    sources, targets = (factor_hbm, sky_hbm, mask_hbm, leg_hbm, sort_hbm), (factor, sky, mask, leg, sort)
    copies = [pltpu.make_async_copy(a, b, sems.at[n]) for n, (a, b) in enumerate(zip(sources, targets))]
    for copy in copies[:3]:
        copy.start()
    copies[0].wait()
    copies[3].start()
    copies[4].start()
    row_of = lax.broadcasted_iota(jnp.int32, (tall, group * chans), 0) // width
    lane_of = lax.broadcasted_iota(jnp.int32, (tall, group * chans), 1) // chans
    lefts = []
    for pack in range(cycles // group):
        rows = []
        for e in range(groups):
            tile = [factor[pack * group + g, e * width : (e + 1) * width, :] for g in range(group)]
            tile = jnp.concatenate(tile, axis=0)
            rows.append(jnp.where(row_of == lane_of, jnp.concatenate([tile] * group, axis=1), 0.0))
        rows = jnp.concatenate(rows, axis=0)
        high = rows.astype(jnp.bfloat16)
        low = (rows - high.astype(jnp.float32)).astype(jnp.bfloat16)
        lefts.append(jnp.concatenate([high, low], axis=1))
    for copy in copies[1:3]:
        copy.wait()
    cycle_of = lax.broadcasted_iota(jnp.int32, (tall, pixels), 0) // width
    for pack in range(cycles // group):
        data = jnp.concatenate([sky[pack * group + g] for g in range(group)] * 2, axis=0)
        value = jnp.dot(lefts[pack], data, preferred_element_type=jnp.float32)
        keep = jnp.broadcast_to(mask[pack * group : pack * group + 1, :], (tall, pixels))
        for g in range(1, group):
            keep = jnp.where(cycle_of < g, keep, mask[pack * group + g : pack * group + g + 1, :])
        keep = keep.astype(jnp.float32)
        for e in range(groups):
            place = (e * (cycles // group) + pack) * tall
            white[place : place + tall, :] = (value[e * tall : (e + 1) * tall] * keep).astype(jnp.bfloat16)
    copies[3].wait()
    count = cycles * width
    rows = jnp.concatenate([leg[r] for r in range(cycles)], axis=0).astype(jnp.bfloat16)
    high = rows.shape[0]
    for n in range(rows.shape[1] // LANES):
        for e in range(groups):
            place = split * count + n * high
            stage[e, place : place + high, :] = rows[:, n * LANES : (n + 1) * LANES]
    copies[4].wait()
    for pair in range(split // 2):
        wide = slice(pair * 2 * LANES, (pair + 1) * 2 * LANES)
        value = jnp.dot(white[...], sort[:, wide], preferred_element_type=jnp.float32).astype(jnp.bfloat16)
        for side in range(2):
            s = pair * 2 + side
            for e in range(groups):
                stage[e, s * count : (s + 1) * count, :] = value[
                    e * count : (e + 1) * count, side * LANES : (side + 1) * LANES
                ]
    me = me_ref[0]
    sends = [
        pltpu.make_async_copy(stage.at[jnp.bitwise_xor(me, n)], outs[slot], sems.at[5 + slot])
        for slot, n in enumerate(order)
    ]
    for send in sends:
        send.start()
    for send in sends:
        send.wait()


def modes_kernel(order, cycles, width, offsets, me_ref, twiddle_ref, table_hbm, *refs):
    slots = refs[: len(order)]
    out_hbm, table, left, leg, prod_a, prod_b, x_ref, out_ref, table_sems, out_sems = refs[len(order) :]
    tiles = table.shape[0]
    split = twiddle_ref.shape[1]
    tall = x_ref.shape[3]
    group = tall // width
    modes = out_ref.shape[3]
    sources = len(order) // PAIR
    blocks = sources * modes // (tiles * LANES)
    per = modes // LANES
    count = cycles // PAIR * width
    high = cycles // PAIR * offsets
    me = me_ref[0]

    def copy(tile):
        return pltpu.make_async_copy(table_hbm.at[tile], table.at[tile], table_sems.at[tile])

    def store(step, n):
        mode_tile = n // 2 * tiles + 2 * step + n % 2
        lanes = pl.ds(pl.multiple_of(mode_tile % per * LANES, LANES), LANES)
        where = (slice(None), mode_tile // per, slice(None), lanes)
        return pltpu.make_async_copy(out_ref.at[where], out_hbm.at[where], out_sems.at[step, n])

    copy(0).start()
    copy(1).start()
    for slot, n in enumerate(order):
        q = jnp.bitwise_xor(me, n) % sources
        lanes = pl.ds(pl.multiple_of(q * LANES, LANES), LANES)
        for s in range(split):
            place = (s * PAIR + n // sources) * count
            left[place : place + count, lanes] = slots[slot][s * count : (s + 1) * count, :]
    for tile in range(2, tiles):
        copy(tile).start()

    def product(tile, prod):
        prod[...] = jnp.dot(left[...], table[tile], preferred_element_type=jnp.float32)

    copy(0).wait()
    product(0, prod_a)
    for slot, n in enumerate(order):
        q = jnp.bitwise_xor(me, n) % sources
        for j in range(per):
            lanes = pl.ds(pl.multiple_of((q * per + j) * LANES, LANES), LANES)
            place = split * count + j * high
            rows = slots[slot][place : place + high, :].astype(jnp.float32)
            leg[n // sources * high : (n // sources + 1) * high, lanes] = rows

    def use(tile, prod):
        lanes = pl.ds(pl.multiple_of(tile * LANES, LANES), LANES)
        cosine, sine = twiddle_ref[0, :, lanes], twiddle_ref[1, :, lanes]
        cycle_of = lax.broadcasted_iota(jnp.int32, (tall, LANES), 0) // width
        for pack in range(cycles // group):
            values = []
            for s in range(split):
                place = (s * cycles + pack * group) * width
                re = prod[place : place + tall, :LANES]
                im = prod[place : place + tall, LANES:]
                if s == 0:
                    values.append((re, -im))
                else:
                    c, d = cosine[s : s + 1, :], sine[s : s + 1, :]
                    values.append((re * c - im * d, -(re * d) - im * c))
            parts = dft(values)
            for b in range(blocks):
                x_ref[b, 0, pack] = parts[b][0]
                x_ref[b, 1, pack] = parts[b][1]
        for b in range(blocks):
            mode_tile = b * tiles + tile
            d, n = mode_tile // per, mode_tile % per
            mode = pl.ds(pl.multiple_of(mode_tile * LANES, LANES), LANES)
            for k in range(offsets):
                total = [None, None]
                for pack in range(cycles // group):
                    row = None
                    for g in range(group):
                        r = pack * group + g
                        next_row = leg[r * offsets + k : r * offsets + k + 1, mode]
                        if g == 0:
                            row = jnp.broadcast_to(next_row, (tall, LANES))
                        else:
                            row = jnp.where(cycle_of < g, row, next_row)
                    for t in range(2):
                        term = row * x_ref[b, t, pack]
                        total[t] = term if pack == 0 else total[t] + term
                step = tall // 2
                while step >= width:
                    total = [value + pltpu.roll(value, step, 0) for value in total]
                    step //= 2
                if group == 1:
                    both = jnp.concatenate(total, axis=0)
                else:
                    both = jnp.where(cycle_of < 1, total[0], total[1])[: 2 * width]
                place = pl.ds(pl.multiple_of(n * LANES, LANES), LANES)
                out_ref[k, d, :, place] = both.astype(jnp.bfloat16)

    @pl.loop(0, tiles // 2)
    def _(step):
        copy(2 * step + 1).wait()

        @pl.when(2 * step + 2 < tiles)
        def _():
            copy(2 * step + 2).wait()

        product(2 * step + 1, prod_b)
        use(2 * step, prod_a)
        product(jnp.minimum(2 * step + 2, tiles - 1), prod_a)
        use(2 * step + 1, prod_b)
        for n in range(2 * blocks):
            store(step, n).start()

    @pl.loop(0, tiles // 2)
    def _(step):
        for n in range(2 * blocks):
            store(step, n).wait()


def sketch_kernel(alm_ref, band_ref, cov_ref, test_ref, out_ref, left_ref):
    patches, groups, rows, lanes = alm_ref.shape
    chans = cov_ref.shape[0]
    width = rows // 2
    for low in range(PAIR):
        for g in range(groups):
            part = alm_ref[low, g].astype(jnp.float32)
            for p in range(low + PAIR, patches, PAIR):
                part += alm_ref[p, g].astype(jnp.float32)
            part = part * band_ref[...]
            place = (low * groups + g) * width
            for t in range(2):
                left_ref[t, place : place + width, :] = part[t * width : (t + 1) * width]
    sketch = None
    for t in range(2):
        term = lax.dot_general(
            test_ref[t],
            left_ref[t].astype(jnp.bfloat16),
            (((0,), (1,)), ((), ())),
            preferred_element_type=jnp.float32,
        )
        sketch = term if t == 0 else sketch + term
    mixed = lax.dot_general(
        sketch,
        cov_ref[...],
        (((1,), (1,)), ((), ())),
        precision=lax.Precision.HIGHEST,
        preferred_element_type=jnp.float32,
    )
    if out_ref.ndim == 2:
        out_ref[...] = mixed
    else:
        owners, block, _ = out_ref.shape
        fold = out_ref.shape[2] // chans
        mixed = mixed.reshape(owners, fold, block, chans)
        out_ref[...] = jnp.concatenate([mixed[:, n] for n in range(fold)], axis=-1)


def total_kernel(part_ref, out_ref):
    block, chans = part_ref.shape[1], out_ref.shape[1]
    total = jnp.sum(part_ref[...], axis=0)
    for n in range(part_ref.shape[2] // chans):
        out_ref[n * block : (n + 1) * block, :] = total[:, n * chans : (n + 1) * chans]


def call(kernel, shape, scratch, mib, spaces, *operands, out_space=pltpu.VMEM, cost=(0, 0)):
    return pl.pallas_call(
        kernel,
        out_shape=shape,
        in_specs=[pl.BlockSpec(memory_space=space) for space in spaces],
        out_specs=jax.tree.map(lambda _: pl.BlockSpec(memory_space=out_space), shape),
        scratch_shapes=scratch,
        compiler_params=pltpu.CompilerParams(vmem_limit_bytes=mib * MIB),
        cost_estimate=pl.CostEstimate(flops=cost[0], bytes_accessed=cost[1], transcendentals=0),
    )(*operands)


def transform_tables(split, cycle):
    half = cycle // split
    step = np.arange(split)[:, None] * np.arange(half)[None, :] % cycle
    angle = step * (2.0 * math.pi / cycle)
    twiddle = np.stack([np.cos(angle), np.sin(angle)]).astype(np.float32)
    step = np.arange(half)[:, None] * np.arange(half)[None, :] % half
    angle = (step * (2.0 * math.pi / half)).reshape(half, half // LANES, LANES)
    table = np.transpose(np.concatenate([np.cos(angle), np.sin(angle)], axis=2), (1, 0, 2))
    return twiddle, table.astype(ml_dtypes.bfloat16)


def sorting(pixels, split):
    place = np.arange(pixels) % split * (pixels // split) + np.arange(pixels) // split
    return (place[:, None] == np.arange(pixels)[None, :]).astype(ml_dtypes.bfloat16)


def local(sky_map, pixel_mask, noise_factor, cycle_legendre, band_power, channel_cov, test_matrix):
    cycles, pixels, chans = sky_map.shape
    modes, _ = band_power.shape
    offsets = cycle_legendre.shape[2]
    columns = test_matrix.shape[3]
    mode_count, patches = lax.axis_size("mode"), lax.axis_size("patch")
    groups = PAIR * mode_count
    width = chans // groups
    group = max(1, SUBLANES // width)
    split = pixels // LANES
    rows = split * cycles * width
    legs = cycles * offsets * (modes // LANES)
    tiles = mode_count
    blocks = modes * mode_count // (tiles * LANES)
    everyone = ("patch", "mode")
    hbm, vmem, bf16, f32, shape = pl.ANY, pltpu.VMEM, jnp.bfloat16, jnp.float32, jax.ShapeDtypeStruct

    place = lax.axis_index("patch") % PAIR * mode_count + lax.axis_index("mode")
    me = place.astype(jnp.int32).reshape(1)

    def partner(place, n):
        return (place // groups) * groups + (place % groups ^ n)

    def swap(value, n):
        pairs = [(i, partner(i, n)) for i in range(patches * mode_count)]
        return lax.ppermute(value, everyone, pairs)

    twiddle, table = transform_tables(split, pixels * mode_count)
    order = sorted(range(groups), key=lambda n: (-(n >> 1).bit_count(), n % 2 - (n < 2), -n))

    messages = call(
        functools.partial(whiten_kernel, order),
        [shape((rows + legs, LANES), bf16)] * groups,
        [
            vmem((cycles, chans, pixels), bf16),
            vmem((cycles, pixels), jnp.int32),
            vmem((cycles, chans, chans), f32),
            vmem((cycles, offsets, modes), f32),
            vmem((pixels, pixels), bf16),
            vmem((cycles * chans, pixels), bf16),
            vmem((groups, rows + legs, LANES), bf16),
            pltpu.SemaphoreType.DMA((5 + groups,)),
        ],
        56,
        [pltpu.SMEM] + [hbm] * 5,
        me,
        jnp.transpose(sky_map, (0, 2, 1)),
        pixel_mask,
        noise_factor[:, 0],
        jnp.transpose(cycle_legendre, (0, 2, 1)),
        jnp.asarray(sorting(pixels, split)),
        out_space=hbm,
        cost=(2 * cycles * chans * pixels * (pixels + 4 * chans), 8 * MIB),
    )
    slots = [messages[slot] if n == 0 else swap(messages[slot], n) for slot, n in enumerate(order)]

    alm = call(
        functools.partial(modes_kernel, order, PAIR * cycles, width, offsets),
        shape((offsets, mode_count, 2 * width, modes), bf16),
        [
            vmem((tiles, tiles * LANES, 2 * LANES), bf16),
            vmem((PAIR * rows, tiles * LANES), bf16),
            vmem((PAIR * cycles * offsets, mode_count * modes), f32),
            vmem((PAIR * rows, 2 * LANES), f32),
            vmem((PAIR * rows, 2 * LANES), f32),
            vmem((blocks, 2, PAIR * cycles // group, group * width, LANES), f32),
            vmem((offsets, mode_count, 2 * width, modes), bf16),
            pltpu.SemaphoreType.DMA((tiles,)),
            pltpu.SemaphoreType.DMA((tiles // 2, 2 * blocks)),
        ],
        40,
        [pltpu.SMEM, vmem, hbm] + [vmem] * groups,
        me,
        jnp.asarray(twiddle),
        jnp.asarray(table),
        *slots,
        out_space=hbm,
        cost=(4 * PAIR * rows * (tiles * LANES) ** 2, 8 * MIB),
    )
    alm = alm.reshape(patches * mode_count, 2 * width, modes)
    alm = lax.all_to_all(alm, everyone, 0, 0, tiled=True)
    alm = alm.reshape(patches, mode_count, 2 * width, modes)

    share = columns // (patches * mode_count)
    fold = LANES // chans
    packed = share % (8 * fold) == 0
    part = call(
        sketch_kernel,
        shape((patches * mode_count, share // fold, LANES) if packed else (columns, chans), f32),
        [vmem((2, chans, modes), f32)],
        24,
        [vmem] * 4,
        alm,
        jnp.transpose(band_power),
        channel_cov,
        jnp.transpose(test_matrix[0], (1, 0, 2)),
    )
    if not packed:
        part = part.reshape(patches * mode_count, share, chans)
    part = lax.all_to_all(part, everyone, 0, 0, tiled=True)
    return jnp.transpose(call(total_kernel, shape((share, chans), f32), [], 16, [vmem], part))


def solution(mesh):
    return jax.shard_map(
        local,
        mesh=mesh,
        in_specs=(
            P("patch", "mode", None),
            P("patch", "mode"),
            P("patch", "mode", None, None),
            P("patch", "mode", None),
            P("mode", "patch"),
            P(),
            P("patch", "mode", None, None),
        ),
        out_specs=P(None, ("patch", "mode")),
        check_vma=False,
    )
```

```python
import functools
import math

import jax
import jax.numpy as jnp
import ml_dtypes
import numpy as np
from jax import lax
from jax.experimental import pallas as pl
from jax.experimental.pallas import tpu as pltpu
from jax.sharding import PartitionSpec as P

LANES = 128
MIB = 1 << 20
SUBLANES = 8


def rotate(value, step, points):
    re, im = value
    step %= points
    if step == 0:
        return re, im
    if 2 * step == points:
        return -re, -im
    if 4 * step == points:
        return im, -re
    if 8 * step == points:
        return (re + im) * math.sqrt(0.5), (im - re) * math.sqrt(0.5)
    if 8 * step == 3 * points:
        return (im - re) * math.sqrt(0.5), (re + im) * -math.sqrt(0.5)
    c, s = math.cos(2 * math.pi * step / points), math.sin(2 * math.pi * step / points)
    return re * c + im * s, im * c - re * s


def dft(values):
    n = len(values)
    if n == 1:
        return values
    half = n // 2
    even, odd = dft(values[0::2]), dft(values[1::2])
    out = [None] * n
    for b in range(half):
        re, im = rotate(odd[b], b, n)
        out[b] = even[b][0] + re, even[b][1] + im
        out[b + half] = even[b][0] - re, even[b][1] - im
    return out


def whiten_kernel(sky_hbm, mask_hbm, factor_hbm, leg_hbm, sort_hbm, out_hbm, *refs):
    sky, mask, factor, leg, sort, white, stage, sems = refs
    cycles, chans, pixels = sky.shape
    groups = stage.shape[0]
    width = chans // groups
    group = max(1, SUBLANES // width)
    tall = group * width
    split = pixels // LANES
    sources, targets = (factor_hbm, sky_hbm, mask_hbm, leg_hbm, sort_hbm), (factor, sky, mask, leg, sort)
    copies = [pltpu.make_async_copy(a, b, sems.at[n]) for n, (a, b) in enumerate(zip(sources, targets))]
    for copy in copies:
        copy.start()
    copies[0].wait()
    row_of = lax.broadcasted_iota(jnp.int32, (tall, group * chans), 0) // width
    lane_of = lax.broadcasted_iota(jnp.int32, (tall, group * chans), 1) // chans
    lefts = []
    for pack in range(cycles // group):
        rows = []
        for e in range(groups):
            tile = [factor[pack * group + g, e * width : (e + 1) * width, :] for g in range(group)]
            tile = jnp.concatenate(tile, axis=0)
            rows.append(jnp.where(row_of == lane_of, jnp.concatenate([tile] * group, axis=1), 0.0))
        rows = jnp.concatenate(rows, axis=0)
        high = rows.astype(jnp.bfloat16)
        low = (rows - high.astype(jnp.float32)).astype(jnp.bfloat16)
        lefts.append(jnp.concatenate([high, low], axis=1))
    for copy in copies[1:3]:
        copy.wait()
    cycle_of = lax.broadcasted_iota(jnp.int32, (tall, pixels), 0) // width
    for pack in range(cycles // group):
        data = jnp.concatenate([sky[pack * group + g] for g in range(group)] * 2, axis=0)
        value = jnp.dot(lefts[pack], data, preferred_element_type=jnp.float32)
        keep = jnp.broadcast_to(mask[pack * group : pack * group + 1, :], (tall, pixels))
        for g in range(1, group):
            keep = jnp.where(cycle_of < g, keep, mask[pack * group + g : pack * group + g + 1, :])
        keep = keep.astype(jnp.float32)
        for e in range(groups):
            place = (e * (cycles // group) + pack) * tall
            white[place : place + tall, :] = (value[e * tall : (e + 1) * tall] * keep).astype(jnp.bfloat16)
    copies[3].wait()
    count = cycles * width
    rows = jnp.concatenate([leg[r] for r in range(cycles)], axis=0).astype(jnp.bfloat16)
    high = rows.shape[0]
    for n in range(rows.shape[1] // LANES):
        for e in range(groups):
            place = split * count + n * high
            stage[e, place : place + high, :] = rows[:, n * LANES : (n + 1) * LANES]
    sends = []

    def send(first, last):
        where = (slice(None), slice(first, last))
        sends.append(pltpu.make_async_copy(stage.at[where], out_hbm.at[where], sems.at[5 + len(sends)]))
        sends[-1].start()

    send(split * count, stage.shape[1])
    copies[4].wait()
    for pair in range(split // 2):
        wide = slice(pair * 2 * LANES, (pair + 1) * 2 * LANES)
        value = jnp.dot(white[...], sort[:, wide], preferred_element_type=jnp.float32).astype(jnp.bfloat16)
        for side in range(2):
            s = pair * 2 + side
            for e in range(groups):
                stage[e, s * count : (s + 1) * count, :] = value[
                    e * count : (e + 1) * count, side * LANES : (side + 1) * LANES
                ]
        send(pair * 2 * count, (pair + 1) * 2 * count)
    for send in sends:
        send.wait()


def modes_kernel(width, offsets, twiddle_ref, table_hbm, z_ref, out_hbm, *refs):
    table, left, leg, prod_a, prod_b, x_ref, out_ref, table_sems, out_sems = refs
    tiles = table.shape[0]
    split = twiddle_ref.shape[1]
    tall = x_ref.shape[3]
    group = tall // width
    modes = out_ref.shape[3]
    sources = out_ref.shape[1]
    parts = z_ref.shape[0] // sources
    cycles = leg.shape[0] // offsets
    blocks = sources * modes // (tiles * LANES)
    per = modes // LANES
    count = cycles // parts * width
    high = cycles // parts * offsets

    def copy(tile):
        return pltpu.make_async_copy(table_hbm.at[tile], table.at[tile], table_sems.at[tile])

    def store(step, n):
        mode_tile = n // 2 * tiles + 2 * step + n % 2
        lanes = pl.ds(pl.multiple_of(mode_tile % per * LANES, LANES), LANES)
        where = (slice(None), mode_tile // per, slice(None), lanes)
        return pltpu.make_async_copy(out_ref.at[where], out_hbm.at[where], out_sems.at[step, n])

    copy(0).start()
    copy(1).start()
    for p in range(parts):
        for q in range(sources):
            for n in range(split):
                place = (n * parts + p) * count
                rows = z_ref[p * sources + q, n * count : (n + 1) * count, :]
                left[place : place + count, q * LANES : (q + 1) * LANES] = rows
    for tile in range(2, tiles):
        copy(tile).start()

    def product(tile, prod):
        prod[...] = jnp.dot(left[...], table[tile], preferred_element_type=jnp.float32)

    copy(0).wait()
    product(0, prod_a)
    for p in range(parts):
        for q in range(sources):
            for n in range(per):
                place = split * count + n * high
                rows = z_ref[p * sources + q, place : place + high, :].astype(jnp.float32)
                leg[p * high : (p + 1) * high, (q * per + n) * LANES : (q * per + n + 1) * LANES] = rows

    def use(tile, prod):
        lanes = pl.ds(pl.multiple_of(tile * LANES, LANES), LANES)
        cosine, sine = twiddle_ref[0, :, lanes], twiddle_ref[1, :, lanes]
        cycle_of = lax.broadcasted_iota(jnp.int32, (tall, LANES), 0) // width
        for pack in range(cycles // group):
            values = []
            for s in range(split):
                place = (s * cycles + pack * group) * width
                re = prod[place : place + tall, :LANES]
                im = prod[place : place + tall, LANES:]
                if s == 0:
                    values.append((re, -im))
                else:
                    c, d = cosine[s : s + 1, :], sine[s : s + 1, :]
                    values.append((re * c - im * d, -(re * d) - im * c))
            parts = dft(values)
            for b in range(blocks):
                x_ref[b, 0, pack] = parts[b][0]
                x_ref[b, 1, pack] = parts[b][1]
        for b in range(blocks):
            mode_tile = b * tiles + tile
            d, n = mode_tile // per, mode_tile % per
            mode = pl.ds(pl.multiple_of(mode_tile * LANES, LANES), LANES)
            for k in range(offsets):
                total = [None, None]
                for pack in range(cycles // group):
                    row = None
                    for g in range(group):
                        r = pack * group + g
                        next_row = leg[r * offsets + k : r * offsets + k + 1, mode]
                        if g == 0:
                            row = jnp.broadcast_to(next_row, (tall, LANES))
                        else:
                            row = jnp.where(cycle_of < g, row, next_row)
                    for t in range(2):
                        term = row * x_ref[b, t, pack]
                        total[t] = term if pack == 0 else total[t] + term
                step = tall // 2
                while step >= width:
                    total = [value + pltpu.roll(value, step, 0) for value in total]
                    step //= 2
                if group == 1:
                    both = jnp.concatenate(total, axis=0)
                else:
                    both = jnp.where(cycle_of < 1, total[0], total[1])[: 2 * width]
                place = pl.ds(pl.multiple_of(n * LANES, LANES), LANES)
                out_ref[k, d, :, place] = both.astype(jnp.bfloat16)

    @pl.loop(0, tiles // 2)
    def _(step):
        copy(2 * step + 1).wait()

        @pl.when(2 * step + 2 < tiles)
        def _():
            copy(2 * step + 2).wait()

        product(2 * step + 1, prod_b)
        use(2 * step, prod_a)
        product(jnp.minimum(2 * step + 2, tiles - 1), prod_a)
        use(2 * step + 1, prod_b)
        for n in range(2 * blocks):
            store(step, n).start()

    @pl.loop(0, tiles // 2)
    def _(step):
        for n in range(2 * blocks):
            store(step, n).wait()


def sketch_kernel(alm_ref, band_ref, cov_ref, test_ref, out_ref, left_ref):
    patches, groups, rows, lanes = alm_ref.shape
    chans = cov_ref.shape[0]
    width = rows // 2
    for g in range(groups):
        part = alm_ref[0, g].astype(jnp.float32)
        for p in range(1, patches):
            part += alm_ref[p, g].astype(jnp.float32)
        part = part * band_ref[...]
        for t in range(2):
            left_ref[t, g * width : (g + 1) * width, :] = part[t * width : (t + 1) * width]
    sketch = None
    for t in range(2):
        term = lax.dot_general(
            test_ref[t],
            left_ref[t].astype(jnp.bfloat16),
            (((0,), (1,)), ((), ())),
            preferred_element_type=jnp.float32,
        )
        sketch = term if t == 0 else sketch + term
    mixed = lax.dot_general(
        sketch,
        cov_ref[...],
        (((1,), (1,)), ((), ())),
        precision=lax.Precision.HIGHEST,
        preferred_element_type=jnp.float32,
    )
    if out_ref.ndim == 2:
        out_ref[...] = mixed
    else:
        owners, block, _ = out_ref.shape
        fold = out_ref.shape[2] // chans
        mixed = mixed.reshape(owners, fold, block, chans)
        out_ref[...] = jnp.concatenate([mixed[:, n] for n in range(fold)], axis=-1)


def total_kernel(part_ref, out_ref):
    block, chans = part_ref.shape[1], out_ref.shape[1]
    total = jnp.sum(part_ref[...], axis=0)
    for n in range(part_ref.shape[2] // chans):
        out_ref[n * block : (n + 1) * block, :] = total[:, n * chans : (n + 1) * chans]


def call(kernel, shape, scratch, mib, spaces, *operands, out_space=pltpu.VMEM, cost=(0, 0)):
    return pl.pallas_call(
        kernel,
        out_shape=shape,
        in_specs=[pl.BlockSpec(memory_space=space) for space in spaces],
        out_specs=jax.tree.map(lambda _: pl.BlockSpec(memory_space=out_space), shape),
        scratch_shapes=scratch,
        compiler_params=pltpu.CompilerParams(vmem_limit_bytes=mib * MIB),
        cost_estimate=pl.CostEstimate(flops=cost[0], bytes_accessed=cost[1], transcendentals=0),
    )(*operands)


def transform_tables(split, cycle):
    half = cycle // split
    step = np.arange(split)[:, None] * np.arange(half)[None, :] % cycle
    angle = step * (2.0 * math.pi / cycle)
    twiddle = np.stack([np.cos(angle), np.sin(angle)]).astype(np.float32)
    step = np.arange(half)[:, None] * np.arange(half)[None, :] % half
    angle = (step * (2.0 * math.pi / half)).reshape(half, half // LANES, LANES)
    table = np.transpose(np.concatenate([np.cos(angle), np.sin(angle)], axis=2), (1, 0, 2))
    return twiddle, table.astype(ml_dtypes.bfloat16)


def sorting(pixels, split):
    place = np.arange(pixels) % split * (pixels // split) + np.arange(pixels) // split
    return (place[:, None] == np.arange(pixels)[None, :]).astype(ml_dtypes.bfloat16)


def local(sky_map, pixel_mask, noise_factor, cycle_legendre, band_power, channel_cov, test_matrix):
    cycles, pixels, chans = sky_map.shape
    modes, _ = band_power.shape
    offsets = cycle_legendre.shape[2]
    columns = test_matrix.shape[3]
    mode_count, pair = lax.axis_size("mode"), lax.axis_size("low")
    groups = pair * mode_count
    devices = lax.axis_size("high") * groups
    width = chans // groups
    group = max(1, SUBLANES // width)
    split = pixels // LANES
    rows = split * cycles * width
    legs = cycles * offsets * (modes // LANES)
    tiles = mode_count
    blocks = modes * mode_count // (tiles * LANES)
    everyone = ("high", "low", "mode")
    hbm, vmem, bf16, f32, shape = pl.ANY, pltpu.VMEM, jnp.bfloat16, jnp.float32, jax.ShapeDtypeStruct
    twiddle, table = transform_tables(split, pixels * mode_count)

    message = call(
        whiten_kernel,
        shape((groups, rows + legs, LANES), bf16),
        [
            vmem((cycles, chans, pixels), bf16),
            vmem((cycles, pixels), jnp.int32),
            vmem((cycles, chans, chans), f32),
            vmem((cycles, offsets, modes), f32),
            vmem((pixels, pixels), bf16),
            vmem((cycles * chans, pixels), bf16),
            vmem((groups, rows + legs, LANES), bf16),
            pltpu.SemaphoreType.DMA((6 + split // 2,)),
        ],
        56,
        [hbm] * 5,
        jnp.transpose(sky_map, (0, 2, 1)),
        pixel_mask,
        noise_factor[:, 0],
        jnp.transpose(cycle_legendre, (0, 2, 1)),
        jnp.asarray(sorting(pixels, split)),
        out_space=hbm,
        cost=(2 * cycles * chans * pixels * (pixels + 4 * chans), 8 * MIB),
    )
    message = lax.all_to_all(message, ("low", "mode"), 0, 0, tiled=True)

    alm = call(
        functools.partial(modes_kernel, width, offsets),
        shape((offsets, mode_count, 2 * width, modes), bf16),
        [
            vmem((tiles, tiles * LANES, 2 * LANES), bf16),
            vmem((pair * rows, tiles * LANES), bf16),
            vmem((pair * cycles * offsets, mode_count * modes), f32),
            vmem((pair * rows, 2 * LANES), f32),
            vmem((pair * rows, 2 * LANES), f32),
            vmem((blocks, 2, pair * cycles // group, group * width, LANES), f32),
            vmem((offsets, mode_count, 2 * width, modes), bf16),
            pltpu.SemaphoreType.DMA((tiles,)),
            pltpu.SemaphoreType.DMA((tiles // 2, 2 * blocks)),
        ],
        40,
        [vmem, hbm, vmem],
        jnp.asarray(twiddle),
        jnp.asarray(table),
        message,
        out_space=hbm,
        cost=(4 * pair * rows * (tiles * LANES) ** 2, 8 * MIB),
    )
    alm = alm.reshape(devices, 2 * width, modes)
    alm = lax.all_to_all(alm, everyone, 0, 0, tiled=True)
    alm = alm.reshape(devices // groups, groups, 2 * width, modes)

    share = columns // (devices)
    fold = LANES // chans
    packed = share % (8 * fold) == 0
    part = call(
        sketch_kernel,
        shape((devices, share // fold, LANES) if packed else (columns, chans), f32),
        [vmem((2, chans, modes), f32)],
        24,
        [vmem] * 4,
        alm,
        jnp.transpose(band_power),
        channel_cov,
        jnp.transpose(test_matrix[0], (1, 0, 2)),
    )
    if not packed:
        part = part.reshape(devices, share, chans)
    part = lax.all_to_all(part, everyone, 0, 0, tiled=True)
    return jnp.transpose(call(total_kernel, shape((share, chans), f32), [], 16, [vmem], part))


def solution(mesh):
    patches, modes = mesh.shape["patch"], mesh.shape["mode"]
    mesh = jax.sharding.Mesh(mesh.devices.reshape(patches // 2, 2, modes), ("high", "low", "mode"))
    patch = ("high", "low")
    return jax.shard_map(
        local,
        mesh=mesh,
        in_specs=(
            P(patch, "mode", None),
            P(patch, "mode"),
            P(patch, "mode", None, None),
            P(patch, "mode", None),
            P("mode", patch),
            P(),
            P(patch, "mode", None, None),
        ),
        out_specs=P(None, (*patch, "mode")),
        check_vma=False,
    )
```

```python
import functools
import math

import jax
import jax.numpy as jnp
import ml_dtypes
import numpy as np
from jax import lax
from jax.experimental import pallas as pl
from jax.experimental.pallas import tpu as pltpu
from jax.sharding import PartitionSpec as P

LANES = 128
MIB = 1 << 20
SUBLANES = 8


def rotate(value, step, points):
    re, im = value
    step %= points
    if step == 0:
        return re, im
    if 2 * step == points:
        return -re, -im
    if 4 * step == points:
        return im, -re
    if 8 * step == points:
        return (re + im) * math.sqrt(0.5), (im - re) * math.sqrt(0.5)
    if 8 * step == 3 * points:
        return (im - re) * math.sqrt(0.5), (re + im) * -math.sqrt(0.5)
    c, s = math.cos(2 * math.pi * step / points), math.sin(2 * math.pi * step / points)
    return re * c + im * s, im * c - re * s


def dft(values):
    n = len(values)
    if n == 1:
        return values
    half = n // 2
    even, odd = dft(values[0::2]), dft(values[1::2])
    out = [None] * n
    for b in range(half):
        re, im = rotate(odd[b], b, n)
        out[b] = even[b][0] + re, even[b][1] + im
        out[b + half] = even[b][0] - re, even[b][1] - im
    return out


def whiten_kernel(sky_hbm, mask_hbm, factor_hbm, leg_hbm, out_hbm, leg_out, *refs):
    sky, mask, factor, leg, sort, white, stage, leg_rows, sems = refs
    cycles, chans, pixels = sky.shape
    groups = stage.shape[0]
    width = chans // groups
    group = max(1, SUBLANES // width)
    tall = group * width
    split = pixels // LANES
    sources, targets = (factor_hbm, sky_hbm, mask_hbm, leg_hbm), (factor, sky, mask, leg)
    copies = [pltpu.make_async_copy(a, b, sems.at[n]) for n, (a, b) in enumerate(zip(sources, targets))]
    for copy in copies:
        copy.start()
    shape = (2 * LANES, LANES)
    ahead = lax.broadcasted_iota(jnp.int32, shape, 0) - split * lax.broadcasted_iota(jnp.int32, shape, 1)
    for first in range(0, pixels, 2 * LANES):
        for s in range(split):
            block = jnp.where(ahead == s - first, 1.0, 0.0).astype(jnp.bfloat16)
            sort[first : first + 2 * LANES, s * LANES : (s + 1) * LANES] = block
    copies[0].wait()
    row_of = lax.broadcasted_iota(jnp.int32, (tall, group * chans), 0) // width
    lane_of = lax.broadcasted_iota(jnp.int32, (tall, group * chans), 1) // chans
    lefts = []
    for pack in range(cycles // group):
        rows = []
        for e in range(groups):
            tile = [factor[pack * group + g, e * width : (e + 1) * width, :] for g in range(group)]
            tile = jnp.concatenate(tile, axis=0)
            rows.append(jnp.where(row_of == lane_of, jnp.concatenate([tile] * group, axis=1), 0.0))
        rows = jnp.concatenate(rows, axis=0)
        high = rows.astype(jnp.bfloat16)
        low = (rows - high.astype(jnp.float32)).astype(jnp.bfloat16)
        lefts.append(jnp.concatenate([high, low], axis=1))
    for copy in copies[1:3]:
        copy.wait()
    cycle_of = lax.broadcasted_iota(jnp.int32, (tall, pixels), 0) // width
    for pack in range(cycles // group):
        data = jnp.concatenate([sky[pack * group + g] for g in range(group)] * 2, axis=0)
        value = jnp.dot(lefts[pack], data, preferred_element_type=jnp.float32)
        keep = jnp.broadcast_to(mask[pack * group : pack * group + 1, :], (tall, pixels))
        for g in range(1, group):
            keep = jnp.where(cycle_of < g, keep, mask[pack * group + g : pack * group + g + 1, :])
        keep = keep.astype(jnp.float32)
        for e in range(groups):
            place = (e * (cycles // group) + pack) * tall
            white[place : place + tall, :] = (value[e * tall : (e + 1) * tall] * keep).astype(jnp.bfloat16)
    copies[3].wait()
    count = cycles * width
    rows = jnp.concatenate([leg[r] for r in range(cycles)], axis=0).astype(jnp.bfloat16)
    high = rows.shape[0]
    for n in range(rows.shape[1] // LANES):
        leg_rows[n * high : (n + 1) * high, :] = rows[:, n * LANES : (n + 1) * LANES]
    sends = [pltpu.make_async_copy(leg_rows, leg_out, sems.at[4])]
    sends[0].start()

    def send(first, last):
        where = (slice(None), slice(first, last))
        sends.append(pltpu.make_async_copy(stage.at[where], out_hbm.at[where], sems.at[4 + len(sends)]))
        sends[-1].start()

    for pair in range(split // 2):
        wide = slice(pair * 2 * LANES, (pair + 1) * 2 * LANES)
        value = jnp.dot(white[...], sort[:, wide], preferred_element_type=jnp.float32).astype(jnp.bfloat16)
        for side in range(2):
            s = pair * 2 + side
            for e in range(groups):
                stage[e, s * count : (s + 1) * count, :] = value[
                    e * count : (e + 1) * count, side * LANES : (side + 1) * LANES
                ]
        send(pair * 2 * count, (pair + 1) * 2 * count)
    for send in sends:
        send.wait()


def modes_kernel(width, offsets, twiddle_ref, table_hbm, leg_hbm, z_ref, out_hbm, *refs):
    table, left, leg_in, leg, prod_a, prod_b, x_ref, out_ref, table_sems, leg_sem, out_sems = refs
    tiles = table.shape[0]
    split = twiddle_ref.shape[1]
    tall = x_ref.shape[3]
    group = tall // width
    modes = out_ref.shape[3]
    sources = out_ref.shape[1]
    parts = z_ref.shape[0] // sources
    cycles = leg.shape[0] // offsets
    blocks = sources * modes // (tiles * LANES)
    per = modes // LANES
    count = cycles // parts * width
    high = cycles // parts * offsets

    def copy(tile):
        return pltpu.make_async_copy(table_hbm.at[tile], table.at[tile], table_sems.at[tile])

    def store(step, n):
        mode_tile = n // 2 * tiles + 2 * step + n % 2
        lanes = pl.ds(pl.multiple_of(mode_tile % per * LANES, LANES), LANES)
        where = (slice(None), mode_tile // per, slice(None), lanes)
        return pltpu.make_async_copy(out_ref.at[where], out_hbm.at[where], out_sems.at[step, n])

    copy(0).start()
    leg_copy = pltpu.make_async_copy(leg_hbm, leg_in, leg_sem)
    leg_copy.start()
    copy(1).start()
    for p in range(parts):
        for q in range(sources):
            for n in range(split):
                place = (n * parts + p) * count
                rows = z_ref[p * sources + q, n * count : (n + 1) * count, :]
                left[place : place + count, q * LANES : (q + 1) * LANES] = rows
    for tile in range(2, tiles):
        copy(tile).start()

    def product(tile, prod):
        prod[...] = jnp.dot(left[...], table[tile], preferred_element_type=jnp.float32)

    copy(0).wait()
    product(0, prod_a)
    leg_copy.wait()
    for p in range(parts):
        for q in range(sources):
            for n in range(per):
                rows = leg_in[p * sources + q, n * high : (n + 1) * high, :].astype(jnp.float32)
                leg[p * high : (p + 1) * high, (q * per + n) * LANES : (q * per + n + 1) * LANES] = rows

    def use(tile, prod):
        lanes = pl.ds(pl.multiple_of(tile * LANES, LANES), LANES)
        cosine, sine = twiddle_ref[0, :, lanes], twiddle_ref[1, :, lanes]
        cycle_of = lax.broadcasted_iota(jnp.int32, (tall, LANES), 0) // width
        for pack in range(cycles // group):
            values = []
            for s in range(split):
                place = (s * cycles + pack * group) * width
                re = prod[place : place + tall, :LANES]
                im = prod[place : place + tall, LANES:]
                if s == 0:
                    values.append((re, -im))
                else:
                    c, d = cosine[s : s + 1, :], sine[s : s + 1, :]
                    values.append((re * c - im * d, -(re * d) - im * c))
            parts = dft(values)
            for b in range(blocks):
                x_ref[b, 0, pack] = parts[b][0]
                x_ref[b, 1, pack] = parts[b][1]
        for b in range(blocks):
            mode_tile = b * tiles + tile
            d, n = mode_tile // per, mode_tile % per
            mode = pl.ds(pl.multiple_of(mode_tile * LANES, LANES), LANES)
            parts = [[x_ref[b, t, pack] for pack in range(cycles // group)] for t in range(2)]
            for k in range(offsets):
                total = [None, None]
                for pack in range(cycles // group):
                    row = None
                    for g in range(group):
                        r = pack * group + g
                        next_row = leg[r * offsets + k : r * offsets + k + 1, mode]
                        if g == 0:
                            row = jnp.broadcast_to(next_row, (tall, LANES))
                        else:
                            row = jnp.where(cycle_of < g, row, next_row)
                    for t in range(2):
                        term = row * parts[t][pack]
                        total[t] = term if pack == 0 else total[t] + term
                step = tall // 2
                while step >= width:
                    total = [value + pltpu.roll(value, step, 0) for value in total]
                    step //= 2
                if group == 1:
                    both = jnp.concatenate(total, axis=0)
                else:
                    both = jnp.where(cycle_of < 1, total[0], total[1])[: 2 * width]
                place = pl.ds(pl.multiple_of(n * LANES, LANES), LANES)
                out_ref[k, d, :, place] = both.astype(jnp.bfloat16)

    @pl.loop(0, tiles // 2)
    def _(step):
        copy(2 * step + 1).wait()

        @pl.when(2 * step + 2 < tiles)
        def _():
            copy(2 * step + 2).wait()

        product(2 * step + 1, prod_b)
        use(2 * step, prod_a)
        product(jnp.minimum(2 * step + 2, tiles - 1), prod_a)
        use(2 * step + 1, prod_b)
        for n in range(2 * blocks):
            store(step, n).start()

    @pl.loop(0, tiles // 2)
    def _(step):
        for n in range(2 * blocks):
            store(step, n).wait()


def sketch_kernel(alm_ref, band_ref, cov_ref, test_ref, out_ref, left_ref):
    patches, groups, rows, lanes = alm_ref.shape
    chans = cov_ref.shape[0]
    width = rows // 2
    for g in range(groups):
        part = alm_ref[0, g].astype(jnp.float32)
        for p in range(1, patches):
            part += alm_ref[p, g].astype(jnp.float32)
        part = part * band_ref[...]
        for t in range(2):
            left_ref[t, g * width : (g + 1) * width, :] = part[t * width : (t + 1) * width]
    sketch = None
    for t in range(2):
        term = lax.dot_general(
            test_ref[t],
            left_ref[t].astype(jnp.bfloat16),
            (((0,), (1,)), ((), ())),
            preferred_element_type=jnp.float32,
        )
        sketch = term if t == 0 else sketch + term
    mixed = lax.dot_general(
        sketch,
        cov_ref[...],
        (((1,), (1,)), ((), ())),
        precision=lax.Precision.HIGHEST,
        preferred_element_type=jnp.float32,
    )
    if out_ref.ndim == 2:
        out_ref[...] = mixed
    else:
        owners, block, _ = out_ref.shape
        fold = out_ref.shape[2] // chans
        mixed = mixed.reshape(owners, fold, block, chans)
        out_ref[...] = jnp.concatenate([mixed[:, n] for n in range(fold)], axis=-1)


def total_kernel(part_ref, out_ref):
    block, chans = part_ref.shape[1], out_ref.shape[1]
    total = jnp.sum(part_ref[...], axis=0)
    for n in range(part_ref.shape[2] // chans):
        out_ref[n * block : (n + 1) * block, :] = total[:, n * chans : (n + 1) * chans]


def call(kernel, shape, scratch, mib, spaces, *operands, out_space=pltpu.VMEM, cost=(0, 0)):
    return pl.pallas_call(
        kernel,
        out_shape=shape,
        in_specs=[pl.BlockSpec(memory_space=space) for space in spaces],
        out_specs=jax.tree.map(lambda _: pl.BlockSpec(memory_space=out_space), shape),
        scratch_shapes=scratch,
        compiler_params=pltpu.CompilerParams(vmem_limit_bytes=mib * MIB),
        cost_estimate=pl.CostEstimate(flops=cost[0], bytes_accessed=cost[1], transcendentals=0),
    )(*operands)


def transform_tables(split, cycle):
    half = cycle // split
    step = np.arange(split)[:, None] * np.arange(half)[None, :] % cycle
    angle = step * (2.0 * math.pi / cycle)
    twiddle = np.stack([np.cos(angle), np.sin(angle)]).astype(np.float32)
    step = np.arange(half)[:, None] * np.arange(half)[None, :] % half
    angle = (step * (2.0 * math.pi / half)).reshape(half, half // LANES, LANES)
    table = np.transpose(np.concatenate([np.cos(angle), np.sin(angle)], axis=2), (1, 0, 2))
    return twiddle, table.astype(ml_dtypes.bfloat16)


def local(sky_map, pixel_mask, noise_factor, cycle_legendre, band_power, channel_cov, test_matrix):
    cycles, pixels, chans = sky_map.shape
    modes, _ = band_power.shape
    offsets = cycle_legendre.shape[2]
    columns = test_matrix.shape[3]
    mode_count, pair = lax.axis_size("mode"), lax.axis_size("low")
    groups = pair * mode_count
    devices = lax.axis_size("high") * groups
    width = chans // groups
    group = max(1, SUBLANES // width)
    split = pixels // LANES
    rows = split * cycles * width
    legs = cycles * offsets * (modes // LANES)
    tiles = mode_count
    blocks = modes * mode_count // (tiles * LANES)
    everyone = ("high", "low", "mode")
    hbm, vmem, bf16, f32, shape = pl.ANY, pltpu.VMEM, jnp.bfloat16, jnp.float32, jax.ShapeDtypeStruct
    twiddle, table = transform_tables(split, pixels * mode_count)

    message, leg = call(
        whiten_kernel,
        [shape((groups, rows, LANES), bf16), shape((legs, LANES), bf16)],
        [
            vmem((cycles, chans, pixels), bf16),
            vmem((cycles, pixels), jnp.int32),
            vmem((cycles, chans, chans), f32),
            vmem((cycles, offsets, modes), f32),
            vmem((pixels, pixels), bf16),
            vmem((cycles * chans, pixels), bf16),
            vmem((groups, rows, LANES), bf16),
            vmem((legs, LANES), bf16),
            pltpu.SemaphoreType.DMA((5 + split // 2,)),
        ],
        56,
        [hbm] * 4,
        jnp.transpose(sky_map, (0, 2, 1)),
        pixel_mask,
        noise_factor[:, 0],
        jnp.transpose(cycle_legendre, (0, 2, 1)),
        out_space=hbm,
        cost=(2 * cycles * chans * pixels * (pixels + 4 * chans), 8 * MIB),
    )
    message = lax.all_to_all(message, ("low", "mode"), 0, 0, tiled=True)
    leg = lax.all_gather(leg, ("low", "mode"), axis=0, tiled=False)

    alm = call(
        functools.partial(modes_kernel, width, offsets),
        shape((offsets, mode_count, 2 * width, modes), bf16),
        [
            vmem((tiles, tiles * LANES, 2 * LANES), bf16),
            vmem((pair * rows, tiles * LANES), bf16),
            vmem((groups, legs, LANES), bf16),
            vmem((pair * cycles * offsets, mode_count * modes), f32),
            vmem((pair * rows, 2 * LANES), f32),
            vmem((pair * rows, 2 * LANES), f32),
            vmem((blocks, 2, pair * cycles // group, group * width, LANES), f32),
            vmem((offsets, mode_count, 2 * width, modes), bf16),
            pltpu.SemaphoreType.DMA((tiles,)),
            pltpu.SemaphoreType.DMA(()),
            pltpu.SemaphoreType.DMA((tiles // 2, 2 * blocks)),
        ],
        40,
        [vmem, hbm, hbm, vmem],
        jnp.asarray(twiddle),
        jnp.asarray(table),
        leg,
        message,
        out_space=hbm,
        cost=(4 * pair * rows * (tiles * LANES) ** 2, 8 * MIB),
    )
    alm = alm.reshape(devices, 2 * width, modes)
    alm = lax.all_to_all(alm, everyone, 0, 0, tiled=True)
    alm = alm.reshape(devices // groups, groups, 2 * width, modes)

    share = columns // (devices)
    fold = LANES // chans
    packed = share % (8 * fold) == 0
    part = call(
        sketch_kernel,
        shape((devices, share // fold, LANES) if packed else (columns, chans), f32),
        [vmem((2, chans, modes), f32)],
        24,
        [vmem] * 4,
        alm,
        jnp.transpose(band_power),
        channel_cov,
        jnp.transpose(test_matrix[0], (1, 0, 2)),
    )
    if not packed:
        part = part.reshape(devices, share, chans)
    part = lax.all_to_all(part, everyone, 0, 0, tiled=True)
    return jnp.transpose(call(total_kernel, shape((share, chans), f32), [], 16, [vmem], part))


def solution(mesh):
    patches, modes = mesh.shape["patch"], mesh.shape["mode"]
    mesh = jax.sharding.Mesh(mesh.devices.reshape(patches // 2, 2, modes), ("high", "low", "mode"))
    patch = ("high", "low")
    return jax.shard_map(
        local,
        mesh=mesh,
        in_specs=(
            P(patch, "mode", None),
            P(patch, "mode"),
            P(patch, "mode", None, None),
            P(patch, "mode", None),
            P("mode", patch),
            P(),
            P(patch, "mode", None, None),
        ),
        out_specs=P(None, (*patch, "mode")),
        check_vma=False,
    )
```

```python
import functools
import math

import jax
import jax.numpy as jnp
import ml_dtypes
import numpy as np
from jax import lax
from jax.experimental import pallas as pl
from jax.experimental.pallas import tpu as pltpu
from jax.sharding import PartitionSpec as P

LANES = 128
MIB = 1 << 20
SUBLANES = 8


def rotate(value, step, points):
    re, im = value
    step %= points
    if step == 0:
        return re, im
    if 2 * step == points:
        return -re, -im
    if 4 * step == points:
        return im, -re
    if 8 * step == points:
        return (re + im) * math.sqrt(0.5), (im - re) * math.sqrt(0.5)
    if 8 * step == 3 * points:
        return (im - re) * math.sqrt(0.5), (re + im) * -math.sqrt(0.5)
    c, s = math.cos(2 * math.pi * step / points), math.sin(2 * math.pi * step / points)
    return re * c + im * s, im * c - re * s


def dft(values):
    n = len(values)
    if n == 1:
        return values
    half = n // 2
    even, odd = dft(values[0::2]), dft(values[1::2])
    out = [None] * n
    for b in range(half):
        re, im = rotate(odd[b], b, n)
        out[b] = even[b][0] + re, even[b][1] + im
        out[b + half] = even[b][0] - re, even[b][1] - im
    return out


def whiten_kernel(sky_hbm, mask_hbm, factor_hbm, leg_hbm, out_hbm, leg_out, *refs):
    sky, mask, factor, leg, sort, white, stage, leg_rows, sems = refs
    cycles, chans, pixels = sky.shape
    groups = stage.shape[0]
    width = chans // groups
    group = max(1, SUBLANES // width)
    tall = group * width
    split = pixels // LANES
    sources, targets = (factor_hbm, sky_hbm, mask_hbm, leg_hbm), (factor, sky, mask, leg)
    copies = [pltpu.make_async_copy(a, b, sems.at[n]) for n, (a, b) in enumerate(zip(sources, targets))]
    for copy in copies:
        copy.start()
    shape = (2 * LANES, LANES)
    ahead = lax.broadcasted_iota(jnp.int32, shape, 0) - split * lax.broadcasted_iota(jnp.int32, shape, 1)
    for first in range(0, pixels, 2 * LANES):
        for s in range(split):
            block = jnp.where(ahead == s - first, 1.0, 0.0).astype(jnp.bfloat16)
            sort[first : first + 2 * LANES, s * LANES : (s + 1) * LANES] = block
    copies[0].wait()
    row_of = lax.broadcasted_iota(jnp.int32, (tall, group * chans), 0) // width
    lane_of = lax.broadcasted_iota(jnp.int32, (tall, group * chans), 1) // chans
    lefts = []
    for pack in range(cycles // group):
        rows = []
        for e in range(groups):
            tile = [factor[pack * group + g, e * width : (e + 1) * width, :] for g in range(group)]
            tile = jnp.concatenate(tile, axis=0)
            rows.append(jnp.where(row_of == lane_of, jnp.concatenate([tile] * group, axis=1), 0.0))
        rows = jnp.concatenate(rows, axis=0)
        high = rows.astype(jnp.bfloat16)
        low = (rows - high.astype(jnp.float32)).astype(jnp.bfloat16)
        lefts.append(jnp.concatenate([high, low], axis=1))
    for copy in copies[1:3]:
        copy.wait()
    cycle_of = lax.broadcasted_iota(jnp.int32, (tall, pixels), 0) // width
    for pack in range(cycles // group):
        data = jnp.concatenate([sky[pack * group + g] for g in range(group)] * 2, axis=0)
        value = jnp.dot(lefts[pack], data, preferred_element_type=jnp.float32)
        keep = jnp.broadcast_to(mask[pack * group : pack * group + 1, :], (tall, pixels))
        for g in range(1, group):
            keep = jnp.where(cycle_of < g, keep, mask[pack * group + g : pack * group + g + 1, :])
        keep = keep.astype(jnp.float32)
        for e in range(groups):
            place = (e * (cycles // group) + pack) * tall
            white[place : place + tall, :] = (value[e * tall : (e + 1) * tall] * keep).astype(jnp.bfloat16)
    copies[3].wait()
    count = cycles * width
    rows = jnp.concatenate([leg[r] for r in range(cycles)], axis=0).astype(jnp.bfloat16)
    high = rows.shape[0]
    for n in range(rows.shape[1] // LANES):
        leg_rows[n * high : (n + 1) * high, :] = rows[:, n * LANES : (n + 1) * LANES]
    sends = [pltpu.make_async_copy(leg_rows, leg_out, sems.at[4])]
    sends[0].start()

    def send(first, last):
        where = (slice(None), slice(first, last))
        sends.append(pltpu.make_async_copy(stage.at[where], out_hbm.at[where], sems.at[4 + len(sends)]))
        sends[-1].start()

    for pair in range(split // 2):
        wide = slice(pair * 2 * LANES, (pair + 1) * 2 * LANES)
        value = jnp.dot(white[...], sort[:, wide], preferred_element_type=jnp.float32).astype(jnp.bfloat16)
        for side in range(2):
            s = pair * 2 + side
            for e in range(groups):
                stage[e, s * count : (s + 1) * count, :] = value[
                    e * count : (e + 1) * count, side * LANES : (side + 1) * LANES
                ]
        send(pair * 2 * count, (pair + 1) * 2 * count)
    for send in sends:
        send.wait()


def modes_kernel(width, offsets, mine_ref, twiddle_ref, table_hbm, leg_hbm, z_ref, out_hbm, *refs):
    table, left, leg_in, leg, prod_a, prod_b, x_ref, out_ref, table_sems, leg_sem, out_sems = refs
    tiles = table.shape[0]
    split = twiddle_ref.shape[1]
    tall = x_ref.shape[3]
    group = tall // width
    modes = out_ref.shape[3]
    sources = out_ref.shape[1]
    parts = z_ref.shape[0] // sources
    cycles = leg.shape[0] // offsets
    blocks = sources * modes // (tiles * LANES)
    per = modes // LANES
    count = cycles // parts * width
    high = cycles // parts * offsets

    mine = mine_ref[0]

    def copy(tile):
        return pltpu.make_async_copy(table_hbm.at[tile], table.at[tile], table_sems.at[tile])

    def store(step, n):
        mode_tile = n // 2 * tiles + 2 * step + n % 2
        lanes = pl.ds(pl.multiple_of(mode_tile % per * LANES, LANES), LANES)
        where = (slice(None), mode_tile // per, slice(None), lanes)
        return pltpu.make_async_copy(out_ref.at[where], out_hbm.at[where], out_sems.at[step, n])

    copy(0).start()
    leg_copy = pltpu.make_async_copy(leg_hbm, leg_in, leg_sem)
    leg_copy.start()
    copy(1).start()
    for p in range(parts):
        for q in range(sources):
            for n in range(split):
                place = (n * parts + p) * count
                rows = z_ref[p * sources + q, n * count : (n + 1) * count, :]
                left[place : place + count, q * LANES : (q + 1) * LANES] = rows
    for tile in range(2, tiles):
        copy(tile).start()

    def product(tile, prod):
        prod[...] = jnp.dot(left[...], table[tile], preferred_element_type=jnp.float32)

    copy(0).wait()
    product(0, prod_a)
    leg_copy.wait()
    for p in range(parts):
        for q in range(sources):
            for n in range(per):
                place = (p * per + n) * high
                rows = leg_in[q, place : place + high, :].astype(jnp.float32)
                place = pl.ds(pl.multiple_of((mine + parts - p) % parts * high, high), high)
                leg[place, (q * per + n) * LANES : (q * per + n + 1) * LANES] = rows

    def use(tile, prod):
        lanes = pl.ds(pl.multiple_of(tile * LANES, LANES), LANES)
        cosine, sine = twiddle_ref[0, :, lanes], twiddle_ref[1, :, lanes]
        cycle_of = lax.broadcasted_iota(jnp.int32, (tall, LANES), 0) // width
        for pack in range(cycles // group):
            values = []
            for s in range(split):
                place = (s * cycles + pack * group) * width
                re = prod[place : place + tall, :LANES]
                im = prod[place : place + tall, LANES:]
                if s == 0:
                    values.append((re, -im))
                else:
                    c, d = cosine[s : s + 1, :], sine[s : s + 1, :]
                    values.append((re * c - im * d, -(re * d) - im * c))
            parts = dft(values)
            for b in range(blocks):
                x_ref[b, 0, pack] = parts[b][0]
                x_ref[b, 1, pack] = parts[b][1]
        for b in range(blocks):
            mode_tile = b * tiles + tile
            d, n = mode_tile // per, mode_tile % per
            mode = pl.ds(pl.multiple_of(mode_tile * LANES, LANES), LANES)
            parts = [[x_ref[b, t, pack] for pack in range(cycles // group)] for t in range(2)]
            for k in range(offsets):
                total = [None, None]
                for pack in range(cycles // group):
                    row = None
                    for g in range(group):
                        r = pack * group + g
                        next_row = leg[r * offsets + k : r * offsets + k + 1, mode]
                        if g == 0:
                            row = jnp.broadcast_to(next_row, (tall, LANES))
                        else:
                            row = jnp.where(cycle_of < g, row, next_row)
                    for t in range(2):
                        term = row * parts[t][pack]
                        total[t] = term if pack == 0 else total[t] + term
                step = tall // 2
                while step >= width:
                    total = [value + pltpu.roll(value, step, 0) for value in total]
                    step //= 2
                if group == 1:
                    both = jnp.concatenate(total, axis=0)
                else:
                    both = jnp.where(cycle_of < 1, total[0], total[1])[: 2 * width]
                place = pl.ds(pl.multiple_of(n * LANES, LANES), LANES)
                out_ref[k, d, :, place] = both.astype(jnp.bfloat16)

    @pl.loop(0, tiles // 2)
    def _(step):
        copy(2 * step + 1).wait()

        @pl.when(2 * step + 2 < tiles)
        def _():
            copy(2 * step + 2).wait()

        product(2 * step + 1, prod_b)
        use(2 * step, prod_a)
        product(jnp.minimum(2 * step + 2, tiles - 1), prod_a)
        use(2 * step + 1, prod_b)
        for n in range(2 * blocks):
            store(step, n).start()

    @pl.loop(0, tiles // 2)
    def _(step):
        for n in range(2 * blocks):
            store(step, n).wait()


def sketch_kernel(alm_ref, band_ref, cov_ref, test_ref, out_ref, left_ref):
    patches, groups, rows, lanes = alm_ref.shape
    chans = cov_ref.shape[0]
    width = rows // 2
    for g in range(groups):
        part = alm_ref[0, g].astype(jnp.float32)
        for p in range(1, patches):
            part += alm_ref[p, g].astype(jnp.float32)
        part = part * band_ref[...]
        for t in range(2):
            left_ref[t, g * width : (g + 1) * width, :] = part[t * width : (t + 1) * width]
    sketch = None
    for t in range(2):
        term = lax.dot_general(
            test_ref[t],
            left_ref[t].astype(jnp.bfloat16),
            (((0,), (1,)), ((), ())),
            preferred_element_type=jnp.float32,
        )
        sketch = term if t == 0 else sketch + term
    mixed = lax.dot_general(
        sketch,
        cov_ref[...],
        (((1,), (1,)), ((), ())),
        precision=lax.Precision.HIGHEST,
        preferred_element_type=jnp.float32,
    )
    if out_ref.ndim == 2:
        out_ref[...] = mixed
    else:
        owners, block, _ = out_ref.shape
        fold = out_ref.shape[2] // chans
        mixed = mixed.reshape(owners, fold, block, chans)
        out_ref[...] = jnp.concatenate([mixed[:, n] for n in range(fold)], axis=-1)


def total_kernel(part_ref, out_ref):
    block, chans = part_ref.shape[1], out_ref.shape[1]
    total = jnp.sum(part_ref[...], axis=0)
    for n in range(part_ref.shape[2] // chans):
        out_ref[n * block : (n + 1) * block, :] = total[:, n * chans : (n + 1) * chans]


def call(kernel, shape, scratch, mib, spaces, *operands, out_space=pltpu.VMEM, cost=(0, 0)):
    return pl.pallas_call(
        kernel,
        out_shape=shape,
        in_specs=[pl.BlockSpec(memory_space=space) for space in spaces],
        out_specs=jax.tree.map(lambda _: pl.BlockSpec(memory_space=out_space), shape),
        scratch_shapes=scratch,
        compiler_params=pltpu.CompilerParams(vmem_limit_bytes=mib * MIB),
        cost_estimate=pl.CostEstimate(flops=cost[0], bytes_accessed=cost[1], transcendentals=0),
    )(*operands)


def transform_tables(split, cycle):
    half = cycle // split
    step = np.arange(split)[:, None] * np.arange(half)[None, :] % cycle
    angle = step * (2.0 * math.pi / cycle)
    twiddle = np.stack([np.cos(angle), np.sin(angle)]).astype(np.float32)
    step = np.arange(half)[:, None] * np.arange(half)[None, :] % half
    angle = (step * (2.0 * math.pi / half)).reshape(half, half // LANES, LANES)
    table = np.transpose(np.concatenate([np.cos(angle), np.sin(angle)], axis=2), (1, 0, 2))
    return twiddle, table.astype(ml_dtypes.bfloat16)


def local(sky_map, pixel_mask, noise_factor, cycle_legendre, band_power, channel_cov, test_matrix):
    cycles, pixels, chans = sky_map.shape
    modes, _ = band_power.shape
    offsets = cycle_legendre.shape[2]
    columns = test_matrix.shape[3]
    mode_count, pair = lax.axis_size("mode"), lax.axis_size("low")
    groups = pair * mode_count
    devices = lax.axis_size("high") * groups
    width = chans // groups
    group = max(1, SUBLANES // width)
    split = pixels // LANES
    rows = split * cycles * width
    legs = cycles * offsets * (modes // LANES)
    tiles = mode_count
    blocks = modes * mode_count // (tiles * LANES)
    everyone = ("high", "low", "mode")
    hbm, vmem, bf16, f32, shape = pl.ANY, pltpu.VMEM, jnp.bfloat16, jnp.float32, jax.ShapeDtypeStruct
    twiddle, table = transform_tables(split, pixels * mode_count)

    message, leg = call(
        whiten_kernel,
        [shape((groups, rows, LANES), bf16), shape((legs, LANES), bf16)],
        [
            vmem((cycles, chans, pixels), bf16),
            vmem((cycles, pixels), jnp.int32),
            vmem((cycles, chans, chans), f32),
            vmem((cycles, offsets, modes), f32),
            vmem((pixels, pixels), bf16),
            vmem((cycles * chans, pixels), bf16),
            vmem((groups, rows, LANES), bf16),
            vmem((legs, LANES), bf16),
            pltpu.SemaphoreType.DMA((5 + split // 2,)),
        ],
        56,
        [hbm] * 4,
        jnp.transpose(sky_map, (0, 2, 1)),
        pixel_mask,
        noise_factor[:, 0],
        jnp.transpose(cycle_legendre, (0, 2, 1)),
        out_space=hbm,
        cost=(2 * cycles * chans * pixels * (pixels + 4 * chans), 8 * MIB),
    )
    message = lax.all_to_all(message, ("low", "mode"), 0, 0, tiled=True)
    legendre = [leg]
    for n in range(1, pair):
        legendre.append(lax.ppermute(leg, "low", [(i, (i + n) % pair) for i in range(pair)]))
    leg = lax.all_gather(jnp.concatenate(legendre), "mode", axis=0, tiled=False)
    mine = lax.axis_index("low").astype(jnp.int32).reshape(1)

    alm = call(
        functools.partial(modes_kernel, width, offsets),
        shape((offsets, mode_count, 2 * width, modes), bf16),
        [
            vmem((tiles, tiles * LANES, 2 * LANES), bf16),
            vmem((pair * rows, tiles * LANES), bf16),
            vmem((mode_count, pair * legs, LANES), bf16),
            vmem((pair * cycles * offsets, mode_count * modes), f32),
            vmem((pair * rows, 2 * LANES), f32),
            vmem((pair * rows, 2 * LANES), f32),
            vmem((blocks, 2, pair * cycles // group, group * width, LANES), f32),
            vmem((offsets, mode_count, 2 * width, modes), bf16),
            pltpu.SemaphoreType.DMA((tiles,)),
            pltpu.SemaphoreType.DMA(()),
            pltpu.SemaphoreType.DMA((tiles // 2, 2 * blocks)),
        ],
        56,
        [pltpu.SMEM, vmem, hbm, hbm, vmem],
        mine,
        jnp.asarray(twiddle),
        jnp.asarray(table),
        leg,
        message,
        out_space=hbm,
        cost=(4 * pair * rows * (tiles * LANES) ** 2, 8 * MIB),
    )
    alm = alm.reshape(devices, 2 * width, modes)
    alm = lax.all_to_all(alm, everyone, 0, 0, tiled=True)
    alm = alm.reshape(devices // groups, groups, 2 * width, modes)

    share = columns // (devices)
    fold = LANES // chans
    packed = share % (8 * fold) == 0
    part = call(
        sketch_kernel,
        shape((devices, share // fold, LANES) if packed else (columns, chans), f32),
        [vmem((2, chans, modes), f32)],
        24,
        [vmem] * 4,
        alm,
        jnp.transpose(band_power),
        channel_cov,
        jnp.transpose(test_matrix[0], (1, 0, 2)),
    )
    if not packed:
        part = part.reshape(devices, share, chans)
    part = lax.all_to_all(part, everyone, 0, 0, tiled=True)
    return jnp.transpose(call(total_kernel, shape((share, chans), f32), [], 16, [vmem], part))


def solution(mesh):
    patches, modes = mesh.shape["patch"], mesh.shape["mode"]
    mesh = jax.sharding.Mesh(mesh.devices.reshape(patches // 2, 2, modes), ("high", "low", "mode"))
    patch = ("high", "low")
    return jax.shard_map(
        local,
        mesh=mesh,
        in_specs=(
            P(patch, "mode", None),
            P(patch, "mode"),
            P(patch, "mode", None, None),
            P(patch, "mode", None),
            P("mode", patch),
            P(),
            P(patch, "mode", None, None),
        ),
        out_specs=P(None, (*patch, "mode")),
        check_vma=False,
    )
```

```python
import functools
import math

import jax
import jax.numpy as jnp
import ml_dtypes
import numpy as np
from jax import lax
from jax.experimental import pallas as pl
from jax.experimental.pallas import tpu as pltpu
from jax.sharding import PartitionSpec as P

LANES = 128
MIB = 1 << 20
SUBLANES = 8


def rotate(value, step, points):
    re, im = value
    step %= points
    if step == 0:
        return re, im
    if 2 * step == points:
        return -re, -im
    if 4 * step == points:
        return im, -re
    if 8 * step == points:
        return (re + im) * math.sqrt(0.5), (im - re) * math.sqrt(0.5)
    if 8 * step == 3 * points:
        return (im - re) * math.sqrt(0.5), (re + im) * -math.sqrt(0.5)
    c, s = math.cos(2 * math.pi * step / points), math.sin(2 * math.pi * step / points)
    return re * c + im * s, im * c - re * s


def dft(values):
    n = len(values)
    if n == 1:
        return values
    half = n // 2
    even, odd = dft(values[0::2]), dft(values[1::2])
    out = [None] * n
    for b in range(half):
        re, im = rotate(odd[b], b, n)
        out[b] = even[b][0] + re, even[b][1] + im
        out[b + half] = even[b][0] - re, even[b][1] - im
    return out


def whiten_kernel(sky_hbm, mask_hbm, factor_hbm, leg_hbm, out_hbm, leg_out, *refs):
    sky, mask, factor, leg, sort, white, stage, leg_rows, sems = refs
    cycles, chans, pixels = sky.shape
    groups = stage.shape[0]
    width = chans // groups
    group = max(1, SUBLANES // width)
    tall = group * width
    split = pixels // LANES
    sources, targets = (factor_hbm, sky_hbm, mask_hbm, leg_hbm), (factor, sky, mask, leg)
    copies = [pltpu.make_async_copy(a, b, sems.at[n]) for n, (a, b) in enumerate(zip(sources, targets))]
    for copy in copies:
        copy.start()
    shape = (2 * LANES, LANES)
    ahead = lax.broadcasted_iota(jnp.int32, shape, 0) - split * lax.broadcasted_iota(jnp.int32, shape, 1)
    for first in range(0, pixels, 2 * LANES):
        for s in range(split):
            block = jnp.where(ahead == s - first, 1.0, 0.0).astype(jnp.bfloat16)
            sort[first : first + 2 * LANES, s * LANES : (s + 1) * LANES] = block
    copies[0].wait()
    row_of = lax.broadcasted_iota(jnp.int32, (tall, group * chans), 0) // width
    lane_of = lax.broadcasted_iota(jnp.int32, (tall, group * chans), 1) // chans
    lefts = []
    for pack in range(cycles // group):
        rows = []
        for e in range(groups):
            tile = [factor[pack * group + g, e * width : (e + 1) * width, :] for g in range(group)]
            tile = jnp.concatenate(tile, axis=0)
            rows.append(jnp.where(row_of == lane_of, jnp.concatenate([tile] * group, axis=1), 0.0))
        rows = jnp.concatenate(rows, axis=0)
        high = rows.astype(jnp.bfloat16)
        low = (rows - high.astype(jnp.float32)).astype(jnp.bfloat16)
        lefts.append(jnp.concatenate([high, low], axis=1))
    for copy in copies[1:3]:
        copy.wait()
    cycle_of = lax.broadcasted_iota(jnp.int32, (tall, pixels), 0) // width
    for pack in range(cycles // group):
        data = jnp.concatenate([sky[pack * group + g] for g in range(group)] * 2, axis=0)
        value = jnp.dot(lefts[pack], data, preferred_element_type=jnp.float32)
        keep = jnp.broadcast_to(mask[pack * group : pack * group + 1, :], (tall, pixels))
        for g in range(1, group):
            keep = jnp.where(cycle_of < g, keep, mask[pack * group + g : pack * group + g + 1, :])
        keep = keep.astype(jnp.float32)
        for e in range(groups):
            place = (e * (cycles // group) + pack) * tall
            white[place : place + tall, :] = (value[e * tall : (e + 1) * tall] * keep).astype(jnp.bfloat16)
    copies[3].wait()
    count = cycles * width
    rows = jnp.concatenate([leg[r] for r in range(cycles)], axis=0).astype(jnp.bfloat16)
    high = rows.shape[0]
    for n in range(rows.shape[1] // LANES):
        leg_rows[n * high : (n + 1) * high, :] = rows[:, n * LANES : (n + 1) * LANES]
    sends = [pltpu.make_async_copy(leg_rows, leg_out, sems.at[4])]
    sends[0].start()

    def send(first, last):
        where = (slice(None), slice(first, last))
        sends.append(pltpu.make_async_copy(stage.at[where], out_hbm.at[where], sems.at[4 + len(sends)]))
        sends[-1].start()

    for pair in range(split // 2):
        wide = slice(pair * 2 * LANES, (pair + 1) * 2 * LANES)
        value = jnp.dot(white[...], sort[:, wide], preferred_element_type=jnp.float32).astype(jnp.bfloat16)
        for side in range(2):
            s = pair * 2 + side
            for e in range(groups):
                stage[e, s * count : (s + 1) * count, :] = value[
                    e * count : (e + 1) * count, side * LANES : (side + 1) * LANES
                ]
        send(pair * 2 * count, (pair + 1) * 2 * count)
    for send in sends:
        send.wait()


def legendre_kernel(mine_ref, own_ref, *refs):
    out_ref = refs[-1]
    mine, pair, high = mine_ref[0], len(refs), own_ref.shape[0]

    def place(n):
        return pl.ds(pl.multiple_of((mine + pair - n) % pair * high, high), high)

    out_ref[place(0), :] = own_ref[...]
    for n in range(1, pair):
        leg = refs[n - 1]
        rows = jnp.concatenate([leg[r] for r in range(leg.shape[0])], axis=0).astype(jnp.bfloat16)
        tiles = [rows[:, n * LANES : (n + 1) * LANES] for n in range(rows.shape[1] // LANES)]
        out_ref[place(n), :] = jnp.concatenate(tiles, axis=0)


def modes_kernel(width, offsets, twiddle_ref, table_hbm, leg_in, z_ref, out_hbm, *refs):
    table, left, leg, prod_a, prod_b, x_ref, out_ref, table_sems, out_sems = refs
    tiles = table.shape[0]
    split = twiddle_ref.shape[1]
    tall = x_ref.shape[3]
    group = tall // width
    modes = out_ref.shape[3]
    sources = out_ref.shape[1]
    parts = z_ref.shape[0] // sources
    cycles = leg.shape[0] // offsets
    blocks = sources * modes // (tiles * LANES)
    per = modes // LANES
    count = cycles // parts * width
    high = cycles // parts * offsets

    def copy(tile):
        return pltpu.make_async_copy(table_hbm.at[tile], table.at[tile], table_sems.at[tile])

    def store(step, n):
        mode_tile = n // 2 * tiles + 2 * step + n % 2
        lanes = pl.ds(pl.multiple_of(mode_tile % per * LANES, LANES), LANES)
        where = (slice(None), mode_tile // per, slice(None), lanes)
        return pltpu.make_async_copy(out_ref.at[where], out_hbm.at[where], out_sems.at[step, n])

    copy(0).start()
    copy(1).start()
    for p in range(parts):
        for q in range(sources):
            for n in range(split):
                place = (n * parts + p) * count
                rows = z_ref[p * sources + q, n * count : (n + 1) * count, :]
                left[place : place + count, q * LANES : (q + 1) * LANES] = rows
    for tile in range(2, tiles):
        copy(tile).start()

    def product(tile, prod):
        prod[...] = jnp.dot(left[...], table[tile], preferred_element_type=jnp.float32)

    copy(0).wait()
    product(0, prod_a)
    for p in range(parts):
        for q in range(sources):
            for n in range(per):
                place = (p * per + n) * high
                rows = leg_in[q, place : place + high, :].astype(jnp.float32)
                leg[p * high : (p + 1) * high, (q * per + n) * LANES : (q * per + n + 1) * LANES] = rows

    def use(tile, prod):
        lanes = pl.ds(pl.multiple_of(tile * LANES, LANES), LANES)
        cosine, sine = twiddle_ref[0, :, lanes], twiddle_ref[1, :, lanes]
        cycle_of = lax.broadcasted_iota(jnp.int32, (tall, LANES), 0) // width
        for pack in range(cycles // group):
            values = []
            for s in range(split):
                place = (s * cycles + pack * group) * width
                re = prod[place : place + tall, :LANES]
                im = prod[place : place + tall, LANES:]
                if s == 0:
                    values.append((re, -im))
                else:
                    c, d = cosine[s : s + 1, :], sine[s : s + 1, :]
                    values.append((re * c - im * d, -(re * d) - im * c))
            parts = dft(values)
            for b in range(blocks):
                x_ref[b, 0, pack] = parts[b][0]
                x_ref[b, 1, pack] = parts[b][1]
        for b in range(blocks):
            mode_tile = b * tiles + tile
            d, n = mode_tile // per, mode_tile % per
            mode = pl.ds(pl.multiple_of(mode_tile * LANES, LANES), LANES)
            parts = [[x_ref[b, t, pack] for pack in range(cycles // group)] for t in range(2)]
            for k in range(offsets):
                total = [None, None]
                for pack in range(cycles // group):
                    row = None
                    for g in range(group):
                        r = pack * group + g
                        next_row = leg[r * offsets + k : r * offsets + k + 1, mode]
                        if g == 0:
                            row = jnp.broadcast_to(next_row, (tall, LANES))
                        else:
                            row = jnp.where(cycle_of < g, row, next_row)
                    for t in range(2):
                        term = row * parts[t][pack]
                        total[t] = term if pack == 0 else total[t] + term
                step = tall // 2
                while step >= width:
                    total = [value + pltpu.roll(value, step, 0) for value in total]
                    step //= 2
                if group == 1:
                    both = jnp.concatenate(total, axis=0)
                else:
                    both = jnp.where(cycle_of < 1, total[0], total[1])[: 2 * width]
                place = pl.ds(pl.multiple_of(n * LANES, LANES), LANES)
                out_ref[k, d, :, place] = both.astype(jnp.bfloat16)

    @pl.loop(0, tiles // 2)
    def _(step):
        copy(2 * step + 1).wait()

        @pl.when(2 * step + 2 < tiles)
        def _():
            copy(2 * step + 2).wait()

        product(2 * step + 1, prod_b)
        use(2 * step, prod_a)
        product(jnp.minimum(2 * step + 2, tiles - 1), prod_a)
        use(2 * step + 1, prod_b)
        for n in range(2 * blocks):
            store(step, n).start()

    @pl.loop(0, tiles // 2)
    def _(step):
        for n in range(2 * blocks):
            store(step, n).wait()


def sketch_kernel(alm_ref, band_ref, cov_ref, test_ref, out_ref, left_ref):
    patches, groups, rows, lanes = alm_ref.shape
    chans = cov_ref.shape[0]
    width = rows // 2
    for g in range(groups):
        part = alm_ref[0, g].astype(jnp.float32)
        for p in range(1, patches):
            part += alm_ref[p, g].astype(jnp.float32)
        part = part * band_ref[...]
        for t in range(2):
            left_ref[t, g * width : (g + 1) * width, :] = part[t * width : (t + 1) * width]
    sketch = None
    for t in range(2):
        term = lax.dot_general(
            test_ref[t],
            left_ref[t].astype(jnp.bfloat16),
            (((0,), (1,)), ((), ())),
            preferred_element_type=jnp.float32,
        )
        sketch = term if t == 0 else sketch + term
    mixed = lax.dot_general(
        sketch,
        cov_ref[...],
        (((1,), (1,)), ((), ())),
        precision=lax.Precision.HIGHEST,
        preferred_element_type=jnp.float32,
    )
    if out_ref.ndim == 2:
        out_ref[...] = mixed
    else:
        owners, block, _ = out_ref.shape
        fold = out_ref.shape[2] // chans
        mixed = mixed.reshape(owners, fold, block, chans)
        out_ref[...] = jnp.concatenate([mixed[:, n] for n in range(fold)], axis=-1)


def total_kernel(part_ref, out_ref):
    block, chans = part_ref.shape[1], out_ref.shape[1]
    total = jnp.sum(part_ref[...], axis=0)
    for n in range(part_ref.shape[2] // chans):
        out_ref[n * block : (n + 1) * block, :] = total[:, n * chans : (n + 1) * chans]


def call(kernel, shape, scratch, mib, spaces, *operands, out_space=pltpu.VMEM, cost=(0, 0)):
    return pl.pallas_call(
        kernel,
        out_shape=shape,
        in_specs=[pl.BlockSpec(memory_space=space) for space in spaces],
        out_specs=jax.tree.map(lambda _: pl.BlockSpec(memory_space=out_space), shape),
        scratch_shapes=scratch,
        compiler_params=pltpu.CompilerParams(vmem_limit_bytes=mib * MIB),
        cost_estimate=pl.CostEstimate(flops=cost[0], bytes_accessed=cost[1], transcendentals=0),
    )(*operands)


def transform_tables(split, cycle):
    half = cycle // split
    step = np.arange(split)[:, None] * np.arange(half)[None, :] % cycle
    angle = step * (2.0 * math.pi / cycle)
    twiddle = np.stack([np.cos(angle), np.sin(angle)]).astype(np.float32)
    step = np.arange(half)[:, None] * np.arange(half)[None, :] % half
    angle = (step * (2.0 * math.pi / half)).reshape(half, half // LANES, LANES)
    table = np.transpose(np.concatenate([np.cos(angle), np.sin(angle)], axis=2), (1, 0, 2))
    return twiddle, table.astype(ml_dtypes.bfloat16)


def local(sky_map, pixel_mask, noise_factor, cycle_legendre, band_power, channel_cov, test_matrix):
    cycles, pixels, chans = sky_map.shape
    modes, _ = band_power.shape
    offsets = cycle_legendre.shape[2]
    columns = test_matrix.shape[3]
    mode_count, pair = lax.axis_size("mode"), lax.axis_size("low")
    groups = pair * mode_count
    devices = lax.axis_size("high") * groups
    width = chans // groups
    group = max(1, SUBLANES // width)
    split = pixels // LANES
    rows = split * cycles * width
    legs = cycles * offsets * (modes // LANES)
    tiles = mode_count
    blocks = modes * mode_count // (tiles * LANES)
    everyone = ("high", "low", "mode")
    hbm, vmem, bf16, f32, shape = pl.ANY, pltpu.VMEM, jnp.bfloat16, jnp.float32, jax.ShapeDtypeStruct
    twiddle, table = transform_tables(split, pixels * mode_count)

    own_leg = jnp.transpose(cycle_legendre, (0, 2, 1))
    others = [lax.ppermute(own_leg, "low", [(i, (i + n) % pair) for i in range(pair)]) for n in range(1, pair)]

    message, leg = call(
        whiten_kernel,
        [shape((groups, rows, LANES), bf16), shape((legs, LANES), bf16)],
        [
            vmem((cycles, chans, pixels), bf16),
            vmem((cycles, pixels), jnp.int32),
            vmem((cycles, chans, chans), f32),
            vmem((cycles, offsets, modes), f32),
            vmem((pixels, pixels), bf16),
            vmem((cycles * chans, pixels), bf16),
            vmem((groups, rows, LANES), bf16),
            vmem((legs, LANES), bf16),
            pltpu.SemaphoreType.DMA((5 + split // 2,)),
        ],
        56,
        [hbm] * 4,
        jnp.transpose(sky_map, (0, 2, 1)),
        pixel_mask,
        noise_factor[:, 0],
        own_leg,
        out_space=hbm,
        cost=(2 * cycles * chans * pixels * (pixels + 4 * chans), 8 * MIB),
    )
    message = lax.all_to_all(message, ("low", "mode"), 0, 0, tiled=True)
    leg = call(
        legendre_kernel,
        shape((pair * legs, LANES), bf16),
        [],
        16,
        [pltpu.SMEM] + [vmem] * pair,
        lax.axis_index("low").astype(jnp.int32).reshape(1),
        leg,
        *others,
    )
    leg = lax.all_gather(leg, "mode", axis=0, tiled=False)

    alm = call(
        functools.partial(modes_kernel, width, offsets),
        shape((offsets, mode_count, 2 * width, modes), bf16),
        [
            vmem((tiles, tiles * LANES, 2 * LANES), bf16),
            vmem((pair * rows, tiles * LANES), bf16),
            vmem((pair * cycles * offsets, mode_count * modes), f32),
            vmem((pair * rows, 2 * LANES), f32),
            vmem((pair * rows, 2 * LANES), f32),
            vmem((blocks, 2, pair * cycles // group, group * width, LANES), f32),
            vmem((offsets, mode_count, 2 * width, modes), bf16),
            pltpu.SemaphoreType.DMA((tiles,)),
            pltpu.SemaphoreType.DMA((tiles // 2, 2 * blocks)),
        ],
        40,
        [vmem, hbm, vmem, vmem],
        jnp.asarray(twiddle),
        jnp.asarray(table),
        leg,
        message,
        out_space=hbm,
        cost=(4 * pair * rows * (tiles * LANES) ** 2, 8 * MIB),
    )
    alm = alm.reshape(devices, 2 * width, modes)
    alm = lax.all_to_all(alm, everyone, 0, 0, tiled=True)
    alm = alm.reshape(devices // groups, groups, 2 * width, modes)

    share = columns // (devices)
    fold = LANES // chans
    packed = share % (8 * fold) == 0
    part = call(
        sketch_kernel,
        shape((devices, share // fold, LANES) if packed else (columns, chans), f32),
        [vmem((2, chans, modes), f32)],
        24,
        [vmem] * 4,
        alm,
        jnp.transpose(band_power),
        channel_cov,
        jnp.transpose(test_matrix[0], (1, 0, 2)),
    )
    if not packed:
        part = part.reshape(devices, share, chans)
    part = lax.all_to_all(part, everyone, 0, 0, tiled=True)
    return jnp.transpose(call(total_kernel, shape((share, chans), f32), [], 16, [vmem], part))


def solution(mesh):
    patches, modes = mesh.shape["patch"], mesh.shape["mode"]
    mesh = jax.sharding.Mesh(mesh.devices.reshape(patches // 2, 2, modes), ("high", "low", "mode"))
    patch = ("high", "low")
    return jax.shard_map(
        local,
        mesh=mesh,
        in_specs=(
            P(patch, "mode", None),
            P(patch, "mode"),
            P(patch, "mode", None, None),
            P(patch, "mode", None),
            P("mode", patch),
            P(),
            P(patch, "mode", None, None),
        ),
        out_specs=P(None, (*patch, "mode")),
        check_vma=False,
    )
```

```python
import functools
import math

import jax
import jax.numpy as jnp
import ml_dtypes
import numpy as np
from jax import lax
from jax.experimental import pallas as pl
from jax.experimental.pallas import tpu as pltpu
from jax.sharding import PartitionSpec as P

LANES = 128
MIB = 1 << 20
SUBLANES = 8


def rotate(value, step, points):
    re, im = value
    step %= points
    if step == 0:
        return re, im
    if 2 * step == points:
        return -re, -im
    if 4 * step == points:
        return im, -re
    if 8 * step == points:
        return (re + im) * math.sqrt(0.5), (im - re) * math.sqrt(0.5)
    if 8 * step == 3 * points:
        return (im - re) * math.sqrt(0.5), (re + im) * -math.sqrt(0.5)
    c, s = math.cos(2 * math.pi * step / points), math.sin(2 * math.pi * step / points)
    return re * c + im * s, im * c - re * s


def dft(values):
    n = len(values)
    if n == 1:
        return values
    half = n // 2
    even, odd = dft(values[0::2]), dft(values[1::2])
    out = [None] * n
    for b in range(half):
        re, im = rotate(odd[b], b, n)
        out[b] = even[b][0] + re, even[b][1] + im
        out[b + half] = even[b][0] - re, even[b][1] - im
    return out


def whiten_kernel(sky_hbm, mask_hbm, factor_hbm, leg_hbm, after_hbm, out_hbm, leg_out, *refs):
    sky, mask, factor, leg, sort, white, stage, leg_rows, sems = refs
    cycles, chans, pixels = sky.shape
    groups = stage.shape[0]
    width = chans // groups
    group = max(1, SUBLANES // width)
    tall = group * width
    split = pixels // LANES
    sources, targets = (factor_hbm, sky_hbm, mask_hbm, leg_hbm), (factor, sky, mask, leg)
    copies = [pltpu.make_async_copy(a, b, sems.at[n]) for n, (a, b) in enumerate(zip(sources, targets))]
    for copy in copies:
        copy.start()
    shape = (2 * LANES, LANES)
    ahead = lax.broadcasted_iota(jnp.int32, shape, 0) - split * lax.broadcasted_iota(jnp.int32, shape, 1)
    for first in range(0, pixels, 2 * LANES):
        for s in range(split):
            block = jnp.where(ahead == s - first, 1.0, 0.0).astype(jnp.bfloat16)
            sort[first : first + 2 * LANES, s * LANES : (s + 1) * LANES] = block
    copies[0].wait()
    row_of = lax.broadcasted_iota(jnp.int32, (tall, group * chans), 0) // width
    lane_of = lax.broadcasted_iota(jnp.int32, (tall, group * chans), 1) // chans
    lefts = []
    for pack in range(cycles // group):
        rows = []
        for e in range(groups):
            tile = [factor[pack * group + g, e * width : (e + 1) * width, :] for g in range(group)]
            tile = jnp.concatenate(tile, axis=0)
            rows.append(jnp.where(row_of == lane_of, jnp.concatenate([tile] * group, axis=1), 0.0))
        rows = jnp.concatenate(rows, axis=0)
        high = rows.astype(jnp.bfloat16)
        low = (rows - high.astype(jnp.float32)).astype(jnp.bfloat16)
        lefts.append(jnp.concatenate([high, low], axis=1))
    for copy in copies[1:3]:
        copy.wait()
    cycle_of = lax.broadcasted_iota(jnp.int32, (tall, pixels), 0) // width
    for pack in range(cycles // group):
        data = jnp.concatenate([sky[pack * group + g] for g in range(group)] * 2, axis=0)
        value = jnp.dot(lefts[pack], data, preferred_element_type=jnp.float32)
        keep = jnp.broadcast_to(mask[pack * group : pack * group + 1, :], (tall, pixels))
        for g in range(1, group):
            keep = jnp.where(cycle_of < g, keep, mask[pack * group + g : pack * group + g + 1, :])
        keep = keep.astype(jnp.float32)
        for e in range(groups):
            place = (e * (cycles // group) + pack) * tall
            white[place : place + tall, :] = (value[e * tall : (e + 1) * tall] * keep).astype(jnp.bfloat16)
    copies[3].wait()
    count = cycles * width
    rows = jnp.concatenate([leg[r] for r in range(cycles)], axis=0).astype(jnp.bfloat16)
    high = rows.shape[0]
    for n in range(rows.shape[1] // LANES):
        leg_rows[n * high : (n + 1) * high, :] = rows[:, n * LANES : (n + 1) * LANES]
    sends = [pltpu.make_async_copy(leg_rows, leg_out, sems.at[4])]
    sends[0].start()

    def send(first, last):
        where = (slice(None), slice(first, last))
        sends.append(pltpu.make_async_copy(stage.at[where], out_hbm.at[where], sems.at[4 + len(sends)]))
        sends[-1].start()

    for pair in range(split // 2):
        wide = slice(pair * 2 * LANES, (pair + 1) * 2 * LANES)
        value = jnp.dot(white[...], sort[:, wide], preferred_element_type=jnp.float32).astype(jnp.bfloat16)
        for side in range(2):
            s = pair * 2 + side
            for e in range(groups):
                stage[e, s * count : (s + 1) * count, :] = value[
                    e * count : (e + 1) * count, side * LANES : (side + 1) * LANES
                ]
        send(pair * 2 * count, (pair + 1) * 2 * count)
    for send in sends:
        send.wait()


def legendre_kernel(mine_ref, own_ref, *refs):
    out_ref = refs[-1]
    mine, pair, high = mine_ref[0], len(refs), own_ref.shape[0]

    def place(n):
        return pl.ds(pl.multiple_of((mine + pair - n) % pair * high, high), high)

    out_ref[place(0), :] = own_ref[...]
    for n in range(1, pair):
        leg = refs[n - 1]
        rows = jnp.concatenate([leg[r] for r in range(leg.shape[0])], axis=0).astype(jnp.bfloat16)
        tiles = [rows[:, n * LANES : (n + 1) * LANES] for n in range(rows.shape[1] // LANES)]
        out_ref[place(n), :] = jnp.concatenate(tiles, axis=0)


def modes_kernel(width, offsets, twiddle_ref, table_hbm, leg_in, z_ref, out_hbm, *refs):
    table, left, leg, prod_a, prod_b, x_ref, out_ref, table_sems, out_sems = refs
    tiles = table.shape[0]
    split = twiddle_ref.shape[1]
    tall = x_ref.shape[3]
    group = tall // width
    modes = out_ref.shape[3]
    sources = out_ref.shape[1]
    parts = z_ref.shape[0] // sources
    cycles = leg.shape[0] // offsets
    blocks = sources * modes // (tiles * LANES)
    per = modes // LANES
    count = cycles // parts * width
    high = cycles // parts * offsets

    def copy(tile):
        return pltpu.make_async_copy(table_hbm.at[tile], table.at[tile], table_sems.at[tile])

    def store(step, n):
        mode_tile = n // 2 * tiles + 2 * step + n % 2
        lanes = pl.ds(pl.multiple_of(mode_tile % per * LANES, LANES), LANES)
        where = (slice(None), mode_tile // per, slice(None), lanes)
        return pltpu.make_async_copy(out_ref.at[where], out_hbm.at[where], out_sems.at[step, n])

    copy(0).start()
    copy(1).start()
    for p in range(parts):
        for q in range(sources):
            for n in range(split):
                place = (n * parts + p) * count
                rows = z_ref[p * sources + q, n * count : (n + 1) * count, :]
                left[place : place + count, q * LANES : (q + 1) * LANES] = rows
    for tile in range(2, tiles):
        copy(tile).start()

    def product(tile, prod):
        prod[...] = jnp.dot(left[...], table[tile], preferred_element_type=jnp.float32)

    copy(0).wait()
    product(0, prod_a)
    for p in range(parts):
        for q in range(sources):
            for n in range(per):
                place = (p * per + n) * high
                rows = leg_in[q, place : place + high, :].astype(jnp.float32)
                leg[p * high : (p + 1) * high, (q * per + n) * LANES : (q * per + n + 1) * LANES] = rows

    def use(tile, prod):
        lanes = pl.ds(pl.multiple_of(tile * LANES, LANES), LANES)
        cosine, sine = twiddle_ref[0, :, lanes], twiddle_ref[1, :, lanes]
        cycle_of = lax.broadcasted_iota(jnp.int32, (tall, LANES), 0) // width
        for pack in range(cycles // group):
            values = []
            for s in range(split):
                place = (s * cycles + pack * group) * width
                re = prod[place : place + tall, :LANES]
                im = prod[place : place + tall, LANES:]
                if s == 0:
                    values.append((re, -im))
                else:
                    c, d = cosine[s : s + 1, :], sine[s : s + 1, :]
                    values.append((re * c - im * d, -(re * d) - im * c))
            parts = dft(values)
            for b in range(blocks):
                x_ref[b, 0, pack] = parts[b][0]
                x_ref[b, 1, pack] = parts[b][1]
        for b in range(blocks):
            mode_tile = b * tiles + tile
            d, n = mode_tile // per, mode_tile % per
            mode = pl.ds(pl.multiple_of(mode_tile * LANES, LANES), LANES)
            parts = [[x_ref[b, t, pack] for pack in range(cycles // group)] for t in range(2)]
            for k in range(offsets):
                total = [None, None]
                for pack in range(cycles // group):
                    row = None
                    for g in range(group):
                        r = pack * group + g
                        next_row = leg[r * offsets + k : r * offsets + k + 1, mode]
                        if g == 0:
                            row = jnp.broadcast_to(next_row, (tall, LANES))
                        else:
                            row = jnp.where(cycle_of < g, row, next_row)
                    for t in range(2):
                        term = row * parts[t][pack]
                        total[t] = term if pack == 0 else total[t] + term
                step = tall // 2
                while step >= width:
                    total = [value + pltpu.roll(value, step, 0) for value in total]
                    step //= 2
                if group == 1:
                    both = jnp.concatenate(total, axis=0)
                else:
                    both = jnp.where(cycle_of < 1, total[0], total[1])[: 2 * width]
                place = pl.ds(pl.multiple_of(n * LANES, LANES), LANES)
                out_ref[k, d, :, place] = both.astype(jnp.bfloat16)

    @pl.loop(0, tiles // 2)
    def _(step):
        copy(2 * step + 1).wait()

        @pl.when(2 * step + 2 < tiles)
        def _():
            copy(2 * step + 2).wait()

        product(2 * step + 1, prod_b)
        use(2 * step, prod_a)
        product(jnp.minimum(2 * step + 2, tiles - 1), prod_a)
        use(2 * step + 1, prod_b)
        for n in range(2 * blocks):
            store(step, n).start()

    @pl.loop(0, tiles // 2)
    def _(step):
        for n in range(2 * blocks):
            store(step, n).wait()


def sketch_kernel(alm_ref, band_ref, cov_ref, test_ref, out_ref, left_ref):
    patches, groups, rows, lanes = alm_ref.shape
    chans = cov_ref.shape[0]
    width = rows // 2
    for g in range(groups):
        part = alm_ref[0, g].astype(jnp.float32)
        for p in range(1, patches):
            part += alm_ref[p, g].astype(jnp.float32)
        part = part * band_ref[...]
        for t in range(2):
            left_ref[t, g * width : (g + 1) * width, :] = part[t * width : (t + 1) * width]
    sketch = None
    for t in range(2):
        term = lax.dot_general(
            test_ref[t],
            left_ref[t].astype(jnp.bfloat16),
            (((0,), (1,)), ((), ())),
            preferred_element_type=jnp.float32,
        )
        sketch = term if t == 0 else sketch + term
    mixed = lax.dot_general(
        sketch,
        cov_ref[...],
        (((1,), (1,)), ((), ())),
        precision=lax.Precision.HIGHEST,
        preferred_element_type=jnp.float32,
    )
    if out_ref.ndim == 2:
        out_ref[...] = mixed
    else:
        owners, block, _ = out_ref.shape
        fold = out_ref.shape[2] // chans
        mixed = mixed.reshape(owners, fold, block, chans)
        out_ref[...] = jnp.concatenate([mixed[:, n] for n in range(fold)], axis=-1)


def total_kernel(part_ref, out_ref):
    block, chans = part_ref.shape[1], out_ref.shape[1]
    total = jnp.sum(part_ref[...], axis=0)
    for n in range(part_ref.shape[2] // chans):
        out_ref[n * block : (n + 1) * block, :] = total[:, n * chans : (n + 1) * chans]


def call(kernel, shape, scratch, mib, spaces, *operands, out_space=pltpu.VMEM, cost=(0, 0)):
    return pl.pallas_call(
        kernel,
        out_shape=shape,
        in_specs=[pl.BlockSpec(memory_space=space) for space in spaces],
        out_specs=jax.tree.map(lambda _: pl.BlockSpec(memory_space=out_space), shape),
        scratch_shapes=scratch,
        compiler_params=pltpu.CompilerParams(vmem_limit_bytes=mib * MIB),
        cost_estimate=pl.CostEstimate(flops=cost[0], bytes_accessed=cost[1], transcendentals=0),
    )(*operands)


def transform_tables(split, cycle):
    half = cycle // split
    step = np.arange(split)[:, None] * np.arange(half)[None, :] % cycle
    angle = step * (2.0 * math.pi / cycle)
    twiddle = np.stack([np.cos(angle), np.sin(angle)]).astype(np.float32)
    step = np.arange(half)[:, None] * np.arange(half)[None, :] % half
    angle = (step * (2.0 * math.pi / half)).reshape(half, half // LANES, LANES)
    table = np.transpose(np.concatenate([np.cos(angle), np.sin(angle)], axis=2), (1, 0, 2))
    return twiddle, table.astype(ml_dtypes.bfloat16)


def local(sky_map, pixel_mask, noise_factor, cycle_legendre, band_power, channel_cov, test_matrix):
    cycles, pixels, chans = sky_map.shape
    modes, _ = band_power.shape
    offsets = cycle_legendre.shape[2]
    columns = test_matrix.shape[3]
    mode_count, pair = lax.axis_size("mode"), lax.axis_size("low")
    groups = pair * mode_count
    devices = lax.axis_size("high") * groups
    width = chans // groups
    group = max(1, SUBLANES // width)
    split = pixels // LANES
    rows = split * cycles * width
    legs = cycles * offsets * (modes // LANES)
    tiles = mode_count
    blocks = modes * mode_count // (tiles * LANES)
    everyone = ("high", "low", "mode")
    hbm, vmem, bf16, f32, shape = pl.ANY, pltpu.VMEM, jnp.bfloat16, jnp.float32, jax.ShapeDtypeStruct
    twiddle, table = transform_tables(split, pixels * mode_count)

    own_leg = jnp.transpose(cycle_legendre, (0, 2, 1))
    others = [lax.ppermute(own_leg, "low", [(i, (i + n) % pair) for i in range(pair)]) for n in range(1, pair)]

    message, leg = call(
        whiten_kernel,
        [shape((groups, rows, LANES), bf16), shape((legs, LANES), bf16)],
        [
            vmem((cycles, chans, pixels), bf16),
            vmem((cycles, pixels), jnp.int32),
            vmem((cycles, chans, chans), f32),
            vmem((cycles, offsets, modes), f32),
            vmem((pixels, pixels), bf16),
            vmem((cycles * chans, pixels), bf16),
            vmem((groups, rows, LANES), bf16),
            vmem((legs, LANES), bf16),
            pltpu.SemaphoreType.DMA((5 + split // 2,)),
        ],
        56,
        [hbm] * 5,
        jnp.transpose(sky_map, (0, 2, 1)),
        pixel_mask,
        noise_factor[:, 0],
        own_leg,
        others[0],
        out_space=hbm,
        cost=(2 * cycles * chans * pixels * (pixels + 4 * chans), 8 * MIB),
    )
    message = lax.all_to_all(message, ("low", "mode"), 0, 0, tiled=True)
    leg = call(
        legendre_kernel,
        shape((pair * legs, LANES), bf16),
        [],
        16,
        [pltpu.SMEM] + [vmem] * pair,
        lax.axis_index("low").astype(jnp.int32).reshape(1),
        leg,
        *others,
    )
    leg = lax.all_gather(leg, "mode", axis=0, tiled=False)

    alm = call(
        functools.partial(modes_kernel, width, offsets),
        shape((offsets, mode_count, 2 * width, modes), bf16),
        [
            vmem((tiles, tiles * LANES, 2 * LANES), bf16),
            vmem((pair * rows, tiles * LANES), bf16),
            vmem((pair * cycles * offsets, mode_count * modes), f32),
            vmem((pair * rows, 2 * LANES), f32),
            vmem((pair * rows, 2 * LANES), f32),
            vmem((blocks, 2, pair * cycles // group, group * width, LANES), f32),
            vmem((offsets, mode_count, 2 * width, modes), bf16),
            pltpu.SemaphoreType.DMA((tiles,)),
            pltpu.SemaphoreType.DMA((tiles // 2, 2 * blocks)),
        ],
        40,
        [vmem, hbm, vmem, vmem],
        jnp.asarray(twiddle),
        jnp.asarray(table),
        leg,
        message,
        out_space=hbm,
        cost=(4 * pair * rows * (tiles * LANES) ** 2, 8 * MIB),
    )
    alm = alm.reshape(devices, 2 * width, modes)
    alm = lax.all_to_all(alm, everyone, 0, 0, tiled=True)
    alm = alm.reshape(devices // groups, groups, 2 * width, modes)

    share = columns // (devices)
    fold = LANES // chans
    packed = share % (8 * fold) == 0
    part = call(
        sketch_kernel,
        shape((devices, share // fold, LANES) if packed else (columns, chans), f32),
        [vmem((2, chans, modes), f32)],
        24,
        [vmem] * 4,
        alm,
        jnp.transpose(band_power),
        channel_cov,
        jnp.transpose(test_matrix[0], (1, 0, 2)),
    )
    if not packed:
        part = part.reshape(devices, share, chans)
    part = lax.all_to_all(part, everyone, 0, 0, tiled=True)
    return jnp.transpose(call(total_kernel, shape((share, chans), f32), [], 16, [vmem], part))


def solution(mesh):
    patches, modes = mesh.shape["patch"], mesh.shape["mode"]
    mesh = jax.sharding.Mesh(mesh.devices.reshape(patches // 2, 2, modes), ("high", "low", "mode"))
    patch = ("high", "low")
    return jax.shard_map(
        local,
        mesh=mesh,
        in_specs=(
            P(patch, "mode", None),
            P(patch, "mode"),
            P(patch, "mode", None, None),
            P(patch, "mode", None),
            P("mode", patch),
            P(),
            P(patch, "mode", None, None),
        ),
        out_specs=P(None, (*patch, "mode")),
        check_vma=False,
    )
```

```python
import functools
import math

import jax
import jax.numpy as jnp
import ml_dtypes
import numpy as np
from jax import lax
from jax.experimental import pallas as pl
from jax.experimental.pallas import tpu as pltpu
from jax.sharding import PartitionSpec as P

LANES = 128
MIB = 1 << 20
SUBLANES = 8


def rotate(value, step, points):
    re, im = value
    step %= points
    if step == 0:
        return re, im
    if 2 * step == points:
        return -re, -im
    if 4 * step == points:
        return im, -re
    if 8 * step == points:
        return (re + im) * math.sqrt(0.5), (im - re) * math.sqrt(0.5)
    if 8 * step == 3 * points:
        return (im - re) * math.sqrt(0.5), (re + im) * -math.sqrt(0.5)
    c, s = math.cos(2 * math.pi * step / points), math.sin(2 * math.pi * step / points)
    return re * c + im * s, im * c - re * s


def dft(values):
    n = len(values)
    if n == 1:
        return values
    half = n // 2
    even, odd = dft(values[0::2]), dft(values[1::2])
    out = [None] * n
    for b in range(half):
        re, im = rotate(odd[b], b, n)
        out[b] = even[b][0] + re, even[b][1] + im
        out[b + half] = even[b][0] - re, even[b][1] - im
    return out


def whiten_kernel(order, place_ref, sky_hbm, mask_hbm, factor_hbm, leg_hbm, *refs):
    sky, mask, factor, leg, sort, white, stage, sems = refs[-8:]
    outs = refs[:-8]
    cycles, chans, pixels = sky.shape
    groups = len(outs)
    width = chans // groups
    group = max(1, SUBLANES // width)
    tall = group * width
    split = pixels // LANES
    sources, targets = (factor_hbm, sky_hbm, mask_hbm, leg_hbm), (factor, sky, mask, leg)
    copies = [pltpu.make_async_copy(a, b, sems.at[n]) for n, (a, b) in enumerate(zip(sources, targets))]
    for copy in copies:
        copy.start()
    shape = (2 * LANES, LANES)
    ahead = lax.broadcasted_iota(jnp.int32, shape, 0) - split * lax.broadcasted_iota(jnp.int32, shape, 1)
    for first in range(0, pixels, 2 * LANES):
        for s in range(split):
            block = jnp.where(ahead == s - first, 1.0, 0.0).astype(jnp.bfloat16)
            sort[first : first + 2 * LANES, s * LANES : (s + 1) * LANES] = block
    copies[0].wait()
    row_of = lax.broadcasted_iota(jnp.int32, (tall, group * chans), 0) // width
    lane_of = lax.broadcasted_iota(jnp.int32, (tall, group * chans), 1) // chans
    lefts = []
    for pack in range(cycles // group):
        rows = []
        for e in range(groups):
            tile = [factor[pack * group + g, e * width : (e + 1) * width, :] for g in range(group)]
            tile = jnp.concatenate(tile, axis=0)
            rows.append(jnp.where(row_of == lane_of, jnp.concatenate([tile] * group, axis=1), 0.0))
        rows = jnp.concatenate(rows, axis=0)
        high = rows.astype(jnp.bfloat16)
        low = (rows - high.astype(jnp.float32)).astype(jnp.bfloat16)
        lefts.append(jnp.concatenate([high, low], axis=1))
    for copy in copies[1:3]:
        copy.wait()
    cycle_of = lax.broadcasted_iota(jnp.int32, (tall, pixels), 0) // width
    for pack in range(cycles // group):
        data = jnp.concatenate([sky[pack * group + g] for g in range(group)] * 2, axis=0)
        value = jnp.dot(lefts[pack], data, preferred_element_type=jnp.float32)
        keep = jnp.broadcast_to(mask[pack * group : pack * group + 1, :], (tall, pixels))
        for g in range(1, group):
            keep = jnp.where(cycle_of < g, keep, mask[pack * group + g : pack * group + g + 1, :])
        keep = keep.astype(jnp.float32)
        for e in range(groups):
            place = (e * (cycles // group) + pack) * tall
            white[place : place + tall, :] = (value[e * tall : (e + 1) * tall] * keep).astype(jnp.bfloat16)
    copies[3].wait()
    count = cycles * width
    rows = jnp.concatenate([leg[r] for r in range(cycles)], axis=0).astype(jnp.bfloat16)
    high = rows.shape[0]
    for n in range(rows.shape[1] // LANES):
        for e in range(groups):
            place = split * count + n * high
            stage[e, place : place + high, :] = rows[:, n * LANES : (n + 1) * LANES]
    for pair in range(split // 2):
        wide = slice(pair * 2 * LANES, (pair + 1) * 2 * LANES)
        value = jnp.dot(white[...], sort[:, wide], preferred_element_type=jnp.float32).astype(jnp.bfloat16)
        for side in range(2):
            s = pair * 2 + side
            for e in range(groups):
                stage[e, s * count : (s + 1) * count, :] = value[
                    e * count : (e + 1) * count, side * LANES : (side + 1) * LANES
                ]
    me = place_ref[0]
    sends = [
        pltpu.make_async_copy(stage.at[jnp.bitwise_xor(me, n)], outs[slot], sems.at[4 + slot])
        for slot, n in enumerate(order)
    ]
    for send in sends:
        send.start()
    for send in sends:
        send.wait()


def modes_kernel(order, cycles, width, offsets, place_ref, twiddle_ref, table_hbm, *refs):
    slots = refs[: len(order)]
    keep_hbm, give_hbm, table, left, leg, prod_a, prod_b, x_ref, out_ref, table_sems, out_sems = refs[len(order) :]
    tiles = table.shape[0]
    split = twiddle_ref.shape[1]
    tall = x_ref.shape[3]
    group = tall // width
    modes = out_ref.shape[4]
    sources = len(order)
    blocks = sources * modes // (tiles * LANES)
    per = modes // LANES
    count = cycles * width
    high = cycles * offsets
    half = sources // 2
    core = place_ref[3]

    def chunk(n):
        return jnp.bitwise_xor(place_ref[1], n % half) * 2 + jnp.bitwise_xor(place_ref[2], n // half)


    def copy(tile):
        return pltpu.make_async_copy(table_hbm.at[tile], table.at[tile], table_sems.at[tile])

    def store(step, n, given):
        mode_tile = n // 2 * tiles + 2 * step + n % 2
        lanes = pl.ds(pl.multiple_of(mode_tile % per * LANES, LANES), LANES)
        where = (slice(None), mode_tile // per, slice(None), lanes)
        source = out_ref.at[(jnp.bitwise_xor(core, given), *where)]
        return pltpu.make_async_copy(source, (keep_hbm, give_hbm)[given].at[where], out_sems.at[step, n, given])

    copy(0).start()
    copy(1).start()
    for slot, n in enumerate(order):
        q = chunk(n)
        lanes = pl.ds(pl.multiple_of(q * LANES, LANES), LANES)
        for s in range(split):
            place = s * count
            left[place : place + count, lanes] = slots[slot][s * count : (s + 1) * count, :]
    for tile in range(2, tiles):
        copy(tile).start()

    def product(tile, prod):
        prod[...] = jnp.dot(left[...], table[tile], preferred_element_type=jnp.float32)

    copy(0).wait()
    product(0, prod_a)
    for slot, n in enumerate(order):
        q = chunk(n)
        for j in range(per):
            lanes = pl.ds(pl.multiple_of((q * per + j) * LANES, LANES), LANES)
            place = split * count + j * high
            rows = slots[slot][place : place + high, :].astype(jnp.float32)
            leg[:, lanes] = rows

    def use(tile, prod):
        lanes = pl.ds(pl.multiple_of(tile * LANES, LANES), LANES)
        cosine, sine = twiddle_ref[0, :, lanes], twiddle_ref[1, :, lanes]
        row_in = lax.broadcasted_iota(jnp.int32, (tall, LANES), 0)
        cycle_of = row_in // width
        for pack in range(cycles // group):
            values = []
            for s in range(split):
                place = (s * cycles + pack * group) * width
                re = prod[place : place + tall, :LANES]
                im = prod[place : place + tall, LANES:]
                if s == 0:
                    values.append((re, -im))
                else:
                    c, d = cosine[s : s + 1, :], sine[s : s + 1, :]
                    values.append((re * c - im * d, -(re * d) - im * c))
            parts = dft(values)
            for b in range(blocks):
                x_ref[b, 0, pack] = parts[b][0]
                x_ref[b, 1, pack] = parts[b][1]
        for b in range(blocks):
            mode_tile = b * tiles + tile
            d, n = mode_tile // per, mode_tile % per
            mode = pl.ds(pl.multiple_of(mode_tile * LANES, LANES), LANES)
            for k in range(offsets):
                total = [None, None]
                for pack in range(cycles // group):
                    row = None
                    for g in range(group):
                        r = pack * group + g
                        next_row = leg[r * offsets + k : r * offsets + k + 1, mode]
                        if g == 0:
                            row = jnp.broadcast_to(next_row, (tall, LANES))
                        else:
                            row = jnp.where(cycle_of < g, row, next_row)
                    for t in range(2):
                        term = row * x_ref[b, t, pack]
                        total[t] = term if pack == 0 else total[t] + term
                step = tall // 2
                while step >= width:
                    total = [value + pltpu.roll(value, step, 0) for value in total]
                    step //= 2
                place = pl.ds(pl.multiple_of(n * LANES, LANES), LANES)
                for part in range(2):
                    shift = (tall - part * width // 2, tall + width // 2 - part * width // 2)
                    rows = [pltpu.roll(v, m % tall, 0) if m % tall else v for v, m in zip(total, shift)]
                    both = jnp.where(row_in < width // 2, rows[0], rows[1])[:width]
                    out_ref[part, k, d, :, place] = both.astype(jnp.bfloat16)

    @pl.loop(0, tiles // 2)
    def _(step):
        copy(2 * step + 1).wait()

        @pl.when(2 * step + 2 < tiles)
        def _():
            copy(2 * step + 2).wait()

        product(2 * step + 1, prod_b)
        use(2 * step, prod_a)
        product(jnp.minimum(2 * step + 2, tiles - 1), prod_a)
        use(2 * step + 1, prod_b)
        for n in range(2 * blocks):
            store(step, n, 0).start()
            store(step, n, 1).start()

    @pl.loop(0, tiles // 2)
    def _(step):
        for n in range(2 * blocks):
            store(step, n, 0).wait()
            store(step, n, 1).wait()


def pair_kernel(one_ref, two_ref, out_ref):
    out_ref[...] = (one_ref[...].astype(jnp.float32) + two_ref[...].astype(jnp.float32)).astype(jnp.bfloat16)


def sketch_kernel(alm_ref, band_ref, cov_ref, test_ref, out_ref, left_ref):
    patches, groups, rows, lanes = alm_ref.shape
    chans = cov_ref.shape[0]
    width = rows // 2
    for g in range(groups):
        part = alm_ref[0, g].astype(jnp.float32)
        for p in range(1, patches):
            part += alm_ref[p, g].astype(jnp.float32)
        part = part * band_ref[...]
        for t in range(2):
            left_ref[t, g * width : (g + 1) * width, :] = part[t * width : (t + 1) * width]
    sketch = None
    for t in range(2):
        term = lax.dot_general(
            test_ref[t],
            left_ref[t].astype(jnp.bfloat16),
            (((0,), (1,)), ((), ())),
            preferred_element_type=jnp.float32,
        )
        sketch = term if t == 0 else sketch + term
    mixed = lax.dot_general(
        sketch,
        cov_ref[...],
        (((1,), (1,)), ((), ())),
        precision=lax.Precision.HIGHEST,
        preferred_element_type=jnp.float32,
    )
    if out_ref.ndim == 2:
        out_ref[...] = mixed
    else:
        owners, block, _ = out_ref.shape
        fold = out_ref.shape[2] // chans
        mixed = mixed.reshape(owners, fold, block, chans)
        out_ref[...] = jnp.concatenate([mixed[:, n] for n in range(fold)], axis=-1)


def total_kernel(part_ref, out_ref):
    block, chans = part_ref.shape[1], out_ref.shape[1]
    total = jnp.sum(part_ref[...], axis=0)
    for n in range(part_ref.shape[2] // chans):
        out_ref[n * block : (n + 1) * block, :] = total[:, n * chans : (n + 1) * chans]


def call(kernel, shape, scratch, mib, spaces, *operands, out_space=pltpu.VMEM, cost=(0, 0)):
    return pl.pallas_call(
        kernel,
        out_shape=shape,
        in_specs=[pl.BlockSpec(memory_space=space) for space in spaces],
        out_specs=jax.tree.map(lambda _: pl.BlockSpec(memory_space=out_space), shape),
        scratch_shapes=scratch,
        compiler_params=pltpu.CompilerParams(vmem_limit_bytes=mib * MIB),
        cost_estimate=pl.CostEstimate(flops=cost[0], bytes_accessed=cost[1], transcendentals=0),
    )(*operands)


def transform_tables(split, cycle):
    half = cycle // split
    step = np.arange(split)[:, None] * np.arange(half)[None, :] % cycle
    angle = step * (2.0 * math.pi / cycle)
    twiddle = np.stack([np.cos(angle), np.sin(angle)]).astype(np.float32)
    step = np.arange(half)[:, None] * np.arange(half)[None, :] % half
    angle = (step * (2.0 * math.pi / half)).reshape(half, half // LANES, LANES)
    table = np.transpose(np.concatenate([np.cos(angle), np.sin(angle)], axis=2), (1, 0, 2))
    return twiddle, table.astype(ml_dtypes.bfloat16)


def local(sky_map, pixel_mask, noise_factor, cycle_legendre, band_power, channel_cov, test_matrix):
    cycles, pixels, chans = sky_map.shape
    modes, _ = band_power.shape
    offsets = cycle_legendre.shape[2]
    columns = test_matrix.shape[3]
    mode_count = lax.axis_size("mode")
    half = mode_count // 2
    devices = lax.axis_size("high") * 2 * mode_count
    width = chans // mode_count
    group = max(1, SUBLANES // width)
    split = pixels // LANES
    rows = split * cycles * width
    legs = cycles * offsets * (modes // LANES)
    tiles = mode_count
    blocks = modes * mode_count // (tiles * LANES)
    everyone = ("high", "low", "mode")
    hbm, vmem, bf16, f32, shape = pl.ANY, pltpu.VMEM, jnp.bfloat16, jnp.float32, jax.ShapeDtypeStruct
    twiddle, table = transform_tables(split, pixels * mode_count)

    low, mode = lax.axis_index("low"), lax.axis_index("mode")
    place = jnp.stack([mode % 2 * half + mode // 2, mode // 2, low, mode % 2]).astype(jnp.int32)
    order = sorted(range(mode_count), key=lambda n: -(n % half).bit_count())

    def target(i, n):
        i_low, i_mode = i // mode_count, i % mode_count
        return (i_mode % 2 ^ n // half) * mode_count + (i_mode // 2 ^ n % half) * 2 + i_low

    messages = call(
        functools.partial(whiten_kernel, order),
        [shape((rows + legs, LANES), bf16)] * mode_count,
        [
            vmem((cycles, chans, pixels), bf16),
            vmem((cycles, pixels), jnp.int32),
            vmem((cycles, chans, chans), f32),
            vmem((cycles, offsets, modes), f32),
            vmem((pixels, pixels), bf16),
            vmem((cycles * chans, pixels), bf16),
            vmem((mode_count, rows + legs, LANES), bf16),
            pltpu.SemaphoreType.DMA((4 + mode_count,)),
        ],
        56,
        [pltpu.SMEM] + [hbm] * 4,
        place,
        jnp.transpose(sky_map, (0, 2, 1)),
        pixel_mask,
        noise_factor[:, 0],
        jnp.transpose(cycle_legendre, (0, 2, 1)),
        out_space=hbm,
        cost=(2 * cycles * chans * pixels * (pixels + 4 * chans), 8 * MIB),
    )
    slots = [
        lax.ppermute(message, ("low", "mode"), [(i, target(i, n)) for i in range(2 * mode_count)])
        for message, n in zip(messages, order)
    ]

    keep, give = call(
        functools.partial(modes_kernel, order, cycles, width, offsets),
        [shape((offsets, mode_count, width, modes), bf16)] * 2,
        [
            vmem((tiles, tiles * LANES, 2 * LANES), bf16),
            vmem((rows, tiles * LANES), bf16),
            vmem((cycles * offsets, mode_count * modes), f32),
            vmem((rows, 2 * LANES), f32),
            vmem((rows, 2 * LANES), f32),
            vmem((blocks, 2, cycles // group, group * width, LANES), f32),
            vmem((2, offsets, mode_count, width, modes), bf16),
            pltpu.SemaphoreType.DMA((tiles,)),
            pltpu.SemaphoreType.DMA((tiles // 2, 2 * blocks, 2)),
        ],
        40,
        [pltpu.SMEM, vmem, hbm] + [vmem] * mode_count,
        place,
        jnp.asarray(twiddle),
        jnp.asarray(table),
        *slots,
        out_space=hbm,
        cost=(4 * rows * (tiles * LANES) ** 2, 8 * MIB),
    )
    other = lax.ppermute(give, "mode", [(i, i ^ 1) for i in range(mode_count)])
    alm = call(pair_kernel, shape(keep.shape, bf16), [], 16, [vmem] * 2, keep, other)
    alm = alm.reshape(devices, width, modes)
    alm = lax.all_to_all(alm, everyone, 0, 0, tiled=True)
    alm = alm.reshape(devices // (2 * mode_count), 2 * mode_count, width, modes)

    share = columns // (devices)
    fold = LANES // chans
    packed = share % (8 * fold) == 0
    part = call(
        sketch_kernel,
        shape((devices, share // fold, LANES) if packed else (columns, chans), f32),
        [vmem((2, chans, modes), f32)],
        24,
        [vmem] * 4,
        alm,
        jnp.transpose(band_power),
        channel_cov,
        jnp.transpose(test_matrix[0], (1, 0, 2)),
    )
    if not packed:
        part = part.reshape(devices, share, chans)
    part = lax.all_to_all(part, everyone, 0, 0, tiled=True)
    return jnp.transpose(call(total_kernel, shape((share, chans), f32), [], 16, [vmem], part))


def solution(mesh):
    patches, modes = mesh.shape["patch"], mesh.shape["mode"]
    mesh = jax.sharding.Mesh(mesh.devices.reshape(patches // 2, 2, modes), ("high", "low", "mode"))
    patch = ("high", "low")
    return jax.shard_map(
        local,
        mesh=mesh,
        in_specs=(
            P(patch, "mode", None),
            P(patch, "mode"),
            P(patch, "mode", None, None),
            P(patch, "mode", None),
            P("mode", patch),
            P(),
            P(patch, "mode", None, None),
        ),
        out_specs=P(None, (*patch, "mode")),
        check_vma=False,
    )
```

```python
import functools
import math

import jax
import jax.numpy as jnp
import ml_dtypes
import numpy as np
from jax import lax
from jax.experimental import pallas as pl
from jax.experimental.pallas import tpu as pltpu
from jax.sharding import PartitionSpec as P

LANES = 128
MIB = 1 << 20
SUBLANES = 8


def rotate(value, step, points):
    re, im = value
    step %= points
    if step == 0:
        return re, im
    if 2 * step == points:
        return -re, -im
    if 4 * step == points:
        return im, -re
    if 8 * step == points:
        return (re + im) * math.sqrt(0.5), (im - re) * math.sqrt(0.5)
    if 8 * step == 3 * points:
        return (im - re) * math.sqrt(0.5), (re + im) * -math.sqrt(0.5)
    c, s = math.cos(2 * math.pi * step / points), math.sin(2 * math.pi * step / points)
    return re * c + im * s, im * c - re * s


def dft(values):
    n = len(values)
    if n == 1:
        return values
    half = n // 2
    even, odd = dft(values[0::2]), dft(values[1::2])
    out = [None] * n
    for b in range(half):
        re, im = rotate(odd[b], b, n)
        out[b] = even[b][0] + re, even[b][1] + im
        out[b + half] = even[b][0] - re, even[b][1] - im
    return out


def whiten_kernel(fold, sky_hbm, mask_hbm, factor_hbm, leg_hbm, out_hbm, *refs):
    sky, mask, factor, leg, sort, white, stage, sems = refs
    cycles, chans, pixels = sky.shape
    groups = stage.shape[0]
    width = chans // groups
    group = max(1, SUBLANES // width)
    tall = group * width
    split = pixels // LANES
    sources, targets = (factor_hbm, sky_hbm, mask_hbm, leg_hbm), (factor, sky, mask, leg)
    copies = [pltpu.make_async_copy(a, b, sems.at[n]) for n, (a, b) in enumerate(zip(sources, targets))]
    for copy in copies:
        copy.start()
    shape = (2 * LANES, LANES)
    ahead = lax.broadcasted_iota(jnp.int32, shape, 0) - split * lax.broadcasted_iota(jnp.int32, shape, 1)
    for first in range(0, pixels, 2 * LANES):
        for s in range(split):
            block = jnp.where(ahead == s - first, 1.0, 0.0).astype(jnp.bfloat16)
            sort[first : first + 2 * LANES, s * LANES : (s + 1) * LANES] = block
    copies[0].wait()
    row_of = lax.broadcasted_iota(jnp.int32, (tall, group * chans), 0) // width
    lane_of = lax.broadcasted_iota(jnp.int32, (tall, group * chans), 1) // chans
    lefts = []
    for pack in range(cycles // group):
        rows = []
        for e in range(groups):
            tile = [factor[pack * group + g, e * width : (e + 1) * width, :] for g in range(group)]
            tile = jnp.concatenate(tile, axis=0)
            rows.append(jnp.where(row_of == lane_of, jnp.concatenate([tile] * group, axis=1), 0.0))
        rows = jnp.concatenate(rows, axis=0)
        high = rows.astype(jnp.bfloat16)
        low = (rows - high.astype(jnp.float32)).astype(jnp.bfloat16)
        lefts.append(jnp.concatenate([high, low], axis=1))
    for copy in copies[1:3]:
        copy.wait()
    cycle_of = lax.broadcasted_iota(jnp.int32, (tall, pixels), 0) // width
    for pack in range(cycles // group):
        data = jnp.concatenate([sky[pack * group + g] for g in range(group)] * 2, axis=0)
        value = jnp.dot(lefts[pack], data, preferred_element_type=jnp.float32)
        keep = jnp.broadcast_to(mask[pack * group : pack * group + 1, :], (tall, pixels))
        for g in range(1, group):
            keep = jnp.where(cycle_of < g, keep, mask[pack * group + g : pack * group + g + 1, :])
        keep = keep.astype(jnp.float32)
        for e in range(groups):
            place = (e * (cycles // group) + pack) * tall
            white[place : place + tall, :] = (value[e * tall : (e + 1) * tall] * keep).astype(jnp.bfloat16)
    copies[3].wait()
    count = cycles * width
    rows = jnp.concatenate([leg[r] for r in range(cycles)], axis=0).astype(jnp.bfloat16)
    high = rows.shape[0]
    if fold > 1:
        shape = (fold * LANES, LANES)
        ahead = lax.broadcasted_iota(jnp.int32, shape, 0) - fold * lax.broadcasted_iota(jnp.int32, shape, 1)
        places = [jnp.where(ahead == n, 1.0, 0.0).astype(jnp.bfloat16) for n in range(fold)]
        places = jnp.concatenate(places, axis=1)
        rows = [
            jnp.dot(rows[:, n : n + fold * LANES], places, preferred_element_type=jnp.float32)
            for n in range(0, rows.shape[1], fold * LANES)
        ]
        rows = jnp.concatenate(rows, axis=1).astype(jnp.bfloat16)
    for n in range(rows.shape[1] // LANES):
        for e in range(groups):
            place = split * count + n * high
            stage[e, place : place + high, :] = rows[:, n * LANES : (n + 1) * LANES]
    sends = []

    def send(first, last):
        where = (slice(None), slice(first, last))
        sends.append(pltpu.make_async_copy(stage.at[where], out_hbm.at[where], sems.at[4 + len(sends)]))
        sends[-1].start()

    send(split * count, stage.shape[1])
    for pair in range(split // 2):
        wide = slice(pair * 2 * LANES, (pair + 1) * 2 * LANES)
        value = jnp.dot(white[...], sort[:, wide], preferred_element_type=jnp.float32).astype(jnp.bfloat16)
        for side in range(2):
            s = pair * 2 + side
            for e in range(groups):
                stage[e, s * count : (s + 1) * count, :] = value[
                    e * count : (e + 1) * count, side * LANES : (side + 1) * LANES
                ]
        send(pair * 2 * count, (pair + 1) * 2 * count)
    for send in sends:
        send.wait()


def modes_kernel(width, offsets, twiddle_ref, table_hbm, z_ref, out_hbm, *refs):
    table, left, leg, prod_a, prod_b, x_ref, out_ref, table_sems, out_sems = refs
    tiles = table.shape[0]
    split = twiddle_ref.shape[1]
    tall = x_ref.shape[3]
    group = tall // width
    modes = out_ref.shape[3]
    sources = out_ref.shape[1]
    parts = z_ref.shape[0] // sources
    cycles = leg.shape[0] // offsets
    blocks = sources * modes // (tiles * LANES)
    per = modes // LANES
    count = cycles // parts * width
    high = cycles // parts * offsets

    def copy(tile):
        return pltpu.make_async_copy(table_hbm.at[tile], table.at[tile], table_sems.at[tile])

    def store(step, n):
        mode_tile = n // 2 * tiles + 2 * step + n % 2
        lanes = pl.ds(pl.multiple_of(mode_tile % per * LANES, LANES), LANES)
        where = (slice(None), mode_tile // per, slice(None), lanes)
        return pltpu.make_async_copy(out_ref.at[where], out_hbm.at[where], out_sems.at[step, n])

    copy(0).start()
    copy(1).start()
    fold = left.shape[0]
    for p in range(parts):
        for q in range(sources // fold):
            lanes = slice(q * LANES, (q + 1) * LANES)
            for n in range(split):
                place = (n * parts + p) * count
                rows = z_ref[p * sources + q, n * count : (n + 1) * count, :]
                if fold == 1:
                    left[0, place : place + count, lanes] = rows
                else:
                    rows = rows.astype(jnp.float32)
                    more = z_ref[p * sources + sources // 2 + q, n * count : (n + 1) * count, :].astype(jnp.float32)
                    left[0, place : place + count, lanes] = (rows + more).astype(jnp.bfloat16)
                    left[1, place : place + count, lanes] = (rows - more).astype(jnp.bfloat16)
    for tile in range(2, tiles):
        copy(tile).start()

    def product(tile, prod, kind):
        prod[...] = jnp.dot(left[kind % fold], table[tile], preferred_element_type=jnp.float32)

    copy(0).wait()
    product(0, prod_a, 0)
    for p in range(parts):
        for q in range(sources):
            for n in range(per):
                place = split * count + n * high
                rows = z_ref[p * sources + q, place : place + high, :].astype(jnp.float32)
                leg[p * high : (p + 1) * high, (q * per + n) * LANES : (q * per + n + 1) * LANES] = rows

    def use(tile, prod):
        lanes = pl.ds(pl.multiple_of(tile * LANES, LANES), LANES)
        cosine, sine = twiddle_ref[0, :, lanes], twiddle_ref[1, :, lanes]
        cycle_of = lax.broadcasted_iota(jnp.int32, (tall, LANES), 0) // width
        for pack in range(cycles // group):
            values = []
            for s in range(split):
                place = (s * cycles + pack * group) * width
                re = prod[place : place + tall, :LANES]
                im = prod[place : place + tall, LANES:]
                if s == 0:
                    values.append((re, -im))
                else:
                    c, d = cosine[s : s + 1, :], sine[s : s + 1, :]
                    values.append((re * c - im * d, -(re * d) - im * c))
            parts = dft(values)
            for b in range(blocks):
                x_ref[b, 0, pack] = parts[b][0]
                x_ref[b, 1, pack] = parts[b][1]
        for b in range(blocks):
            mode_tile = b * tiles + tile
            d, n = mode_tile // per, mode_tile % per
            mode = pl.ds(pl.multiple_of(mode_tile * LANES, LANES), LANES)
            for k in range(offsets):
                total = [None, None]
                for pack in range(cycles // group):
                    row = None
                    for g in range(group):
                        r = pack * group + g
                        next_row = leg[r * offsets + k : r * offsets + k + 1, mode]
                        if g == 0:
                            row = jnp.broadcast_to(next_row, (tall, LANES))
                        else:
                            row = jnp.where(cycle_of < g, row, next_row)
                    for t in range(2):
                        term = row * x_ref[b, t, pack]
                        total[t] = term if pack == 0 else total[t] + term
                step = tall // 2
                while step >= width:
                    total = [value + pltpu.roll(value, step, 0) for value in total]
                    step //= 2
                if group == 1:
                    both = jnp.concatenate(total, axis=0)
                else:
                    both = jnp.where(cycle_of < 1, total[0], total[1])[: 2 * width]
                place = pl.ds(pl.multiple_of(n * LANES, LANES), LANES)
                out_ref[k, d, :, place] = both.astype(jnp.bfloat16)

    @pl.loop(0, tiles // 2)
    def _(step):
        copy(2 * step + 1).wait()

        @pl.when(2 * step + 2 < tiles)
        def _():
            copy(2 * step + 2).wait()

        product(2 * step + 1, prod_b, 1)
        use(2 * step, prod_a)
        product(jnp.minimum(2 * step + 2, tiles - 2), prod_a, 0)
        use(2 * step + 1, prod_b)
        for n in range(2 * blocks):
            store(step, n).start()

    @pl.loop(0, tiles // 2)
    def _(step):
        for n in range(2 * blocks):
            store(step, n).wait()


def sketch_kernel(alm_ref, band_ref, cov_ref, test_ref, out_ref, left_ref):
    patches, groups, rows, lanes = alm_ref.shape
    chans = cov_ref.shape[0]
    width = rows // 2
    for g in range(groups):
        part = alm_ref[0, g].astype(jnp.float32)
        for p in range(1, patches):
            part += alm_ref[p, g].astype(jnp.float32)
        part = part * band_ref[...]
        for t in range(2):
            left_ref[t, g * width : (g + 1) * width, :] = part[t * width : (t + 1) * width]
    sketch = None
    for t in range(2):
        term = lax.dot_general(
            test_ref[t],
            left_ref[t].astype(jnp.bfloat16),
            (((0,), (1,)), ((), ())),
            preferred_element_type=jnp.float32,
        )
        sketch = term if t == 0 else sketch + term
    mixed = lax.dot_general(
        sketch,
        cov_ref[...],
        (((1,), (1,)), ((), ())),
        precision=lax.Precision.HIGHEST,
        preferred_element_type=jnp.float32,
    )
    if out_ref.ndim == 2:
        out_ref[...] = mixed
    else:
        owners, block, _ = out_ref.shape
        fold = out_ref.shape[2] // chans
        mixed = mixed.reshape(owners, fold, block, chans)
        out_ref[...] = jnp.concatenate([mixed[:, n] for n in range(fold)], axis=-1)


def total_kernel(part_ref, out_ref):
    block, chans = part_ref.shape[1], out_ref.shape[1]
    total = jnp.sum(part_ref[...], axis=0)
    for n in range(part_ref.shape[2] // chans):
        out_ref[n * block : (n + 1) * block, :] = total[:, n * chans : (n + 1) * chans]


def call(kernel, shape, scratch, mib, spaces, *operands, out_space=pltpu.VMEM, cost=(0, 0)):
    return pl.pallas_call(
        kernel,
        out_shape=shape,
        in_specs=[pl.BlockSpec(memory_space=space) for space in spaces],
        out_specs=jax.tree.map(lambda _: pl.BlockSpec(memory_space=out_space), shape),
        scratch_shapes=scratch,
        compiler_params=pltpu.CompilerParams(vmem_limit_bytes=mib * MIB),
        cost_estimate=pl.CostEstimate(flops=cost[0], bytes_accessed=cost[1], transcendentals=0),
    )(*operands)


def in_order(modes, fold):
    return np.arange(modes).reshape(-1, LANES, fold).swapaxes(1, 2).reshape(-1)


def transform_tables(split, cycle, fold):
    half = cycle // split
    modes = in_order(half, fold)
    step = np.arange(split)[:, None] * modes[None, :] % cycle
    angle = step * (2.0 * math.pi / cycle)
    twiddle = np.stack([np.cos(angle), np.sin(angle)]).astype(np.float32)
    step = np.arange(half // fold)[:, None] * modes[None, :] % half
    angle = (step * (2.0 * math.pi / half)).reshape(half // fold, half // LANES, LANES)
    table = np.transpose(np.concatenate([np.cos(angle), np.sin(angle)], axis=2), (1, 0, 2))
    return twiddle, table.astype(ml_dtypes.bfloat16)


def local(sky_map, pixel_mask, noise_factor, cycle_legendre, band_power, channel_cov, test_matrix):
    cycles, pixels, chans = sky_map.shape
    modes, _ = band_power.shape
    offsets = cycle_legendre.shape[2]
    columns = test_matrix.shape[3]
    mode_count, pair = lax.axis_size("mode"), lax.axis_size("low")
    groups = pair * mode_count
    devices = lax.axis_size("high") * groups
    width = chans // groups
    group = max(1, SUBLANES // width)
    split = pixels // LANES
    rows = split * cycles * width
    legs = cycles * offsets * (modes // LANES)
    tiles = mode_count
    blocks = modes * mode_count // (tiles * LANES)
    everyone = ("high", "low", "mode")
    hbm, vmem, bf16, f32, shape = pl.ANY, pltpu.VMEM, jnp.bfloat16, jnp.float32, jax.ShapeDtypeStruct
    fold = 2 if modes % (2 * LANES) == 0 else 1
    twiddle, table = transform_tables(split, pixels * mode_count, fold)

    message = call(
        functools.partial(whiten_kernel, fold),
        shape((groups, rows + legs, LANES), bf16),
        [
            vmem((cycles, chans, pixels), bf16),
            vmem((cycles, pixels), jnp.int32),
            vmem((cycles, chans, chans), f32),
            vmem((cycles, offsets, modes), f32),
            vmem((pixels, pixels), bf16),
            vmem((cycles * chans, pixels), bf16),
            vmem((groups, rows + legs, LANES), bf16),
            pltpu.SemaphoreType.DMA((5 + split // 2,)),
        ],
        56,
        [hbm] * 4,
        jnp.transpose(sky_map, (0, 2, 1)),
        pixel_mask,
        noise_factor[:, 0],
        jnp.transpose(cycle_legendre, (0, 2, 1)),
        out_space=hbm,
        cost=(2 * cycles * chans * pixels * (pixels + 4 * chans), 8 * MIB),
    )
    message = lax.all_to_all(message, ("low", "mode"), 0, 0, tiled=True)

    alm = call(
        functools.partial(modes_kernel, width, offsets),
        shape((offsets, mode_count, 2 * width, modes), bf16),
        [
            vmem((tiles, tiles * LANES // fold, 2 * LANES), bf16),
            vmem((fold, pair * rows, tiles * LANES // fold), bf16),
            vmem((pair * cycles * offsets, mode_count * modes), f32),
            vmem((pair * rows, 2 * LANES), f32),
            vmem((pair * rows, 2 * LANES), f32),
            vmem((blocks, 2, pair * cycles // group, group * width, LANES), f32),
            vmem((offsets, mode_count, 2 * width, modes), bf16),
            pltpu.SemaphoreType.DMA((tiles,)),
            pltpu.SemaphoreType.DMA((tiles // 2, 2 * blocks)),
        ],
        40,
        [vmem, hbm, vmem],
        jnp.asarray(twiddle),
        jnp.asarray(table),
        message,
        out_space=hbm,
        cost=(4 * pair * rows * (tiles * LANES) ** 2 // fold, 8 * MIB),
    )
    alm = alm.reshape(devices, 2 * width, modes)
    alm = lax.all_to_all(alm, everyone, 0, 0, tiled=True)
    alm = alm.reshape(devices // groups, groups, 2 * width, modes)

    right = test_matrix.reshape(modes // (fold * LANES), LANES, fold, 2, columns)
    right = jnp.transpose(right, (3, 0, 2, 1, 4)).reshape(2, modes, columns)
    band = jnp.swapaxes(band_power.reshape(-1, LANES, fold), 1, 2).reshape(1, modes)
    share = columns // (devices)
    fold = LANES // chans
    packed = share % (8 * fold) == 0
    part = call(
        sketch_kernel,
        shape((devices, share // fold, LANES) if packed else (columns, chans), f32),
        [vmem((2, chans, modes), f32)],
        24,
        [vmem] * 4,
        alm,
        band,
        channel_cov,
        right,
    )
    if not packed:
        part = part.reshape(devices, share, chans)
    part = lax.all_to_all(part, everyone, 0, 0, tiled=True)
    return jnp.transpose(call(total_kernel, shape((share, chans), f32), [], 16, [vmem], part))


def solution(mesh):
    patches, modes = mesh.shape["patch"], mesh.shape["mode"]
    mesh = jax.sharding.Mesh(mesh.devices.reshape(patches // 2, 2, modes), ("high", "low", "mode"))
    patch = ("high", "low")
    return jax.shard_map(
        local,
        mesh=mesh,
        in_specs=(
            P(patch, "mode", None),
            P(patch, "mode"),
            P(patch, "mode", None, None),
            P(patch, "mode", None),
            P("mode", patch),
            P(),
            P(patch, "mode", None, None),
        ),
        out_specs=P(None, (*patch, "mode")),
        check_vma=False,
    )
```

```python
import functools
import math

import jax
import jax.numpy as jnp
import ml_dtypes
import numpy as np
from jax import lax
from jax.experimental import pallas as pl
from jax.experimental.pallas import tpu as pltpu
from jax.sharding import PartitionSpec as P

LANES = 128
MIB = 1 << 20
SUBLANES = 8


def rotate(value, step, points):
    re, im = value
    step %= points
    if step == 0:
        return re, im
    if 2 * step == points:
        return -re, -im
    if 4 * step == points:
        return im, -re
    if 8 * step == points:
        return (re + im) * math.sqrt(0.5), (im - re) * math.sqrt(0.5)
    if 8 * step == 3 * points:
        return (im - re) * math.sqrt(0.5), (re + im) * -math.sqrt(0.5)
    c, s = math.cos(2 * math.pi * step / points), math.sin(2 * math.pi * step / points)
    return re * c + im * s, im * c - re * s


def dft(values):
    n = len(values)
    if n == 1:
        return values
    half = n // 2
    even, odd = dft(values[0::2]), dft(values[1::2])
    out = [None] * n
    for b in range(half):
        re, im = rotate(odd[b], b, n)
        out[b] = even[b][0] + re, even[b][1] + im
        out[b + half] = even[b][0] - re, even[b][1] - im
    return out


def whiten_kernel(fold, sky_hbm, mask_hbm, factor_hbm, leg_hbm, out_hbm, *refs):
    sky, mask, factor, leg, sort, white, stage, sems = refs
    cycles, chans, pixels = sky.shape
    groups = stage.shape[0]
    width = chans // groups
    group = max(1, SUBLANES // width)
    tall = group * width
    split = pixels // LANES
    sources, targets = (factor_hbm, sky_hbm, mask_hbm, leg_hbm), (factor, sky, mask, leg)
    copies = [pltpu.make_async_copy(a, b, sems.at[n]) for n, (a, b) in enumerate(zip(sources, targets))]
    for copy in copies:
        copy.start()
    shape = (2 * LANES, LANES)
    ahead = lax.broadcasted_iota(jnp.int32, shape, 0) - split * lax.broadcasted_iota(jnp.int32, shape, 1)
    for first in range(0, pixels, 2 * LANES):
        for s in range(split):
            block = jnp.where(ahead == s - first, 1.0, 0.0).astype(jnp.bfloat16)
            sort[first : first + 2 * LANES, s * LANES : (s + 1) * LANES] = block
    copies[0].wait()
    row_of = lax.broadcasted_iota(jnp.int32, (tall, group * chans), 0) // width
    lane_of = lax.broadcasted_iota(jnp.int32, (tall, group * chans), 1) // chans
    lefts = []
    for pack in range(cycles // group):
        rows = []
        for e in range(groups):
            tile = [factor[pack * group + g, e * width : (e + 1) * width, :] for g in range(group)]
            tile = jnp.concatenate(tile, axis=0)
            rows.append(jnp.where(row_of == lane_of, jnp.concatenate([tile] * group, axis=1), 0.0))
        rows = jnp.concatenate(rows, axis=0)
        high = rows.astype(jnp.bfloat16)
        low = (rows - high.astype(jnp.float32)).astype(jnp.bfloat16)
        lefts.append(jnp.concatenate([high, low], axis=1))
    for copy in copies[1:3]:
        copy.wait()
    cycle_of = lax.broadcasted_iota(jnp.int32, (tall, pixels), 0) // width
    for pack in range(cycles // group):
        data = jnp.concatenate([sky[pack * group + g] for g in range(group)] * 2, axis=0)
        value = jnp.dot(lefts[pack], data, preferred_element_type=jnp.float32)
        keep = jnp.broadcast_to(mask[pack * group : pack * group + 1, :], (tall, pixels))
        for g in range(1, group):
            keep = jnp.where(cycle_of < g, keep, mask[pack * group + g : pack * group + g + 1, :])
        keep = keep.astype(jnp.float32)
        for e in range(groups):
            place = (e * (cycles // group) + pack) * tall
            white[place : place + tall, :] = (value[e * tall : (e + 1) * tall] * keep).astype(jnp.bfloat16)
    copies[3].wait()
    count = cycles * width
    rows = jnp.concatenate([leg[r] for r in range(cycles)], axis=0).astype(jnp.bfloat16)
    high = rows.shape[0]
    if fold > 1:
        shape = (fold * LANES, LANES)
        ahead = lax.broadcasted_iota(jnp.int32, shape, 0) - fold * lax.broadcasted_iota(jnp.int32, shape, 1)
        places = [jnp.where(ahead == n, 1.0, 0.0).astype(jnp.bfloat16) for n in range(fold)]
        places = jnp.concatenate(places, axis=1)
        rows = [
            jnp.dot(rows[:, n : n + fold * LANES], places, preferred_element_type=jnp.float32)
            for n in range(0, rows.shape[1], fold * LANES)
        ]
        rows = jnp.concatenate(rows, axis=1).astype(jnp.bfloat16)
    for n in range(rows.shape[1] // LANES):
        for e in range(groups):
            place = split * count + n * high
            stage[e, place : place + high, :] = rows[:, n * LANES : (n + 1) * LANES]
    sends = []

    def send(first, last):
        where = (slice(None), slice(first, last))
        sends.append(pltpu.make_async_copy(stage.at[where], out_hbm.at[where], sems.at[4 + len(sends)]))
        sends[-1].start()

    send(split * count, stage.shape[1])
    for pair in range(split // 2):
        wide = slice(pair * 2 * LANES, (pair + 1) * 2 * LANES)
        value = jnp.dot(white[...], sort[:, wide], preferred_element_type=jnp.float32).astype(jnp.bfloat16)
        for side in range(2):
            s = pair * 2 + side
            for e in range(groups):
                stage[e, s * count : (s + 1) * count, :] = value[
                    e * count : (e + 1) * count, side * LANES : (side + 1) * LANES
                ]
        send(pair * 2 * count, (pair + 1) * 2 * count)
    for send in sends:
        send.wait()


def modes_kernel(width, offsets, twiddle_ref, table, z_ref, out_hbm, *refs):
    left, leg, prod_a, prod_b, x_ref, out_ref, out_sems = refs
    tiles = table.shape[0]
    split = twiddle_ref.shape[1]
    tall = x_ref.shape[3]
    group = tall // width
    modes = out_ref.shape[3]
    sources = out_ref.shape[1]
    parts = z_ref.shape[0] // sources
    cycles = leg.shape[0] // offsets
    blocks = sources * modes // (tiles * LANES)
    per = modes // LANES
    count = cycles // parts * width
    high = cycles // parts * offsets

    def store(step, n):
        mode_tile = n // 2 * tiles + 2 * step + n % 2
        lanes = pl.ds(pl.multiple_of(mode_tile % per * LANES, LANES), LANES)
        where = (slice(None), mode_tile // per, slice(None), lanes)
        return pltpu.make_async_copy(out_ref.at[where], out_hbm.at[where], out_sems.at[step, n])

    fold = left.shape[0]
    for p in range(parts):
        for q in range(sources // fold):
            lanes = slice(q * LANES, (q + 1) * LANES)
            for n in range(split):
                place = (n * parts + p) * count
                rows = z_ref[p * sources + q, n * count : (n + 1) * count, :]
                if fold == 1:
                    left[0, place : place + count, lanes] = rows
                else:
                    rows = rows.astype(jnp.float32)
                    more = z_ref[p * sources + sources // 2 + q, n * count : (n + 1) * count, :].astype(jnp.float32)
                    left[0, place : place + count, lanes] = (rows + more).astype(jnp.bfloat16)
                    left[1, place : place + count, lanes] = (rows - more).astype(jnp.bfloat16)

    def product(tile, prod, kind):
        prod[...] = jnp.dot(left[kind % fold], table[tile], preferred_element_type=jnp.float32)

    product(0, prod_a, 0)
    for p in range(parts):
        for q in range(sources):
            for n in range(per):
                place = split * count + n * high
                rows = z_ref[p * sources + q, place : place + high, :].astype(jnp.float32)
                leg[p * high : (p + 1) * high, (q * per + n) * LANES : (q * per + n + 1) * LANES] = rows

    def use(tile, prod):
        lanes = pl.ds(pl.multiple_of(tile * LANES, LANES), LANES)
        cosine, sine = twiddle_ref[0, :, lanes], twiddle_ref[1, :, lanes]
        cycle_of = lax.broadcasted_iota(jnp.int32, (tall, LANES), 0) // width
        for pack in range(cycles // group):
            values = []
            for s in range(split):
                place = (s * cycles + pack * group) * width
                re = prod[place : place + tall, :LANES]
                im = prod[place : place + tall, LANES:]
                if s == 0:
                    values.append((re, -im))
                else:
                    c, d = cosine[s : s + 1, :], sine[s : s + 1, :]
                    values.append((re * c - im * d, -(re * d) - im * c))
            parts = dft(values)
            for b in range(blocks):
                x_ref[b, 0, pack] = parts[b][0]
                x_ref[b, 1, pack] = parts[b][1]
        for b in range(blocks):
            mode_tile = b * tiles + tile
            d, n = mode_tile // per, mode_tile % per
            mode = pl.ds(pl.multiple_of(mode_tile * LANES, LANES), LANES)
            for k in range(offsets):
                total = [None, None]
                for pack in range(cycles // group):
                    row = None
                    for g in range(group):
                        r = pack * group + g
                        next_row = leg[r * offsets + k : r * offsets + k + 1, mode]
                        if g == 0:
                            row = jnp.broadcast_to(next_row, (tall, LANES))
                        else:
                            row = jnp.where(cycle_of < g, row, next_row)
                    for t in range(2):
                        term = row * x_ref[b, t, pack]
                        total[t] = term if pack == 0 else total[t] + term
                step = tall // 2
                while step >= width:
                    total = [value + pltpu.roll(value, step, 0) for value in total]
                    step //= 2
                if group == 1:
                    both = jnp.concatenate(total, axis=0)
                else:
                    both = jnp.where(cycle_of < 1, total[0], total[1])[: 2 * width]
                place = pl.ds(pl.multiple_of(n * LANES, LANES), LANES)
                out_ref[k, d, :, place] = both.astype(jnp.bfloat16)

    @pl.loop(0, tiles // 2)
    def _(step):
        product(2 * step + 1, prod_b, 1)
        use(2 * step, prod_a)
        product(jnp.minimum(2 * step + 2, tiles - 2), prod_a, 0)
        use(2 * step + 1, prod_b)
        for n in range(2 * blocks):
            store(step, n).start()

    @pl.loop(0, tiles // 2)
    def _(step):
        for n in range(2 * blocks):
            store(step, n).wait()


def sketch_kernel(alm_ref, band_ref, cov_ref, test_ref, out_ref, left_ref):
    patches, groups, rows, lanes = alm_ref.shape
    chans = cov_ref.shape[0]
    width = rows // 2
    for g in range(groups):
        part = alm_ref[0, g].astype(jnp.float32)
        for p in range(1, patches):
            part += alm_ref[p, g].astype(jnp.float32)
        part = part * band_ref[...]
        for t in range(2):
            left_ref[t, g * width : (g + 1) * width, :] = part[t * width : (t + 1) * width]
    sketch = None
    for t in range(2):
        term = lax.dot_general(
            test_ref[t],
            left_ref[t].astype(jnp.bfloat16),
            (((0,), (1,)), ((), ())),
            preferred_element_type=jnp.float32,
        )
        sketch = term if t == 0 else sketch + term
    mixed = lax.dot_general(
        sketch,
        cov_ref[...],
        (((1,), (1,)), ((), ())),
        precision=lax.Precision.HIGHEST,
        preferred_element_type=jnp.float32,
    )
    if out_ref.ndim == 2:
        out_ref[...] = mixed
    else:
        owners, block, _ = out_ref.shape
        fold = out_ref.shape[2] // chans
        mixed = mixed.reshape(owners, fold, block, chans)
        out_ref[...] = jnp.concatenate([mixed[:, n] for n in range(fold)], axis=-1)


def total_kernel(part_ref, out_ref):
    block, chans = part_ref.shape[1], out_ref.shape[1]
    total = jnp.sum(part_ref[...], axis=0)
    for n in range(part_ref.shape[2] // chans):
        out_ref[n * block : (n + 1) * block, :] = total[:, n * chans : (n + 1) * chans]


def call(kernel, shape, scratch, mib, spaces, *operands, out_space=pltpu.VMEM, cost=(0, 0)):
    return pl.pallas_call(
        kernel,
        out_shape=shape,
        in_specs=[pl.BlockSpec(memory_space=space) for space in spaces],
        out_specs=jax.tree.map(lambda _: pl.BlockSpec(memory_space=out_space), shape),
        scratch_shapes=scratch,
        compiler_params=pltpu.CompilerParams(vmem_limit_bytes=mib * MIB),
        cost_estimate=pl.CostEstimate(flops=cost[0], bytes_accessed=cost[1], transcendentals=0),
    )(*operands)


def in_order(modes, fold):
    return np.arange(modes).reshape(-1, LANES, fold).swapaxes(1, 2).reshape(-1)


def transform_tables(split, cycle, fold):
    half = cycle // split
    modes = in_order(half, fold)
    step = np.arange(split)[:, None] * modes[None, :] % cycle
    angle = step * (2.0 * math.pi / cycle)
    twiddle = np.stack([np.cos(angle), np.sin(angle)]).astype(np.float32)
    step = np.arange(half // fold)[:, None] * modes[None, :] % half
    angle = (step * (2.0 * math.pi / half)).reshape(half // fold, half // LANES, LANES)
    table = np.transpose(np.concatenate([np.cos(angle), np.sin(angle)], axis=2), (1, 0, 2))
    return twiddle, table.astype(ml_dtypes.bfloat16)


def local(sky_map, pixel_mask, noise_factor, cycle_legendre, band_power, channel_cov, test_matrix):
    cycles, pixels, chans = sky_map.shape
    modes, _ = band_power.shape
    offsets = cycle_legendre.shape[2]
    columns = test_matrix.shape[3]
    mode_count, pair = lax.axis_size("mode"), lax.axis_size("low")
    groups = pair * mode_count
    devices = lax.axis_size("high") * groups
    width = chans // groups
    group = max(1, SUBLANES // width)
    split = pixels // LANES
    rows = split * cycles * width
    legs = cycles * offsets * (modes // LANES)
    tiles = mode_count
    blocks = modes * mode_count // (tiles * LANES)
    everyone = ("high", "low", "mode")
    hbm, vmem, bf16, f32, shape = pl.ANY, pltpu.VMEM, jnp.bfloat16, jnp.float32, jax.ShapeDtypeStruct
    fold = 2 if modes % (2 * LANES) == 0 else 1
    twiddle, table = transform_tables(split, pixels * mode_count, fold)

    message = call(
        functools.partial(whiten_kernel, fold),
        shape((groups, rows + legs, LANES), bf16),
        [
            vmem((cycles, chans, pixels), bf16),
            vmem((cycles, pixels), jnp.int32),
            vmem((cycles, chans, chans), f32),
            vmem((cycles, offsets, modes), f32),
            vmem((pixels, pixels), bf16),
            vmem((cycles * chans, pixels), bf16),
            vmem((groups, rows + legs, LANES), bf16),
            pltpu.SemaphoreType.DMA((5 + split // 2,)),
        ],
        56,
        [hbm] * 4,
        jnp.transpose(sky_map, (0, 2, 1)),
        pixel_mask,
        noise_factor[:, 0],
        jnp.transpose(cycle_legendre, (0, 2, 1)),
        out_space=hbm,
        cost=(2 * cycles * chans * pixels * (pixels + 4 * chans), 8 * MIB),
    )
    message = lax.all_to_all(message, ("low", "mode"), 0, 0, tiled=True)

    alm = call(
        functools.partial(modes_kernel, width, offsets),
        shape((offsets, mode_count, 2 * width, modes), bf16),
        [
            vmem((fold, pair * rows, tiles * LANES // fold), bf16),
            vmem((pair * cycles * offsets, mode_count * modes), f32),
            vmem((pair * rows, 2 * LANES), f32),
            vmem((pair * rows, 2 * LANES), f32),
            vmem((blocks, 2, pair * cycles // group, group * width, LANES), f32),
            vmem((offsets, mode_count, 2 * width, modes), bf16),
            pltpu.SemaphoreType.DMA((tiles // 2, 2 * blocks)),
        ],
        24,
        [vmem] * 3,
        jnp.asarray(twiddle),
        jnp.asarray(table),
        message,
        out_space=hbm,
        cost=(4 * pair * rows * (tiles * LANES) ** 2 // fold, 8 * MIB),
    )
    alm = alm.reshape(devices, 2 * width, modes)
    alm = lax.all_to_all(alm, everyone, 0, 0, tiled=True)
    alm = alm.reshape(devices // groups, groups, 2 * width, modes)

    right = test_matrix.reshape(modes // (fold * LANES), LANES, fold, 2, columns)
    right = jnp.transpose(right, (3, 0, 2, 1, 4)).reshape(2, modes, columns)
    band = jnp.swapaxes(band_power.reshape(-1, LANES, fold), 1, 2).reshape(1, modes)
    share = columns // (devices)
    fold = LANES // chans
    packed = share % (8 * fold) == 0
    part = call(
        sketch_kernel,
        shape((devices, share // fold, LANES) if packed else (columns, chans), f32),
        [vmem((2, chans, modes), f32)],
        24,
        [vmem] * 4,
        alm,
        band,
        channel_cov,
        right,
    )
    if not packed:
        part = part.reshape(devices, share, chans)
    part = lax.all_to_all(part, everyone, 0, 0, tiled=True)
    return jnp.transpose(call(total_kernel, shape((share, chans), f32), [], 16, [vmem], part))


def solution(mesh):
    patches, modes = mesh.shape["patch"], mesh.shape["mode"]
    mesh = jax.sharding.Mesh(mesh.devices.reshape(patches // 2, 2, modes), ("high", "low", "mode"))
    patch = ("high", "low")
    return jax.shard_map(
        local,
        mesh=mesh,
        in_specs=(
            P(patch, "mode", None),
            P(patch, "mode"),
            P(patch, "mode", None, None),
            P(patch, "mode", None),
            P("mode", patch),
            P(),
            P(patch, "mode", None, None),
        ),
        out_specs=P(None, (*patch, "mode")),
        check_vma=False,
    )
```

```python
import functools
import math

import jax
import jax.numpy as jnp
import ml_dtypes
import numpy as np
from jax import lax
from jax.experimental import pallas as pl
from jax.experimental.pallas import tpu as pltpu
from jax.sharding import PartitionSpec as P

LANES = 128
MIB = 1 << 20
SUBLANES = 8


def rotate(value, step, points):
    re, im = value
    step %= points
    if step == 0:
        return re, im
    if 2 * step == points:
        return -re, -im
    if 4 * step == points:
        return im, -re
    if 8 * step == points:
        return (re + im) * math.sqrt(0.5), (im - re) * math.sqrt(0.5)
    if 8 * step == 3 * points:
        return (im - re) * math.sqrt(0.5), (re + im) * -math.sqrt(0.5)
    c, s = math.cos(2 * math.pi * step / points), math.sin(2 * math.pi * step / points)
    return re * c + im * s, im * c - re * s


def dft(values):
    n = len(values)
    if n == 1:
        return values
    half = n // 2
    even, odd = dft(values[0::2]), dft(values[1::2])
    out = [None] * n
    for b in range(half):
        re, im = rotate(odd[b], b, n)
        out[b] = even[b][0] + re, even[b][1] + im
        out[b + half] = even[b][0] - re, even[b][1] - im
    return out


def whiten_kernel(fold, sky_hbm, mask_hbm, factor_hbm, leg_hbm, out_hbm, *refs):
    sky, mask, factor, leg, sort, white, stage, sems = refs
    cycles, chans, pixels = sky.shape
    groups = stage.shape[0]
    width = chans // groups
    group = max(1, SUBLANES // width)
    tall = group * width
    split = pixels // LANES
    sources, targets = (factor_hbm, sky_hbm, mask_hbm, leg_hbm), (factor, sky, mask, leg)
    copies = [pltpu.make_async_copy(a, b, sems.at[n]) for n, (a, b) in enumerate(zip(sources, targets))]
    for copy in copies:
        copy.start()
    shape = (2 * LANES, LANES)
    ahead = lax.broadcasted_iota(jnp.int32, shape, 0) - split * lax.broadcasted_iota(jnp.int32, shape, 1)
    for first in range(0, pixels, 2 * LANES):
        for s in range(split):
            block = jnp.where(ahead == s - first, 1.0, 0.0).astype(jnp.bfloat16)
            sort[first : first + 2 * LANES, s * LANES : (s + 1) * LANES] = block
    copies[0].wait()
    row_of = lax.broadcasted_iota(jnp.int32, (tall, group * chans), 0) // width
    lane_of = lax.broadcasted_iota(jnp.int32, (tall, group * chans), 1) // chans
    lefts = []
    for pack in range(cycles // group):
        rows = []
        for e in range(groups):
            tile = [factor[pack * group + g, e * width : (e + 1) * width, :] for g in range(group)]
            tile = jnp.concatenate(tile, axis=0)
            rows.append(jnp.where(row_of == lane_of, jnp.concatenate([tile] * group, axis=1), 0.0))
        rows = jnp.concatenate(rows, axis=0)
        high = rows.astype(jnp.bfloat16)
        low = (rows - high.astype(jnp.float32)).astype(jnp.bfloat16)
        lefts.append(jnp.concatenate([high, low], axis=1))
    for copy in copies[1:3]:
        copy.wait()
    cycle_of = lax.broadcasted_iota(jnp.int32, (tall, pixels), 0) // width
    for pack in range(cycles // group):
        data = jnp.concatenate([sky[pack * group + g] for g in range(group)] * 2, axis=0)
        value = jnp.dot(lefts[pack], data, preferred_element_type=jnp.float32)
        keep = jnp.broadcast_to(mask[pack * group : pack * group + 1, :], (tall, pixels))
        for g in range(1, group):
            keep = jnp.where(cycle_of < g, keep, mask[pack * group + g : pack * group + g + 1, :])
        keep = keep.astype(jnp.float32)
        for e in range(groups):
            place = (e * (cycles // group) + pack) * tall
            white[place : place + tall, :] = (value[e * tall : (e + 1) * tall] * keep).astype(jnp.bfloat16)
    copies[3].wait()
    count = cycles * width
    rows = jnp.concatenate([leg[r] for r in range(cycles)], axis=0).astype(jnp.bfloat16)
    high = rows.shape[0]
    if fold > 1:
        shape = (fold * LANES, LANES)
        ahead = lax.broadcasted_iota(jnp.int32, shape, 0) - fold * lax.broadcasted_iota(jnp.int32, shape, 1)
        places = [jnp.where(ahead == n, 1.0, 0.0).astype(jnp.bfloat16) for n in range(fold)]
        places = jnp.concatenate(places, axis=1)
        rows = [
            jnp.dot(rows[:, n : n + fold * LANES], places, preferred_element_type=jnp.float32)
            for n in range(0, rows.shape[1], fold * LANES)
        ]
        rows = jnp.concatenate(rows, axis=1).astype(jnp.bfloat16)
    for n in range(rows.shape[1] // LANES):
        for e in range(groups):
            place = split * count + n * high
            stage[e, place : place + high, :] = rows[:, n * LANES : (n + 1) * LANES]
    sends = []

    def send(first, last):
        where = (slice(None), slice(first, last))
        sends.append(pltpu.make_async_copy(stage.at[where], out_hbm.at[where], sems.at[4 + len(sends)]))
        sends[-1].start()

    send(split * count, stage.shape[1])
    for pair in range(split // 2):
        wide = slice(pair * 2 * LANES, (pair + 1) * 2 * LANES)
        value = jnp.dot(white[...], sort[:, wide], preferred_element_type=jnp.float32).astype(jnp.bfloat16)
        for side in range(2):
            s = pair * 2 + side
            for e in range(groups):
                stage[e, s * count : (s + 1) * count, :] = value[
                    e * count : (e + 1) * count, side * LANES : (side + 1) * LANES
                ]
        send(pair * 2 * count, (pair + 1) * 2 * count)
    for send in sends:
        send.wait()


def modes_kernel(width, offsets, twiddle_ref, table, z_ref, out_hbm, *refs):
    left, leg, prod_a, prod_b, x_ref, out_ref, out_sems = refs
    tiles = table.shape[0]
    split = twiddle_ref.shape[1]
    tall = x_ref.shape[2]
    group = tall // width
    modes = out_ref.shape[3]
    sources = out_ref.shape[1]
    parts = z_ref.shape[0] // sources
    cycles = leg.shape[0] // offsets
    blocks = sources * modes // (tiles * LANES)
    per = modes // LANES
    count = cycles // parts * width
    high = cycles // parts * offsets

    def store(step, n):
        mode_tile = n // 2 * tiles + 2 * step + n % 2
        lanes = pl.ds(pl.multiple_of(mode_tile % per * LANES, LANES), LANES)
        where = (slice(None), mode_tile // per, slice(None), lanes)
        return pltpu.make_async_copy(out_ref.at[where], out_hbm.at[where], out_sems.at[step, n])

    fold = left.shape[0]
    for p in range(parts):
        for q in range(sources // fold):
            lanes = slice(q * LANES, (q + 1) * LANES)
            for n in range(split):
                place = (n * parts + p) * count
                rows = z_ref[p * sources + q, n * count : (n + 1) * count, :]
                if fold == 1:
                    left[0, place : place + count, lanes] = rows
                else:
                    rows = rows.astype(jnp.float32)
                    more = z_ref[p * sources + sources // 2 + q, n * count : (n + 1) * count, :].astype(jnp.float32)
                    left[0, place : place + count, lanes] = (rows + more).astype(jnp.bfloat16)
                    left[1, place : place + count, lanes] = (rows - more).astype(jnp.bfloat16)

    def product(tile, prod, kind):
        prod[...] = jnp.dot(left[kind % fold], table[tile], preferred_element_type=jnp.float32)

    product(0, prod_a, 0)
    for p in range(parts):
        for q in range(sources):
            for n in range(per):
                place = split * count + n * high
                rows = z_ref[p * sources + q, place : place + high, :].astype(jnp.float32)
                leg[p * high : (p + 1) * high, (q * per + n) * LANES : (q * per + n + 1) * LANES] = rows

    def use(tile, prod):
        lanes = pl.ds(pl.multiple_of(tile * LANES, LANES), LANES)
        cosine, sine = twiddle_ref[0, :, lanes], twiddle_ref[1, :, lanes]
        row_in = lax.broadcasted_iota(jnp.int32, (tall, LANES), 0)
        for pack in range(cycles // group):
            values = []
            for s in range(split):
                place = (s * cycles + pack * group) * width
                re = prod[place : place + tall, :LANES]
                im = prod[place : place + tall, LANES:]
                if s == 0:
                    values.append((re, im))
                else:
                    c, d = cosine[s : s + 1, :], sine[s : s + 1, :]
                    values.append((re * c + im * d, im * c - re * d))
            parts = dft(values)
            for b in range(blocks):
                for g in range(group):
                    shifts = ((group - g) * width % tall, (group + 1 - g) * width % tall)
                    rows = [pltpu.roll(v, m, 0) if m else v for v, m in zip(parts[b], shifts)]
                    x_ref[b, pack * group + g] = jnp.where(row_in < width, rows[0], rows[1])
        for b in range(blocks):
            mode_tile = b * tiles + tile
            d, n = mode_tile // per, mode_tile % per
            mode = pl.ds(pl.multiple_of(mode_tile * LANES, LANES), LANES)
            values = [x_ref[b, r] for r in range(cycles)]
            for k in range(offsets):
                total = None
                for r in range(cycles):
                    term = leg[r * offsets + k : r * offsets + k + 1, mode] * values[r]
                    total = term if r == 0 else total + term
                place = pl.ds(pl.multiple_of(n * LANES, LANES), LANES)
                out_ref[k, d, :, place] = total[: 2 * width].astype(jnp.bfloat16)

    @pl.loop(0, tiles // 2)
    def _(step):
        product(2 * step + 1, prod_b, 1)
        use(2 * step, prod_a)
        product(jnp.minimum(2 * step + 2, tiles - 2), prod_a, 0)
        use(2 * step + 1, prod_b)
        for n in range(2 * blocks):
            store(step, n).start()

    @pl.loop(0, tiles // 2)
    def _(step):
        for n in range(2 * blocks):
            store(step, n).wait()


def sketch_kernel(alm_ref, band_ref, cov_ref, test_ref, out_ref, left_ref):
    patches, groups, rows, lanes = alm_ref.shape
    chans = cov_ref.shape[0]
    width = rows // 2
    for g in range(groups):
        part = alm_ref[0, g].astype(jnp.float32)
        for p in range(1, patches):
            part += alm_ref[p, g].astype(jnp.float32)
        part = part * band_ref[...]
        for t in range(2):
            left_ref[t, g * width : (g + 1) * width, :] = part[t * width : (t + 1) * width]
    sketch = None
    for t in range(2):
        term = lax.dot_general(
            test_ref[t],
            left_ref[t].astype(jnp.bfloat16),
            (((0,), (1,)), ((), ())),
            preferred_element_type=jnp.float32,
        )
        sketch = term if t == 0 else sketch + term
    mixed = lax.dot_general(
        sketch,
        cov_ref[...],
        (((1,), (1,)), ((), ())),
        precision=lax.Precision.HIGHEST,
        preferred_element_type=jnp.float32,
    )
    if out_ref.ndim == 2:
        out_ref[...] = mixed
    else:
        owners, block, _ = out_ref.shape
        fold = out_ref.shape[2] // chans
        mixed = mixed.reshape(owners, fold, block, chans)
        out_ref[...] = jnp.concatenate([mixed[:, n] for n in range(fold)], axis=-1)


def total_kernel(part_ref, out_ref):
    block, chans = part_ref.shape[1], out_ref.shape[1]
    total = jnp.sum(part_ref[...], axis=0)
    for n in range(part_ref.shape[2] // chans):
        out_ref[n * block : (n + 1) * block, :] = total[:, n * chans : (n + 1) * chans]


def call(kernel, shape, scratch, mib, spaces, *operands, out_space=pltpu.VMEM, cost=(0, 0)):
    return pl.pallas_call(
        kernel,
        out_shape=shape,
        in_specs=[pl.BlockSpec(memory_space=space) for space in spaces],
        out_specs=jax.tree.map(lambda _: pl.BlockSpec(memory_space=out_space), shape),
        scratch_shapes=scratch,
        compiler_params=pltpu.CompilerParams(vmem_limit_bytes=mib * MIB),
        cost_estimate=pl.CostEstimate(flops=cost[0], bytes_accessed=cost[1], transcendentals=0),
    )(*operands)


def in_order(modes, fold):
    return np.arange(modes).reshape(-1, LANES, fold).swapaxes(1, 2).reshape(-1)


def transform_tables(split, cycle, fold):
    half = cycle // split
    modes = in_order(half, fold)
    step = np.arange(split)[:, None] * modes[None, :] % cycle
    angle = step * (2.0 * math.pi / cycle)
    twiddle = np.stack([np.cos(angle), np.sin(angle)]).astype(np.float32)
    step = np.arange(half // fold)[:, None] * modes[None, :] % half
    angle = (step * (2.0 * math.pi / half)).reshape(half // fold, half // LANES, LANES)
    table = np.transpose(np.concatenate([np.cos(angle), -np.sin(angle)], axis=2), (1, 0, 2))
    return twiddle, table.astype(ml_dtypes.bfloat16)


def local(sky_map, pixel_mask, noise_factor, cycle_legendre, band_power, channel_cov, test_matrix):
    cycles, pixels, chans = sky_map.shape
    modes, _ = band_power.shape
    offsets = cycle_legendre.shape[2]
    columns = test_matrix.shape[3]
    mode_count, pair = lax.axis_size("mode"), lax.axis_size("low")
    groups = pair * mode_count
    devices = lax.axis_size("high") * groups
    width = chans // groups
    group = max(1, SUBLANES // width)
    split = pixels // LANES
    rows = split * cycles * width
    legs = cycles * offsets * (modes // LANES)
    tiles = mode_count
    blocks = modes * mode_count // (tiles * LANES)
    everyone = ("high", "low", "mode")
    hbm, vmem, bf16, f32, shape = pl.ANY, pltpu.VMEM, jnp.bfloat16, jnp.float32, jax.ShapeDtypeStruct
    fold = 2 if modes % (2 * LANES) == 0 else 1
    twiddle, table = transform_tables(split, pixels * mode_count, fold)

    message = call(
        functools.partial(whiten_kernel, fold),
        shape((groups, rows + legs, LANES), bf16),
        [
            vmem((cycles, chans, pixels), bf16),
            vmem((cycles, pixels), jnp.int32),
            vmem((cycles, chans, chans), f32),
            vmem((cycles, offsets, modes), f32),
            vmem((pixels, pixels), bf16),
            vmem((cycles * chans, pixels), bf16),
            vmem((groups, rows + legs, LANES), bf16),
            pltpu.SemaphoreType.DMA((5 + split // 2,)),
        ],
        56,
        [hbm] * 4,
        jnp.transpose(sky_map, (0, 2, 1)),
        pixel_mask,
        noise_factor[:, 0],
        jnp.transpose(cycle_legendre, (0, 2, 1)),
        out_space=hbm,
        cost=(2 * cycles * chans * pixels * (pixels + 4 * chans), 8 * MIB),
    )
    message = lax.all_to_all(message, ("low", "mode"), 0, 0, tiled=True)

    alm = call(
        functools.partial(modes_kernel, width, offsets),
        shape((offsets, mode_count, 2 * width, modes), bf16),
        [
            vmem((fold, pair * rows, tiles * LANES // fold), bf16),
            vmem((pair * cycles * offsets, mode_count * modes), f32),
            vmem((pair * rows, 2 * LANES), f32),
            vmem((pair * rows, 2 * LANES), f32),
            vmem((blocks, pair * cycles, group * width, LANES), f32),
            vmem((offsets, mode_count, 2 * width, modes), bf16),
            pltpu.SemaphoreType.DMA((tiles // 2, 2 * blocks)),
        ],
        24,
        [vmem] * 3,
        jnp.asarray(twiddle),
        jnp.asarray(table),
        message,
        out_space=hbm,
        cost=(4 * pair * rows * (tiles * LANES) ** 2 // fold, 8 * MIB),
    )
    alm = alm.reshape(devices, 2 * width, modes)
    alm = lax.all_to_all(alm, everyone, 0, 0, tiled=True)
    alm = alm.reshape(devices // groups, groups, 2 * width, modes)

    right = test_matrix.reshape(modes // (fold * LANES), LANES, fold, 2, columns)
    right = jnp.transpose(right, (3, 0, 2, 1, 4)).reshape(2, modes, columns)
    band = jnp.swapaxes(band_power.reshape(-1, LANES, fold), 1, 2).reshape(1, modes)
    share = columns // (devices)
    fold = LANES // chans
    packed = share % (8 * fold) == 0
    part = call(
        sketch_kernel,
        shape((devices, share // fold, LANES) if packed else (columns, chans), f32),
        [vmem((2, chans, modes), f32)],
        24,
        [vmem] * 4,
        alm,
        band,
        channel_cov,
        right,
    )
    if not packed:
        part = part.reshape(devices, share, chans)
    part = lax.all_to_all(part, everyone, 0, 0, tiled=True)
    return jnp.transpose(call(total_kernel, shape((share, chans), f32), [], 16, [vmem], part))


def solution(mesh):
    patches, modes = mesh.shape["patch"], mesh.shape["mode"]
    mesh = jax.sharding.Mesh(mesh.devices.reshape(patches // 2, 2, modes), ("high", "low", "mode"))
    patch = ("high", "low")
    return jax.shard_map(
        local,
        mesh=mesh,
        in_specs=(
            P(patch, "mode", None),
            P(patch, "mode"),
            P(patch, "mode", None, None),
            P(patch, "mode", None),
            P("mode", patch),
            P(),
            P(patch, "mode", None, None),
        ),
        out_specs=P(None, (*patch, "mode")),
        check_vma=False,
    )
```

```python
import functools
import math

import jax
import jax.numpy as jnp
import ml_dtypes
import numpy as np
from jax import lax
from jax.experimental import pallas as pl
from jax.experimental.pallas import tpu as pltpu
from jax.sharding import PartitionSpec as P

LANES = 128
MIB = 1 << 20
SUBLANES = 8


def rotate(value, step, points):
    re, im = value
    step %= points
    if step == 0:
        return re, im
    if 2 * step == points:
        return -re, -im
    if 4 * step == points:
        return im, -re
    if 8 * step == points:
        return (re + im) * math.sqrt(0.5), (im - re) * math.sqrt(0.5)
    if 8 * step == 3 * points:
        return (im - re) * math.sqrt(0.5), (re + im) * -math.sqrt(0.5)
    c, s = math.cos(2 * math.pi * step / points), math.sin(2 * math.pi * step / points)
    return re * c + im * s, im * c - re * s


def dft(values):
    n = len(values)
    if n == 1:
        return values
    half = n // 2
    even, odd = dft(values[0::2]), dft(values[1::2])
    out = [None] * n
    for b in range(half):
        re, im = rotate(odd[b], b, n)
        out[b] = even[b][0] + re, even[b][1] + im
        out[b + half] = even[b][0] - re, even[b][1] - im
    return out


def whiten_kernel(fold, sky_hbm, mask_hbm, factor_hbm, leg_hbm, out_hbm, *refs):
    sky, mask, factor, leg, sort, white, stage, sems = refs
    cycles, chans, pixels = sky.shape
    groups = stage.shape[0]
    width = chans // groups
    group = max(1, SUBLANES // width)
    tall = group * width
    split = pixels // LANES
    sources, targets = (factor_hbm, sky_hbm, mask_hbm, leg_hbm), (factor, sky, mask, leg)
    copies = [pltpu.make_async_copy(a, b, sems.at[n]) for n, (a, b) in enumerate(zip(sources, targets))]
    for copy in copies:
        copy.start()
    shape = (2 * LANES, LANES)
    ahead = lax.broadcasted_iota(jnp.int32, shape, 0) - split * lax.broadcasted_iota(jnp.int32, shape, 1)
    for first in range(0, pixels, 2 * LANES):
        for s in range(split):
            block = jnp.where(ahead == s - first, 1.0, 0.0).astype(jnp.bfloat16)
            sort[first : first + 2 * LANES, s * LANES : (s + 1) * LANES] = block
    copies[0].wait()
    row_of = lax.broadcasted_iota(jnp.int32, (tall, group * chans), 0) // width
    lane_of = lax.broadcasted_iota(jnp.int32, (tall, group * chans), 1) // chans
    lefts = []
    for pack in range(cycles // group):
        rows = []
        for e in range(groups):
            tile = [factor[pack * group + g, e * width : (e + 1) * width, :] for g in range(group)]
            tile = jnp.concatenate(tile, axis=0)
            rows.append(jnp.where(row_of == lane_of, jnp.concatenate([tile] * group, axis=1), 0.0))
        rows = jnp.concatenate(rows, axis=0)
        high = rows.astype(jnp.bfloat16)
        low = (rows - high.astype(jnp.float32)).astype(jnp.bfloat16)
        lefts.append(jnp.concatenate([high, low], axis=1))
    for copy in copies[1:3]:
        copy.wait()
    cycle_of = lax.broadcasted_iota(jnp.int32, (tall, pixels), 0) // width
    for pack in range(cycles // group):
        data = jnp.concatenate([sky[pack * group + g] for g in range(group)] * 2, axis=0)
        value = jnp.dot(lefts[pack], data, preferred_element_type=jnp.float32)
        keep = jnp.broadcast_to(mask[pack * group : pack * group + 1, :], (tall, pixels))
        for g in range(1, group):
            keep = jnp.where(cycle_of < g, keep, mask[pack * group + g : pack * group + g + 1, :])
        keep = keep.astype(jnp.float32)
        for e in range(groups):
            place = (e * (cycles // group) + pack) * tall
            white[place : place + tall, :] = (value[e * tall : (e + 1) * tall] * keep).astype(jnp.bfloat16)
    copies[3].wait()
    count = cycles * width
    rows = jnp.concatenate([leg[r] for r in range(cycles)], axis=0).astype(jnp.bfloat16)
    high = rows.shape[0]
    if fold > 1:
        shape = (fold * LANES, LANES)
        ahead = lax.broadcasted_iota(jnp.int32, shape, 0) - fold * lax.broadcasted_iota(jnp.int32, shape, 1)
        places = [jnp.where(ahead == n, 1.0, 0.0).astype(jnp.bfloat16) for n in range(fold)]
        places = jnp.concatenate(places, axis=1)
        rows = [
            jnp.dot(rows[:, n : n + fold * LANES], places, preferred_element_type=jnp.float32)
            for n in range(0, rows.shape[1], fold * LANES)
        ]
        rows = jnp.concatenate(rows, axis=1).astype(jnp.bfloat16)
    for n in range(rows.shape[1] // LANES):
        for e in range(groups):
            place = split * count + n * high
            stage[e, place : place + high, :] = rows[:, n * LANES : (n + 1) * LANES]
    sends = []

    def send(first, last):
        where = (slice(None), slice(first, last))
        sends.append(pltpu.make_async_copy(stage.at[where], out_hbm.at[where], sems.at[4 + len(sends)]))
        sends[-1].start()

    send(split * count, stage.shape[1])
    for pair in range(split // 2):
        wide = slice(pair * 2 * LANES, (pair + 1) * 2 * LANES)
        value = jnp.dot(white[...], sort[:, wide], preferred_element_type=jnp.float32).astype(jnp.bfloat16)
        for side in range(2):
            s = pair * 2 + side
            for e in range(groups):
                stage[e, s * count : (s + 1) * count, :] = value[
                    e * count : (e + 1) * count, side * LANES : (side + 1) * LANES
                ]
        send(pair * 2 * count, (pair + 1) * 2 * count)
    for send in sends:
        send.wait()


def modes_kernel(width, offsets, twiddle_ref, table, z_ref, out_hbm, *refs):
    left, leg, prod_a, prod_b, x_ref, out_ref, out_sems = refs
    tiles = table.shape[0]
    split = twiddle_ref.shape[1]
    tall = x_ref.shape[2]
    group = tall // width
    modes = out_ref.shape[3]
    sources = out_ref.shape[1]
    parts = z_ref.shape[0] // sources
    cycles = leg.shape[0] // offsets
    blocks = sources * modes // (tiles * LANES)
    per = modes // LANES
    count = cycles // parts * width
    high = cycles // parts * offsets

    def store(step, n):
        mode_tile = n // 2 * tiles + 2 * step + n % 2
        lanes = pl.ds(pl.multiple_of(mode_tile % per * LANES, LANES), LANES)
        where = (slice(None), mode_tile // per, slice(None), lanes)
        return pltpu.make_async_copy(out_ref.at[where], out_hbm.at[where], out_sems.at[step, n])

    fold = left.shape[0]
    for p in range(parts):
        for q in range(sources // fold):
            lanes = slice(q * LANES, (q + 1) * LANES)
            for n in range(split):
                place = (n * parts + p) * count
                rows = z_ref[p * sources + q, n * count : (n + 1) * count, :]
                if fold == 1:
                    left[0, place : place + count, lanes] = rows
                else:
                    rows = rows.astype(jnp.float32)
                    more = z_ref[p * sources + sources // 2 + q, n * count : (n + 1) * count, :].astype(jnp.float32)
                    left[0, place : place + count, lanes] = (rows + more).astype(jnp.bfloat16)
                    left[1, place : place + count, lanes] = (rows - more).astype(jnp.bfloat16)

    def product(tile, prod, kind):
        prod[...] = jnp.dot(left[kind % fold], table[tile], preferred_element_type=jnp.float32)

    product(0, prod_a, 0)
    for p in range(parts):
        for q in range(sources):
            for n in range(per):
                place = split * count + n * high
                rows = z_ref[p * sources + q, place : place + high, :].astype(jnp.float32)
                leg[p * high : (p + 1) * high, (q * per + n) * LANES : (q * per + n + 1) * LANES] = rows

    def use(tile, prod):
        lanes = pl.ds(pl.multiple_of(tile * LANES, LANES), LANES)
        cosine, sine = twiddle_ref[0, :, lanes], twiddle_ref[1, :, lanes]
        row_in = lax.broadcasted_iota(jnp.int32, (tall, LANES), 0)
        for pack in range(cycles // group):
            values = []
            for s in range(split):
                place = (s * cycles + pack * group) * width
                re = prod[place : place + tall, :LANES]
                im = prod[place : place + tall, LANES:]
                if s == 0:
                    values.append((re, im))
                else:
                    c, d = cosine[s : s + 1, :], sine[s : s + 1, :]
                    values.append((re * c + im * d, im * c - re * d))
            parts = dft(values)
            for b in range(blocks):
                for g in range(group):
                    shifts = ((group - g) * width % tall, (group + 1 - g) * width % tall)
                    rows = [pltpu.roll(v, m, 0) if m else v for v, m in zip(parts[b], shifts)]
                    x_ref[b, pack * group + g] = jnp.where(row_in < width, rows[0], rows[1])
        for b in range(blocks):
            mode_tile = b * tiles + tile
            d, n = mode_tile // per, mode_tile % per
            mode = pl.ds(pl.multiple_of(mode_tile * LANES, LANES), LANES)
            values = [x_ref[b, r] for r in range(cycles)]
            for k in range(offsets):
                total = None
                for r in range(cycles):
                    term = leg[r * offsets + k : r * offsets + k + 1, mode] * values[r]
                    total = term if r == 0 else total + term
                place = pl.ds(pl.multiple_of(n * LANES, LANES), LANES)
                out_ref[k, d, :, place] = total[: 2 * width].astype(jnp.bfloat16)

    @pl.loop(0, tiles // 2)
    def _(step):
        product(2 * step + 1, prod_b, 1)
        use(2 * step, prod_a)
        product(jnp.minimum(2 * step + 2, tiles - 2), prod_a, 0)
        use(2 * step + 1, prod_b)
        for n in range(2 * blocks):
            store(step, n).start()

    @pl.loop(0, tiles // 2)
    def _(step):
        for n in range(2 * blocks):
            store(step, n).wait()


def sketch_kernel(alm_ref, band_ref, cov_ref, test_ref, out_ref, left_ref):
    patches, groups, rows, lanes = alm_ref.shape
    chans = cov_ref.shape[0]
    width = rows // 2
    for g in range(groups):
        part = alm_ref[0, g].astype(jnp.float32)
        for p in range(1, patches):
            part += alm_ref[p, g].astype(jnp.float32)
        part = part * band_ref[...]
        for t in range(2):
            left_ref[t, g * width : (g + 1) * width, :] = part[t * width : (t + 1) * width]
    sketch = None
    for t in range(2):
        term = jnp.dot(left_ref[t].astype(jnp.bfloat16), test_ref[t], preferred_element_type=jnp.float32)
        sketch = term if t == 0 else sketch + term
    mixed = jnp.dot(
        cov_ref[...], sketch, precision=lax.Precision.HIGHEST, preferred_element_type=jnp.float32
    )
    mixed = jnp.transpose(mixed)
    if out_ref.ndim == 2:
        out_ref[...] = mixed
    else:
        owners, block, _ = out_ref.shape
        fold = out_ref.shape[2] // chans
        mixed = mixed.reshape(owners, fold, block, chans)
        out_ref[...] = jnp.concatenate([mixed[:, n] for n in range(fold)], axis=-1)


def total_kernel(part_ref, out_ref):
    block, chans = part_ref.shape[1], out_ref.shape[1]
    total = jnp.sum(part_ref[...], axis=0)
    for n in range(part_ref.shape[2] // chans):
        out_ref[n * block : (n + 1) * block, :] = total[:, n * chans : (n + 1) * chans]


def call(kernel, shape, scratch, mib, spaces, *operands, out_space=pltpu.VMEM, cost=(0, 0)):
    return pl.pallas_call(
        kernel,
        out_shape=shape,
        in_specs=[pl.BlockSpec(memory_space=space) for space in spaces],
        out_specs=jax.tree.map(lambda _: pl.BlockSpec(memory_space=out_space), shape),
        scratch_shapes=scratch,
        compiler_params=pltpu.CompilerParams(vmem_limit_bytes=mib * MIB),
        cost_estimate=pl.CostEstimate(flops=cost[0], bytes_accessed=cost[1], transcendentals=0),
    )(*operands)


def in_order(modes, fold):
    return np.arange(modes).reshape(-1, LANES, fold).swapaxes(1, 2).reshape(-1)


def transform_tables(split, cycle, fold):
    half = cycle // split
    modes = in_order(half, fold)
    step = np.arange(split)[:, None] * modes[None, :] % cycle
    angle = step * (2.0 * math.pi / cycle)
    twiddle = np.stack([np.cos(angle), np.sin(angle)]).astype(np.float32)
    step = np.arange(half // fold)[:, None] * modes[None, :] % half
    angle = (step * (2.0 * math.pi / half)).reshape(half // fold, half // LANES, LANES)
    table = np.transpose(np.concatenate([np.cos(angle), -np.sin(angle)], axis=2), (1, 0, 2))
    return twiddle, table.astype(ml_dtypes.bfloat16)


def local(sky_map, pixel_mask, noise_factor, cycle_legendre, band_power, channel_cov, test_matrix):
    cycles, pixels, chans = sky_map.shape
    modes, _ = band_power.shape
    offsets = cycle_legendre.shape[2]
    columns = test_matrix.shape[3]
    mode_count, pair = lax.axis_size("mode"), lax.axis_size("low")
    groups = pair * mode_count
    devices = lax.axis_size("high") * groups
    width = chans // groups
    group = max(1, SUBLANES // width)
    split = pixels // LANES
    rows = split * cycles * width
    legs = cycles * offsets * (modes // LANES)
    tiles = mode_count
    blocks = modes * mode_count // (tiles * LANES)
    everyone = ("high", "low", "mode")
    hbm, vmem, bf16, f32, shape = pl.ANY, pltpu.VMEM, jnp.bfloat16, jnp.float32, jax.ShapeDtypeStruct
    fold = 2 if modes % (2 * LANES) == 0 else 1
    twiddle, table = transform_tables(split, pixels * mode_count, fold)

    message = call(
        functools.partial(whiten_kernel, fold),
        shape((groups, rows + legs, LANES), bf16),
        [
            vmem((cycles, chans, pixels), bf16),
            vmem((cycles, pixels), jnp.int32),
            vmem((cycles, chans, chans), f32),
            vmem((cycles, offsets, modes), f32),
            vmem((pixels, pixels), bf16),
            vmem((cycles * chans, pixels), bf16),
            vmem((groups, rows + legs, LANES), bf16),
            pltpu.SemaphoreType.DMA((5 + split // 2,)),
        ],
        56,
        [hbm] * 4,
        jnp.transpose(sky_map, (0, 2, 1)),
        pixel_mask,
        noise_factor[:, 0],
        jnp.transpose(cycle_legendre, (0, 2, 1)),
        out_space=hbm,
        cost=(2 * cycles * chans * pixels * (pixels + 4 * chans), 8 * MIB),
    )
    message = lax.all_to_all(message, ("low", "mode"), 0, 0, tiled=True)

    alm = call(
        functools.partial(modes_kernel, width, offsets),
        shape((offsets, mode_count, 2 * width, modes), bf16),
        [
            vmem((fold, pair * rows, tiles * LANES // fold), bf16),
            vmem((pair * cycles * offsets, mode_count * modes), f32),
            vmem((pair * rows, 2 * LANES), f32),
            vmem((pair * rows, 2 * LANES), f32),
            vmem((blocks, pair * cycles, group * width, LANES), f32),
            vmem((offsets, mode_count, 2 * width, modes), bf16),
            pltpu.SemaphoreType.DMA((tiles // 2, 2 * blocks)),
        ],
        24,
        [vmem] * 3,
        jnp.asarray(twiddle),
        jnp.asarray(table),
        message,
        out_space=hbm,
        cost=(4 * pair * rows * (tiles * LANES) ** 2 // fold, 8 * MIB),
    )
    alm = alm.reshape(devices, 2 * width, modes)
    alm = lax.all_to_all(alm, everyone, 0, 0, tiled=True)
    alm = alm.reshape(devices // groups, groups, 2 * width, modes)

    right = test_matrix.reshape(modes // (fold * LANES), LANES, fold, 2, columns)
    right = jnp.transpose(right, (3, 0, 2, 1, 4)).reshape(2, modes, columns)
    band = jnp.swapaxes(band_power.reshape(-1, LANES, fold), 1, 2).reshape(1, modes)
    share = columns // (devices)
    fold = LANES // chans
    packed = share % (8 * fold) == 0
    part = call(
        sketch_kernel,
        shape((devices, share // fold, LANES) if packed else (columns, chans), f32),
        [vmem((2, chans, modes), f32)],
        24,
        [vmem] * 4,
        alm,
        band,
        channel_cov,
        right,
    )
    if not packed:
        part = part.reshape(devices, share, chans)
    part = lax.all_to_all(part, everyone, 0, 0, tiled=True)
    return jnp.transpose(call(total_kernel, shape((share, chans), f32), [], 16, [vmem], part))


def solution(mesh):
    patches, modes = mesh.shape["patch"], mesh.shape["mode"]
    mesh = jax.sharding.Mesh(mesh.devices.reshape(patches // 2, 2, modes), ("high", "low", "mode"))
    patch = ("high", "low")
    return jax.shard_map(
        local,
        mesh=mesh,
        in_specs=(
            P(patch, "mode", None),
            P(patch, "mode"),
            P(patch, "mode", None, None),
            P(patch, "mode", None),
            P("mode", patch),
            P(),
            P(patch, "mode", None, None),
        ),
        out_specs=P(None, (*patch, "mode")),
        check_vma=False,
    )
```

```python
import functools
import math

import jax
import jax.numpy as jnp
import ml_dtypes
import numpy as np
from jax import lax
from jax.experimental import pallas as pl
from jax.experimental.pallas import tpu as pltpu
from jax.sharding import PartitionSpec as P

LANES = 128
MIB = 1 << 20
SUBLANES = 8


def rotate(value, step, points):
    re, im = value
    step %= points
    if step == 0:
        return re, im
    if 2 * step == points:
        return -re, -im
    if 4 * step == points:
        return im, -re
    if 8 * step == points:
        return (re + im) * math.sqrt(0.5), (im - re) * math.sqrt(0.5)
    if 8 * step == 3 * points:
        return (im - re) * math.sqrt(0.5), (re + im) * -math.sqrt(0.5)
    c, s = math.cos(2 * math.pi * step / points), math.sin(2 * math.pi * step / points)
    return re * c + im * s, im * c - re * s


def dft(values):
    n = len(values)
    if n == 1:
        return values
    half = n // 2
    even, odd = dft(values[0::2]), dft(values[1::2])
    out = [None] * n
    for b in range(half):
        re, im = rotate(odd[b], b, n)
        out[b] = even[b][0] + re, even[b][1] + im
        out[b + half] = even[b][0] - re, even[b][1] - im
    return out


def whiten_kernel(fold, sky_hbm, mask_hbm, factor_hbm, leg_hbm, out_hbm, *refs):
    sky, mask, factor, leg, sort, white, stage, leg_rows, sems = refs
    cycles, chans, pixels = sky.shape
    groups = stage.shape[0]
    width = chans // groups
    group = max(1, SUBLANES // width)
    tall = group * width
    split = pixels // LANES
    sources, targets = (factor_hbm, leg_hbm, sky_hbm, mask_hbm), (factor, leg, sky, mask)
    copies = [pltpu.make_async_copy(a, b, sems.at[n]) for n, (a, b) in enumerate(zip(sources, targets))]
    for copy in copies:
        copy.start()
    shape = (2 * LANES, LANES)
    ahead = lax.broadcasted_iota(jnp.int32, shape, 0) - split * lax.broadcasted_iota(jnp.int32, shape, 1)
    for first in range(0, pixels, 2 * LANES):
        for s in range(split):
            block = jnp.where(ahead == s - first, 1.0, 0.0).astype(jnp.bfloat16)
            sort[first : first + 2 * LANES, s * LANES : (s + 1) * LANES] = block
    copies[0].wait()
    row_of = lax.broadcasted_iota(jnp.int32, (tall, group * chans), 0) // width
    lane_of = lax.broadcasted_iota(jnp.int32, (tall, group * chans), 1) // chans
    lefts = []
    for pack in range(cycles // group):
        rows = []
        for e in range(groups):
            tile = [factor[pack * group + g, e * width : (e + 1) * width, :] for g in range(group)]
            tile = jnp.concatenate(tile, axis=0)
            rows.append(jnp.where(row_of == lane_of, jnp.concatenate([tile] * group, axis=1), 0.0))
        rows = jnp.concatenate(rows, axis=0)
        high = rows.astype(jnp.bfloat16)
        low = (rows - high.astype(jnp.float32)).astype(jnp.bfloat16)
        lefts.append(jnp.concatenate([high, low], axis=1))
    copies[1].wait()
    count = cycles * width
    rows = jnp.concatenate([leg[r] for r in range(cycles)], axis=0).astype(jnp.bfloat16)
    high = rows.shape[0]
    if fold > 1:
        shape = (fold * LANES, LANES)
        ahead = lax.broadcasted_iota(jnp.int32, shape, 0) - fold * lax.broadcasted_iota(jnp.int32, shape, 1)
        places = [jnp.where(ahead == n, 1.0, 0.0).astype(jnp.bfloat16) for n in range(fold)]
        places = jnp.concatenate(places, axis=1)
        rows = [
            jnp.dot(rows[:, n : n + fold * LANES], places, preferred_element_type=jnp.float32)
            for n in range(0, rows.shape[1], fold * LANES)
        ]
        rows = jnp.concatenate(rows, axis=1).astype(jnp.bfloat16)
    for n in range(rows.shape[1] // LANES):
        leg_rows[n * high : (n + 1) * high, :] = rows[:, n * LANES : (n + 1) * LANES]
    sends = []

    def send(source, target):
        sends.append(pltpu.make_async_copy(source, target, sems.at[4 + len(sends)]))
        sends[-1].start()

    for e in range(groups):
        send(leg_rows, out_hbm.at[e, split * count :])
    for copy in copies[2:]:
        copy.wait()
    cycle_of = lax.broadcasted_iota(jnp.int32, (tall, pixels), 0) // width
    for pack in range(cycles // group):
        data = jnp.concatenate([sky[pack * group + g] for g in range(group)] * 2, axis=0)
        value = jnp.dot(lefts[pack], data, preferred_element_type=jnp.float32)
        keep = jnp.broadcast_to(mask[pack * group : pack * group + 1, :], (tall, pixels))
        for g in range(1, group):
            keep = jnp.where(cycle_of < g, keep, mask[pack * group + g : pack * group + g + 1, :])
        keep = keep.astype(jnp.float32)
        for e in range(groups):
            place = (e * (cycles // group) + pack) * tall
            white[place : place + tall, :] = (value[e * tall : (e + 1) * tall] * keep).astype(jnp.bfloat16)
    for pair in range(split // 2):
        wide = slice(pair * 2 * LANES, (pair + 1) * 2 * LANES)
        value = jnp.dot(white[...], sort[:, wide], preferred_element_type=jnp.float32).astype(jnp.bfloat16)
        for side in range(2):
            s = pair * 2 + side
            for e in range(groups):
                stage[e, s * count : (s + 1) * count, :] = value[
                    e * count : (e + 1) * count, side * LANES : (side + 1) * LANES
                ]
        where = (slice(None), slice(pair * 2 * count, (pair + 1) * 2 * count))
        send(stage.at[where], out_hbm.at[where])
    for send in sends:
        send.wait()


def modes_kernel(width, offsets, twiddle_ref, table, z_ref, out_hbm, *refs):
    left, leg, prod_a, prod_b, x_ref, out_ref, out_sems = refs
    tiles = table.shape[0]
    split = twiddle_ref.shape[1]
    tall = x_ref.shape[2]
    group = tall // width
    modes = out_ref.shape[3]
    sources = out_ref.shape[1]
    parts = z_ref.shape[0] // sources
    cycles = leg.shape[0] // offsets
    blocks = sources * modes // (tiles * LANES)
    per = modes // LANES
    count = cycles // parts * width
    high = cycles // parts * offsets

    def store(step, n):
        mode_tile = n // 2 * tiles + 2 * step + n % 2
        lanes = pl.ds(pl.multiple_of(mode_tile % per * LANES, LANES), LANES)
        where = (slice(None), mode_tile // per, slice(None), lanes)
        return pltpu.make_async_copy(out_ref.at[where], out_hbm.at[where], out_sems.at[step, n])

    fold = left.shape[0]
    for p in range(parts):
        for q in range(sources // fold):
            lanes = slice(q * LANES, (q + 1) * LANES)
            for n in range(split):
                place = (n * parts + p) * count
                rows = z_ref[p * sources + q, n * count : (n + 1) * count, :]
                if fold == 1:
                    left[0, place : place + count, lanes] = rows
                else:
                    rows = rows.astype(jnp.float32)
                    more = z_ref[p * sources + sources // 2 + q, n * count : (n + 1) * count, :].astype(jnp.float32)
                    left[0, place : place + count, lanes] = (rows + more).astype(jnp.bfloat16)
                    left[1, place : place + count, lanes] = (rows - more).astype(jnp.bfloat16)

    def product(tile, prod, kind):
        prod[...] = jnp.dot(left[kind % fold], table[tile], preferred_element_type=jnp.float32)

    product(0, prod_a, 0)
    for p in range(parts):
        for q in range(sources):
            for n in range(per):
                place = split * count + n * high
                rows = z_ref[p * sources + q, place : place + high, :].astype(jnp.float32)
                leg[p * high : (p + 1) * high, (q * per + n) * LANES : (q * per + n + 1) * LANES] = rows

    def use(tile, prod):
        lanes = pl.ds(pl.multiple_of(tile * LANES, LANES), LANES)
        cosine, sine = twiddle_ref[0, :, lanes], twiddle_ref[1, :, lanes]
        row_in = lax.broadcasted_iota(jnp.int32, (tall, LANES), 0)
        for pack in range(cycles // group):
            values = []
            for s in range(split):
                place = (s * cycles + pack * group) * width
                re = prod[place : place + tall, :LANES]
                im = prod[place : place + tall, LANES:]
                if s == 0:
                    values.append((re, im))
                else:
                    c, d = cosine[s : s + 1, :], sine[s : s + 1, :]
                    values.append((re * c + im * d, im * c - re * d))
            parts = dft(values)
            for b in range(blocks):
                for g in range(group):
                    shifts = ((group - g) * width % tall, (group + 1 - g) * width % tall)
                    rows = [pltpu.roll(v, m, 0) if m else v for v, m in zip(parts[b], shifts)]
                    x_ref[b, pack * group + g] = jnp.where(row_in < width, rows[0], rows[1])
        for b in range(blocks):
            mode_tile = b * tiles + tile
            d, n = mode_tile // per, mode_tile % per
            mode = pl.ds(pl.multiple_of(mode_tile * LANES, LANES), LANES)
            values = [x_ref[b, r] for r in range(cycles)]
            for k in range(offsets):
                total = None
                for r in range(cycles):
                    term = leg[r * offsets + k : r * offsets + k + 1, mode] * values[r]
                    total = term if r == 0 else total + term
                place = pl.ds(pl.multiple_of(n * LANES, LANES), LANES)
                out_ref[k, d, :, place] = total[: 2 * width].astype(jnp.bfloat16)

    @pl.loop(0, tiles // 2)
    def _(step):
        product(2 * step + 1, prod_b, 1)
        use(2 * step, prod_a)
        product(jnp.minimum(2 * step + 2, tiles - 2), prod_a, 0)
        use(2 * step + 1, prod_b)
        for n in range(2 * blocks):
            store(step, n).start()

    @pl.loop(0, tiles // 2)
    def _(step):
        for n in range(2 * blocks):
            store(step, n).wait()


def sketch_kernel(alm_ref, band_ref, cov_ref, test_ref, out_ref, left_ref):
    patches, groups, rows, lanes = alm_ref.shape
    chans = cov_ref.shape[0]
    width = rows // 2
    for g in range(groups):
        part = alm_ref[0, g].astype(jnp.float32)
        for p in range(1, patches):
            part += alm_ref[p, g].astype(jnp.float32)
        part = part * band_ref[...]
        for t in range(2):
            left_ref[t, g * width : (g + 1) * width, :] = part[t * width : (t + 1) * width]
    sketch = None
    for t in range(2):
        term = jnp.dot(left_ref[t].astype(jnp.bfloat16), test_ref[t], preferred_element_type=jnp.float32)
        sketch = term if t == 0 else sketch + term
    mixed = jnp.dot(
        cov_ref[...], sketch, precision=lax.Precision.HIGHEST, preferred_element_type=jnp.float32
    )
    mixed = jnp.transpose(mixed)
    if out_ref.ndim == 2:
        out_ref[...] = mixed
    else:
        owners, block, _ = out_ref.shape
        fold = out_ref.shape[2] // chans
        mixed = mixed.reshape(owners, fold, block, chans)
        out_ref[...] = jnp.concatenate([mixed[:, n] for n in range(fold)], axis=-1)


def total_kernel(part_ref, out_ref):
    block, chans = part_ref.shape[1], out_ref.shape[1]
    total = jnp.sum(part_ref[...], axis=0)
    for n in range(part_ref.shape[2] // chans):
        out_ref[n * block : (n + 1) * block, :] = total[:, n * chans : (n + 1) * chans]


def call(kernel, shape, scratch, mib, spaces, *operands, out_space=pltpu.VMEM, cost=(0, 0)):
    return pl.pallas_call(
        kernel,
        out_shape=shape,
        in_specs=[pl.BlockSpec(memory_space=space) for space in spaces],
        out_specs=jax.tree.map(lambda _: pl.BlockSpec(memory_space=out_space), shape),
        scratch_shapes=scratch,
        compiler_params=pltpu.CompilerParams(vmem_limit_bytes=mib * MIB),
        cost_estimate=pl.CostEstimate(flops=cost[0], bytes_accessed=cost[1], transcendentals=0),
    )(*operands)


def in_order(modes, fold):
    return np.arange(modes).reshape(-1, LANES, fold).swapaxes(1, 2).reshape(-1)


def transform_tables(split, cycle, fold):
    half = cycle // split
    modes = in_order(half, fold)
    step = np.arange(split)[:, None] * modes[None, :] % cycle
    angle = step * (2.0 * math.pi / cycle)
    twiddle = np.stack([np.cos(angle), np.sin(angle)]).astype(np.float32)
    step = np.arange(half // fold)[:, None] * modes[None, :] % half
    angle = (step * (2.0 * math.pi / half)).reshape(half // fold, half // LANES, LANES)
    table = np.transpose(np.concatenate([np.cos(angle), -np.sin(angle)], axis=2), (1, 0, 2))
    return twiddle, table.astype(ml_dtypes.bfloat16)


def local(sky_map, pixel_mask, noise_factor, cycle_legendre, band_power, channel_cov, test_matrix):
    cycles, pixels, chans = sky_map.shape
    modes, _ = band_power.shape
    offsets = cycle_legendre.shape[2]
    columns = test_matrix.shape[3]
    mode_count, pair = lax.axis_size("mode"), lax.axis_size("low")
    groups = pair * mode_count
    devices = lax.axis_size("high") * groups
    width = chans // groups
    group = max(1, SUBLANES // width)
    split = pixels // LANES
    rows = split * cycles * width
    legs = cycles * offsets * (modes // LANES)
    tiles = mode_count
    blocks = modes * mode_count // (tiles * LANES)
    everyone = ("high", "low", "mode")
    hbm, vmem, bf16, f32, shape = pl.ANY, pltpu.VMEM, jnp.bfloat16, jnp.float32, jax.ShapeDtypeStruct
    fold = 2 if modes % (2 * LANES) == 0 else 1
    twiddle, table = transform_tables(split, pixels * mode_count, fold)

    message = call(
        functools.partial(whiten_kernel, fold),
        shape((groups, rows + legs, LANES), bf16),
        [
            vmem((cycles, chans, pixels), bf16),
            vmem((cycles, pixels), jnp.int32),
            vmem((cycles, chans, chans), f32),
            vmem((cycles, offsets, modes), f32),
            vmem((pixels, pixels), bf16),
            vmem((cycles * chans, pixels), bf16),
            vmem((groups, rows, LANES), bf16),
            vmem((legs, LANES), bf16),
            pltpu.SemaphoreType.DMA((4 + groups + split // 2,)),
        ],
        56,
        [hbm] * 4,
        jnp.transpose(sky_map, (0, 2, 1)),
        pixel_mask,
        noise_factor[:, 0],
        jnp.transpose(cycle_legendre, (0, 2, 1)),
        out_space=hbm,
        cost=(2 * cycles * chans * pixels * (pixels + 4 * chans), 8 * MIB),
    )
    message = lax.all_to_all(message, ("low", "mode"), 0, 0, tiled=True)

    alm = call(
        functools.partial(modes_kernel, width, offsets),
        shape((offsets, mode_count, 2 * width, modes), bf16),
        [
            vmem((fold, pair * rows, tiles * LANES // fold), bf16),
            vmem((pair * cycles * offsets, mode_count * modes), f32),
            vmem((pair * rows, 2 * LANES), f32),
            vmem((pair * rows, 2 * LANES), f32),
            vmem((blocks, pair * cycles, group * width, LANES), f32),
            vmem((offsets, mode_count, 2 * width, modes), bf16),
            pltpu.SemaphoreType.DMA((tiles // 2, 2 * blocks)),
        ],
        24,
        [vmem] * 3,
        jnp.asarray(twiddle),
        jnp.asarray(table),
        message,
        out_space=hbm,
        cost=(4 * pair * rows * (tiles * LANES) ** 2 // fold, 8 * MIB),
    )
    alm = alm.reshape(devices, 2 * width, modes)
    alm = lax.all_to_all(alm, everyone, 0, 0, tiled=True)
    alm = alm.reshape(devices // groups, groups, 2 * width, modes)

    right = test_matrix.reshape(modes // (fold * LANES), LANES, fold, 2, columns)
    right = jnp.transpose(right, (3, 0, 2, 1, 4)).reshape(2, modes, columns)
    band = jnp.swapaxes(band_power.reshape(-1, LANES, fold), 1, 2).reshape(1, modes)
    share = columns // (devices)
    fold = LANES // chans
    packed = share % (8 * fold) == 0
    part = call(
        sketch_kernel,
        shape((devices, share // fold, LANES) if packed else (columns, chans), f32),
        [vmem((2, chans, modes), f32)],
        24,
        [vmem] * 4,
        alm,
        band,
        channel_cov,
        right,
    )
    if not packed:
        part = part.reshape(devices, share, chans)
    part = lax.all_to_all(part, everyone, 0, 0, tiled=True)
    return jnp.transpose(call(total_kernel, shape((share, chans), f32), [], 16, [vmem], part))


def solution(mesh):
    patches, modes = mesh.shape["patch"], mesh.shape["mode"]
    mesh = jax.sharding.Mesh(mesh.devices.reshape(patches // 2, 2, modes), ("high", "low", "mode"))
    patch = ("high", "low")
    return jax.shard_map(
        local,
        mesh=mesh,
        in_specs=(
            P(patch, "mode", None),
            P(patch, "mode"),
            P(patch, "mode", None, None),
            P(patch, "mode", None),
            P("mode", patch),
            P(),
            P(patch, "mode", None, None),
        ),
        out_specs=P(None, (*patch, "mode")),
        check_vma=False,
    )
```

```python
import functools
import math

import jax
import jax.numpy as jnp
import ml_dtypes
import numpy as np
from jax import lax
from jax.experimental import pallas as pl
from jax.experimental.pallas import tpu as pltpu
from jax.sharding import PartitionSpec as P

LANES = 128
MIB = 1 << 20
SUBLANES = 8


def rotate(value, step, points):
    re, im = value
    step %= points
    if step == 0:
        return re, im
    if 2 * step == points:
        return -re, -im
    if 4 * step == points:
        return im, -re
    if 8 * step == points:
        return (re + im) * math.sqrt(0.5), (im - re) * math.sqrt(0.5)
    if 8 * step == 3 * points:
        return (im - re) * math.sqrt(0.5), (re + im) * -math.sqrt(0.5)
    c, s = math.cos(2 * math.pi * step / points), math.sin(2 * math.pi * step / points)
    return re * c + im * s, im * c - re * s


def dft(values):
    n = len(values)
    if n == 1:
        return values
    half = n // 2
    even, odd = dft(values[0::2]), dft(values[1::2])
    out = [None] * n
    for b in range(half):
        re, im = rotate(odd[b], b, n)
        out[b] = even[b][0] + re, even[b][1] + im
        out[b + half] = even[b][0] - re, even[b][1] - im
    return out


def whiten_kernel(fold, sky_hbm, mask_hbm, factor_hbm, leg_hbm, out_hbm, *refs):
    sky, mask, factor, leg, sort, white, stage, sems = refs
    cycles, chans, pixels = sky.shape
    groups = stage.shape[0]
    width = chans // groups
    group = max(1, SUBLANES // width)
    tall = group * width
    split = pixels // LANES
    sources, targets = (factor_hbm, sky_hbm, mask_hbm, leg_hbm), (factor, sky, mask, leg)
    copies = [pltpu.make_async_copy(a, b, sems.at[n]) for n, (a, b) in enumerate(zip(sources, targets))]
    for copy in copies:
        copy.start()
    shape = (2 * LANES, LANES)
    ahead = lax.broadcasted_iota(jnp.int32, shape, 0) - split * lax.broadcasted_iota(jnp.int32, shape, 1)
    for first in range(0, pixels, 2 * LANES):
        for s in range(split):
            block = jnp.where(ahead == s - first, 1.0, 0.0).astype(jnp.bfloat16)
            sort[first : first + 2 * LANES, s * LANES : (s + 1) * LANES] = block
    copies[0].wait()
    row_of = lax.broadcasted_iota(jnp.int32, (tall, group * chans), 0) // width
    lane_of = lax.broadcasted_iota(jnp.int32, (tall, group * chans), 1) // chans
    lefts = []
    for pack in range(cycles // group):
        rows = []
        for e in range(groups):
            tile = [factor[pack * group + g, e * width : (e + 1) * width, :] for g in range(group)]
            tile = jnp.concatenate(tile, axis=0)
            rows.append(jnp.where(row_of == lane_of, jnp.concatenate([tile] * group, axis=1), 0.0))
        rows = jnp.concatenate(rows, axis=0)
        high = rows.astype(jnp.bfloat16)
        low = (rows - high.astype(jnp.float32)).astype(jnp.bfloat16)
        lefts.append(jnp.concatenate([high, low], axis=1))
    for copy in copies[1:3]:
        copy.wait()
    cycle_of = lax.broadcasted_iota(jnp.int32, (tall, pixels), 0) // width
    for pack in range(cycles // group):
        data = jnp.concatenate([sky[pack * group + g] for g in range(group)] * 2, axis=0)
        value = jnp.dot(lefts[pack], data, preferred_element_type=jnp.float32)
        keep = jnp.broadcast_to(mask[pack * group : pack * group + 1, :], (tall, pixels))
        for g in range(1, group):
            keep = jnp.where(cycle_of < g, keep, mask[pack * group + g : pack * group + g + 1, :])
        keep = keep.astype(jnp.float32)
        for e in range(groups):
            place = (e * (cycles // group) + pack) * tall
            white[place : place + tall, :] = (value[e * tall : (e + 1) * tall] * keep).astype(jnp.bfloat16)
    copies[3].wait()
    count = cycles * width
    rows = jnp.concatenate([leg[r] for r in range(cycles)], axis=0).astype(jnp.bfloat16)
    high = rows.shape[0]
    if fold > 1:
        shape = (fold * LANES, LANES)
        ahead = lax.broadcasted_iota(jnp.int32, shape, 0) - fold * lax.broadcasted_iota(jnp.int32, shape, 1)
        places = [jnp.where(ahead == n, 1.0, 0.0).astype(jnp.bfloat16) for n in range(fold)]
        places = jnp.concatenate(places, axis=1)
        rows = [
            jnp.dot(rows[:, n : n + fold * LANES], places, preferred_element_type=jnp.float32)
            for n in range(0, rows.shape[1], fold * LANES)
        ]
        rows = jnp.concatenate(rows, axis=1).astype(jnp.bfloat16)
    for n in range(rows.shape[1] // LANES):
        for e in range(groups):
            place = split * count + n * high
            stage[e, place : place + high, :] = rows[:, n * LANES : (n + 1) * LANES]
    sends = []

    def send(first, last):
        where = (slice(None), slice(first, last))
        sends.append(pltpu.make_async_copy(stage.at[where], out_hbm.at[where], sems.at[4 + len(sends)]))
        sends[-1].start()

    send(split * count, stage.shape[1])
    for pair in range(split // 2):
        wide = slice(pair * 2 * LANES, (pair + 1) * 2 * LANES)
        value = jnp.dot(white[...], sort[:, wide], preferred_element_type=jnp.float32).astype(jnp.bfloat16)
        for side in range(2):
            s = pair * 2 + side
            for e in range(groups):
                stage[e, s * count : (s + 1) * count, :] = value[
                    e * count : (e + 1) * count, side * LANES : (side + 1) * LANES
                ]
        send(pair * 2 * count, (pair + 1) * 2 * count)
    for send in sends:
        send.wait()


def modes_kernel(width, offsets, twiddle_ref, table, z_ref, out_hbm, *refs):
    left, leg, prod_a, prod_b, x_ref, out_ref, out_sems = refs
    tiles = table.shape[0]
    split = twiddle_ref.shape[1]
    tall = x_ref.shape[2]
    group = tall // width
    modes = out_ref.shape[3]
    sources = out_ref.shape[1]
    parts = z_ref.shape[0] // sources
    cycles = leg.shape[0] // offsets
    blocks = sources * modes // (tiles * LANES)
    per = modes // LANES
    count = cycles // parts * width
    high = cycles // parts * offsets

    def store(step, n):
        mode_tile = n // 2 * tiles + 2 * step + n % 2
        lanes = pl.ds(pl.multiple_of(mode_tile % per * LANES, LANES), LANES)
        where = (slice(None), mode_tile // per, slice(None), lanes)
        return pltpu.make_async_copy(out_ref.at[where], out_hbm.at[where], out_sems.at[step, n])

    fold = left.shape[0]
    for p in range(parts):
        for q in range(sources // fold):
            lanes = slice(q * LANES, (q + 1) * LANES)
            for n in range(split):
                place = (n * parts + p) * count
                rows = z_ref[p * sources + q, n * count : (n + 1) * count, :]
                if fold == 1:
                    left[0, place : place + count, lanes] = rows
                else:
                    rows = rows.astype(jnp.float32)
                    more = z_ref[p * sources + sources // 2 + q, n * count : (n + 1) * count, :].astype(jnp.float32)
                    left[0, place : place + count, lanes] = (rows + more).astype(jnp.bfloat16)
                    left[1, place : place + count, lanes] = (rows - more).astype(jnp.bfloat16)

    def product(tile, prod, kind):
        prod[...] = jnp.dot(left[kind % fold], table[tile], preferred_element_type=jnp.float32)

    product(0, prod_a, 0)
    for p in range(parts):
        for q in range(sources):
            for n in range(per):
                place = split * count + n * high
                rows = z_ref[p * sources + q, place : place + high, :].astype(jnp.float32)
                leg[p * high : (p + 1) * high, (q * per + n) * LANES : (q * per + n + 1) * LANES] = rows

    def use(tile, prod):
        lanes = pl.ds(pl.multiple_of(tile * LANES, LANES), LANES)
        cosine, sine = twiddle_ref[0, :, lanes], twiddle_ref[1, :, lanes]
        row_in = lax.broadcasted_iota(jnp.int32, (tall, LANES), 0)
        for pack in range(cycles // group):
            values = []
            for s in range(split):
                place = (s * cycles + pack * group) * width
                re = prod[place : place + tall, :LANES]
                im = prod[place : place + tall, LANES:]
                if s == 0:
                    values.append((re, im))
                else:
                    c, d = cosine[s : s + 1, :], sine[s : s + 1, :]
                    values.append((re * c + im * d, im * c - re * d))
            parts = dft(values)
            for b in range(blocks):
                for g in range(group):
                    shifts = ((group - g) * width % tall, (group + 1 - g) * width % tall)
                    rows = [pltpu.roll(v, m, 0) if m else v for v, m in zip(parts[b], shifts)]
                    x_ref[b, pack * group + g] = jnp.where(row_in < width, rows[0], rows[1])
        for b in range(blocks):
            mode_tile = b * tiles + tile
            d, n = mode_tile // per, mode_tile % per
            mode = pl.ds(pl.multiple_of(mode_tile * LANES, LANES), LANES)
            values = [x_ref[b, r] for r in range(cycles)]
            for k in range(offsets):
                total = None
                for r in range(cycles):
                    term = leg[r * offsets + k : r * offsets + k + 1, mode] * values[r]
                    total = term if r == 0 else total + term
                place = pl.ds(pl.multiple_of(n * LANES, LANES), LANES)
                out_ref[k, d, :, place] = total[: 2 * width].astype(jnp.bfloat16)

    def both(step, last):
        product(2 * step + 1, prod_b, 1)
        use(2 * step, prod_a)
        if not last:
            product(2 * step + 2, prod_a, 0)
        use(2 * step + 1, prod_b)
        for n in range(2 * blocks):
            store(step, n).start()

    @pl.loop(0, tiles // 2 - 1)
    def _(step):
        both(step, False)

    both(jnp.int32(tiles // 2 - 1), True)

    @pl.loop(0, tiles // 2)
    def _(step):
        for n in range(2 * blocks):
            store(step, n).wait()


def sketch_kernel(alm_ref, band_ref, cov_ref, test_ref, out_ref, left_ref):
    patches, groups, rows, lanes = alm_ref.shape
    chans = cov_ref.shape[0]
    width = rows // 2
    for g in range(groups):
        part = alm_ref[0, g].astype(jnp.float32)
        for p in range(1, patches):
            part += alm_ref[p, g].astype(jnp.float32)
        part = part * band_ref[...]
        for t in range(2):
            left_ref[t, g * width : (g + 1) * width, :] = part[t * width : (t + 1) * width]
    sketch = None
    for t in range(2):
        term = jnp.dot(left_ref[t].astype(jnp.bfloat16), test_ref[t], preferred_element_type=jnp.float32)
        sketch = term if t == 0 else sketch + term
    mixed = jnp.dot(
        cov_ref[...], sketch, precision=lax.Precision.HIGHEST, preferred_element_type=jnp.float32
    )
    mixed = jnp.transpose(mixed)
    if out_ref.ndim == 2:
        out_ref[...] = mixed
    else:
        owners, block, _ = out_ref.shape
        fold = out_ref.shape[2] // chans
        mixed = mixed.reshape(owners, fold, block, chans)
        out_ref[...] = jnp.concatenate([mixed[:, n] for n in range(fold)], axis=-1)


def total_kernel(part_ref, out_ref):
    block, chans = part_ref.shape[1], out_ref.shape[1]
    total = jnp.sum(part_ref[...], axis=0)
    for n in range(part_ref.shape[2] // chans):
        out_ref[n * block : (n + 1) * block, :] = total[:, n * chans : (n + 1) * chans]


def call(kernel, shape, scratch, mib, spaces, *operands, out_space=pltpu.VMEM, cost=(0, 0)):
    return pl.pallas_call(
        kernel,
        out_shape=shape,
        in_specs=[pl.BlockSpec(memory_space=space) for space in spaces],
        out_specs=jax.tree.map(lambda _: pl.BlockSpec(memory_space=out_space), shape),
        scratch_shapes=scratch,
        compiler_params=pltpu.CompilerParams(vmem_limit_bytes=mib * MIB),
        cost_estimate=pl.CostEstimate(flops=cost[0], bytes_accessed=cost[1], transcendentals=0),
    )(*operands)


def in_order(modes, fold):
    return np.arange(modes).reshape(-1, LANES, fold).swapaxes(1, 2).reshape(-1)


def transform_tables(split, cycle, fold):
    half = cycle // split
    modes = in_order(half, fold)
    step = np.arange(split)[:, None] * modes[None, :] % cycle
    angle = step * (2.0 * math.pi / cycle)
    twiddle = np.stack([np.cos(angle), np.sin(angle)]).astype(np.float32)
    step = np.arange(half // fold)[:, None] * modes[None, :] % half
    angle = (step * (2.0 * math.pi / half)).reshape(half // fold, half // LANES, LANES)
    table = np.transpose(np.concatenate([np.cos(angle), -np.sin(angle)], axis=2), (1, 0, 2))
    return twiddle, table.astype(ml_dtypes.bfloat16)


def local(sky_map, pixel_mask, noise_factor, cycle_legendre, band_power, channel_cov, test_matrix):
    cycles, pixels, chans = sky_map.shape
    modes, _ = band_power.shape
    offsets = cycle_legendre.shape[2]
    columns = test_matrix.shape[3]
    mode_count, pair = lax.axis_size("mode"), lax.axis_size("low")
    groups = pair * mode_count
    devices = lax.axis_size("high") * groups
    width = chans // groups
    group = max(1, SUBLANES // width)
    split = pixels // LANES
    rows = split * cycles * width
    legs = cycles * offsets * (modes // LANES)
    tiles = mode_count
    blocks = modes * mode_count // (tiles * LANES)
    everyone = ("high", "low", "mode")
    hbm, vmem, bf16, f32, shape = pl.ANY, pltpu.VMEM, jnp.bfloat16, jnp.float32, jax.ShapeDtypeStruct
    fold = 2 if modes % (2 * LANES) == 0 else 1
    twiddle, table = transform_tables(split, pixels * mode_count, fold)

    message = call(
        functools.partial(whiten_kernel, fold),
        shape((groups, rows + legs, LANES), bf16),
        [
            vmem((cycles, chans, pixels), bf16),
            vmem((cycles, pixels), jnp.int32),
            vmem((cycles, chans, chans), f32),
            vmem((cycles, offsets, modes), f32),
            vmem((pixels, pixels), bf16),
            vmem((cycles * chans, pixels), bf16),
            vmem((groups, rows + legs, LANES), bf16),
            pltpu.SemaphoreType.DMA((5 + split // 2,)),
        ],
        56,
        [hbm] * 4,
        jnp.transpose(sky_map, (0, 2, 1)),
        pixel_mask,
        noise_factor[:, 0],
        jnp.transpose(cycle_legendre, (0, 2, 1)),
        out_space=hbm,
        cost=(2 * cycles * chans * pixels * (pixels + 4 * chans), 8 * MIB),
    )
    message = lax.all_to_all(message, ("low", "mode"), 0, 0, tiled=True)

    alm = call(
        functools.partial(modes_kernel, width, offsets),
        shape((offsets, mode_count, 2 * width, modes), bf16),
        [
            vmem((fold, pair * rows, tiles * LANES // fold), bf16),
            vmem((pair * cycles * offsets, mode_count * modes), f32),
            vmem((pair * rows, 2 * LANES), f32),
            vmem((pair * rows, 2 * LANES), f32),
            vmem((blocks, pair * cycles, group * width, LANES), f32),
            vmem((offsets, mode_count, 2 * width, modes), bf16),
            pltpu.SemaphoreType.DMA((tiles // 2, 2 * blocks)),
        ],
        24,
        [vmem] * 3,
        jnp.asarray(twiddle),
        jnp.asarray(table),
        message,
        out_space=hbm,
        cost=(4 * pair * rows * (tiles * LANES) ** 2 // fold, 8 * MIB),
    )
    alm = alm.reshape(devices, 2 * width, modes)
    alm = lax.all_to_all(alm, everyone, 0, 0, tiled=True)
    alm = alm.reshape(devices // groups, groups, 2 * width, modes)

    right = test_matrix.reshape(modes // (fold * LANES), LANES, fold, 2, columns)
    right = jnp.transpose(right, (3, 0, 2, 1, 4)).reshape(2, modes, columns)
    band = jnp.swapaxes(band_power.reshape(-1, LANES, fold), 1, 2).reshape(1, modes)
    share = columns // (devices)
    fold = LANES // chans
    packed = share % (8 * fold) == 0
    part = call(
        sketch_kernel,
        shape((devices, share // fold, LANES) if packed else (columns, chans), f32),
        [vmem((2, chans, modes), f32)],
        24,
        [vmem] * 4,
        alm,
        band,
        channel_cov,
        right,
    )
    if not packed:
        part = part.reshape(devices, share, chans)
    part = lax.all_to_all(part, everyone, 0, 0, tiled=True)
    return jnp.transpose(call(total_kernel, shape((share, chans), f32), [], 16, [vmem], part))


def solution(mesh):
    patches, modes = mesh.shape["patch"], mesh.shape["mode"]
    mesh = jax.sharding.Mesh(mesh.devices.reshape(patches // 2, 2, modes), ("high", "low", "mode"))
    patch = ("high", "low")
    return jax.shard_map(
        local,
        mesh=mesh,
        in_specs=(
            P(patch, "mode", None),
            P(patch, "mode"),
            P(patch, "mode", None, None),
            P(patch, "mode", None),
            P("mode", patch),
            P(),
            P(patch, "mode", None, None),
        ),
        out_specs=P(None, (*patch, "mode")),
        check_vma=False,
    )
```
